512 devices in a mesh: dp: 16 (over y_lo, x, core), tm: 32 (over y_hi, z).
Axes of the slice: x: 4, y: 4 (y_hi: 2, y_lo: 2; y = y_hi * 2 + y_lo), z: 16, core: 2. Of those that a mesh axis runs over, the one named last changes fastest.
Arguments:
- latent: float32 [16, 64, 16384], P('dp', None, 'tm'), may hold values from -40 to 40
- target: float32 [16, 32768], P('dp', 'tm'), may hold values from -20 to 20
- up_kernel: float32 [4, 32, 64], replicated, may hold values from -0.5 to 0.5
- inner_kernel: float32 [3, 16, 32], replicated, may hold values from -0.625 to 0.625
- outer_kernel: float32 [32, 16], replicated, may hold values from -1.5 to 1.5
- out_kernel: float32 [7, 32], replicated, may hold values from -0.375 to 0.375
Outputs:
- latent_grad: float32 [16, 64, 16384], P('dp', None, 'tm')
- up_update: float32 [4, 32, 64], replicated
- inner_update: float32 [3, 16, 32], replicated
- outer_update: float32 [32, 16], replicated
- out_update: float32 [7, 32], replicated
The draws below stay inside these ranges and needn't reach their ends.
All inputs are finite; a program needn't handle non-finite values.
Results may differ from the reference program's by a relative error of at most 0.0003.
Values sent between devices are 32-bit elements; how exact they have to be, the bound alone decides.
A program may use at most 64 MiB of HBM per device.

```python
import jax
import jax.numpy as jnp
from jax import lax

CH = 64
MELS = 64
WIN_COARSE = 1024
WIN_FINE = 256
CLIPS = 16
TIME = 32768
FRAMES = 16384
PARAMS = 10464


def draw_latent(key, part):
    noise_key, clip_key, block_key = jax.random.split(jax.random.fold_in(key, 11), 3)
    positions = jnp.arange(FRAMES, dtype=jnp.float32) / FRAMES
    gaussian = jax.random.truncated_normal(noise_key, -4.0, 4.0, (CLIPS, CH, FRAMES), jnp.float32)
    rising = 1.0 + positions
    blocks_scale = jnp.exp(jax.random.uniform(block_key, (CLIPS, 1, FRAMES // 16), jnp.float32, jnp.log(0.5), jnp.log(2.5)))
    clip_scale = jnp.exp(jax.random.uniform(clip_key, (CLIPS, 1, 1), jnp.float32, jnp.log(0.5), jnp.log(2.0)))
    return gaussian * rising * clip_scale * jnp.repeat(blocks_scale, 16, axis=2)


def draw_target(key, part):
    noise_key, block_key = jax.random.split(jax.random.fold_in(key, 23), 2)
    positions = jnp.arange(TIME, dtype=jnp.float32) / TIME
    gaussian = jax.random.truncated_normal(noise_key, -4.0, 4.0, (CLIPS, TIME), jnp.float32)
    rising = 1.0 + positions
    blocks_scale = jnp.exp(jax.random.uniform(block_key, (CLIPS, TIME // 128), jnp.float32, jnp.log(0.5), jnp.log(2.5)))
    return gaussian * rising * jnp.repeat(blocks_scale, 128, axis=1)


def normal_values(own_key, dims, spread, most, kind=jnp.bfloat16):
    drawn = spread * jax.random.normal(own_key, dims, jnp.float32)
    return jnp.clip(drawn, min=-most, max=most).astype(kind)


def setup_inputs(seed: int = 0) -> dict:
    keys = jax.random.split(jax.random.key(seed), 7)
    return {
        "latent": draw_latent(jax.random.fold_in(keys[6], 71), 0),
        "target": draw_target(jax.random.fold_in(keys[6], 71), 0),
        "up_kernel": normal_values(keys[2], (4, CH // 2, CH), (2 * CH) ** -0.5, 0.5, jnp.float32),
        "inner_kernel": normal_values(keys[3], (3, CH // 4, CH // 2), (3 * CH // 2) ** -0.5, 0.625, jnp.float32),
        "outer_kernel": normal_values(keys[4], (CH // 2, CH // 4), (CH // 4) ** -0.5, 1.5, jnp.float32),
        "out_kernel": normal_values(keys[5], (7, CH // 2), (7 * CH // 2) ** -0.5, 0.375, jnp.float32),
    }


LOSS_WEIGHTS = (0.25, 0.5, 0.5)

def product(form, left, right):
    return jnp.einsum(form, left, right, precision=lax.Precision.HIGHEST, preferred_element_type=jnp.float32)

def mel_bank(window, mel_count):
    half_window = window // 2
    top_mel = 2595.0 * jnp.log10(1.0 + 12000.0 / 700.0)
    points = (jnp.arange(mel_count + 1, dtype=jnp.float32) + 1.0) / (mel_count + 2.0) * top_mel
    centers = 700.0 * (jnp.power(10.0, points / 2595.0) - 1.0) / 12000.0 * half_window
    spacing = jnp.maximum(centers[1:] - centers[:-1], 1.0)
    places = jnp.arange(half_window, dtype=jnp.float32)[:, None]
    return jnp.maximum(0.0, 1.0 - jnp.abs(places - centers[None, :mel_count]) / spacing[None, :])

def dft_table(window):
    half_window = window // 2
    sample = jnp.arange(window, dtype=jnp.int32)[:, None]
    freq_index = jnp.arange(half_window, dtype=jnp.int32)[None, :]
    angles = (sample * freq_index % window).astype(jnp.float32) * (2.0 * jnp.pi / window)
    hann_taper = 0.5 - 0.5 * jnp.cos(sample.astype(jnp.float32) * (2.0 * jnp.pi / window))
    return jnp.concatenate([hann_taper * jnp.cos(angles), -hann_taper * jnp.sin(angles)], axis=1)

def framed(signal, window, frame_count):
    hop_size = window // 4
    blocks = signal[..., :(frame_count + 3) * hop_size].reshape(signal.shape[:-1] + (frame_count + 3, hop_size))
    return jnp.concatenate([blocks[..., offset:offset + frame_count, :] for offset in range(4)], axis=-1)

def mel_energy(signal, window, frame_count):
    frames = framed(signal, window, frame_count)
    spectra = product('...nf,fk->...nk', frames, dft_table(window))
    half_window = window // 2
    energy = spectra[..., :half_window] ** 2 + spectra[..., half_window:] ** 2
    return product('...nk,km->...nm', energy, mel_bank(window, MELS))

def spectral_loss(signal, target_mel, window, frame_count):
    level = jnp.sqrt(mel_energy(signal, window, frame_count) + 1.0)
    return jnp.sum((level - jnp.sqrt(target_mel + 1.0)) ** 2)

def upsample(values, kernel, stride):
    lagged = jnp.pad(values[:, :-1], ((0, 0), (1, 0)))
    phases = product('pij,jm->imp', kernel[:stride], values) + product('pij,jm->imp', kernel[stride:], lagged)
    return phases.reshape(phases.shape[0], -1)

def convolve(values, kernel):
    tap_count = kernel.shape[0]
    half_taps = tap_count // 2
    length = values.shape[-1]
    padded = jnp.pad(values, ((0, 0), (half_taps, half_taps)))
    summed = product('oi,il->ol', kernel[0], padded[:, :length])
    for offset in range(1, tap_count):
        summed = summed + product('oi,il->ol', kernel[offset], padded[:, offset:offset + length])
    return summed

def residual_unit(values, inner_kernel, outer_kernel):
    hidden = jax.nn.elu(convolve(jax.nn.elu(values), inner_kernel))
    return values + product('oi,il->ol', outer_kernel, hidden)

def decode(latent_clip, weights):
    up_kernel, inner_kernel, outer_kernel, out_kernel = weights
    values = upsample(jax.nn.elu(latent_clip), up_kernel, 2)
    values = residual_unit(values, inner_kernel, outer_kernel)
    return convolve(jax.nn.elu(values), out_kernel[:, None, :])[0]

def reference(latent, target, up_kernel, inner_kernel, outer_kernel, out_kernel):
    weights = (up_kernel, inner_kernel, outer_kernel, out_kernel)
    time_length = target.shape[1]

    def clip_step(totals, clip_pair):
        latent_clip, target_clip = clip_pair
        waveform, pullback = jax.vjp(decode, latent_clip, weights)
        gradients = [2.0 * (waveform - target_clip)]
        for window in (WIN_COARSE, WIN_FINE):
            hop_size = window // 4
            frame_count = time_length // hop_size
            target_mel = mel_energy(jnp.pad(target_clip, (0, 3 * hop_size)), window, frame_count)

            def scale_loss(signal):
                return spectral_loss(jnp.pad(signal, (0, 3 * hop_size)), target_mel, window, frame_count)
            gradients.append(jax.grad(scale_loss)(waveform))
        balanced = jnp.zeros_like(waveform)
        for weight_value, member in zip(LOSS_WEIGHTS, gradients):
            balanced = balanced + member * (weight_value / jnp.sqrt(jnp.mean(member * member) + 1e-06))
        grad_latent, grad_weights = pullback(balanced)
        return (jax.tree.map(jnp.add, totals, grad_weights), grad_latent)
    totals, latent_grad = lax.scan(clip_step, jax.tree.map(jnp.zeros_like, weights), (latent, target))
    squares = sum((jnp.sum(member * member) for member in totals))
    factor = jnp.minimum(1.0, 1.0 / jnp.sqrt(squares / PARAMS + 1e-06))
    return (latent_grad, totals[0] * factor, totals[1] * factor, totals[2] * factor, totals[3] * factor)
```

```python
import functools

import jax
import jax.numpy as jnp
import ml_dtypes
import numpy as np
from jax import lax
from jax.experimental import pallas as pl
from jax.experimental.pallas import tpu as pltpu
from jax.sharding import PartitionSpec as P

F32 = jnp.float32
BF16 = jnp.bfloat16
MESH = pl.DeviceIdType.MESH
MELS = 64
COEFFS = (0.25, 0.5, 0.5)
PARAMS = 10464
Y_HI = 2
TILES = 11


def mel_bank(window):
    half = window // 2
    top = 2595.0 * np.log10(1.0 + 12000.0 / 700.0)
    points = (np.arange(MELS + 1) + 1.0) / (MELS + 2.0) * top
    centers = 700.0 * (np.power(10.0, points / 2595.0) - 1.0) / 12000.0 * half
    spacing = np.maximum(centers[1:] - centers[:-1], 1.0)
    places = np.arange(half)[:, None]
    return np.maximum(0.0, 1.0 - np.abs(places - centers[None, :MELS]) / spacing[None, :])


def halves(x):
    high = x.astype(ml_dtypes.bfloat16)
    low = (x - high.astype(np.float64)).astype(ml_dtypes.bfloat16)
    return high, low


@functools.cache
def tables():
    lane = np.arange(256)
    place = np.where(lane < 128, 2 * lane, 2 * (lane - 128) + 1)

    def waves(bins, window):
        angle = 2.0 * np.pi * ((place[:, None] * bins[None, :]) % window) / window
        return np.cos(angle), np.sin(angle)

    p = np.arange(128)
    cos0, sin0 = waves(4 * p, 1024)
    cos2, sin2 = waves(4 * p + 2, 1024)
    cos1, sin1 = waves(4 * p + 1, 1024)
    cos3, sin3 = waves(4 * p + 3, 1024)
    t0 = np.concatenate([cos0, -sin0], axis=1)
    t2 = np.concatenate([cos2, -sin2], axis=1)
    real = np.concatenate(
        [np.concatenate([cos1, cos3], axis=1), np.concatenate([-sin1, sin3], axis=1)], axis=0
    )
    imag = np.concatenate(
        [np.concatenate([-sin1, -sin3], axis=1), np.concatenate([-cos1, cos3], axis=1)], axis=0
    )
    cosf, sinf = waves(p, 256)
    fine = np.concatenate([cosf, -sinf], axis=1)
    high, low = halves(np.concatenate([t0, t2, real, imag], axis=0))
    fine_high, fine_low = halves(fine)
    move = np.zeros((256, 256))
    move[place, lane] = 1.0
    dft = np.concatenate(
        [high, low, fine_high, fine_low, move.astype(ml_dtypes.bfloat16)], axis=0
    )
    order = np.concatenate([4 * p, 4 * p + 2, 4 * p + 1, 4 * p + 3])
    mels = np.concatenate([mel_bank(1024)[order], mel_bank(256)], axis=0)
    mels = np.concatenate(halves(mels), axis=1)
    taper = 0.5 - 0.5 * np.cos(2.0 * np.pi * (np.arange(4)[:, None] * 256 + place) / 1024)
    taper_fine = 0.5 - 0.5 * np.cos(2.0 * np.pi * place[None, :] / 256)
    tapers = np.concatenate([taper, taper_fine, np.zeros((3, 256))], axis=0).astype(np.float32)
    return dft, mels, tapers


HIGH, LOW, FINE_HIGH, FINE_LOW, MOVE, ROWS = 0, 1536, 3072, 3328, 3584, 3840


def split(x):
    high = x.astype(BF16)
    return high, (x - high.astype(F32)).astype(BF16)


def dot(a, b):
    return lax.dot_general(a, b, (((1,), (0,)), ((), ())), preferred_element_type=F32)


def dot_nt(a, b):
    return lax.dot_general(a, b, (((1,), (1,)), ((), ())), preferred_element_type=F32)


def weight_dot(w, x):
    high, low = w
    m = high.shape[0]
    xh, xl = split(x)
    both = dot(jnp.concatenate([high, low], axis=0), xh)
    return both[:m] + both[m:] + dot(high, xl)


def rows_dot(x, high, low, product=dot):
    m = x.shape[0]
    xh, xl = split(x)
    both = product(jnp.concatenate([xh, xl], axis=0), high)
    return both[:m] + both[m:] + product(xh, low)


def gram(a, b):
    m = a.shape[0]
    ah, al = split(a)
    bh, bl = split(b)
    both = dot_nt(jnp.concatenate([ah, al], axis=0), bh)
    return both[:m] + both[m:] + dot_nt(ah, bl)


def elu_and_slope(x):
    slope = jnp.exp(jnp.minimum(x, 0.0))
    return jnp.maximum(x, 0.0) + (slope - 1.0), slope


def roll(x, by, axis=1):
    return pltpu.roll(x, by % x.shape[axis], axis)


def coarse_spectrum(blocks, tapers, table):
    x = [blocks[b : b + 16, :] * tapers[b : b + 1, :] for b in range(4)]
    even, odd = x[0] + x[2], x[1] + x[3]
    cross = jnp.concatenate([x[0] - x[2], x[1] - x[3]], axis=1)
    return (
        rows_dot(even + odd, table[HIGH : HIGH + 256, :], table[LOW : LOW + 256, :]),
        rows_dot(even - odd, table[HIGH + 256 : HIGH + 512, :], table[LOW + 256 : LOW + 512, :]),
        rows_dot(cross, table[HIGH + 512 : HIGH + 1024, :], table[LOW + 512 : LOW + 1024, :]),
        rows_dot(cross, table[HIGH + 1024 : HIGH + 1536, :], table[LOW + 1024 : LOW + 1536, :]),
    )


def coarse_energy(parts):
    s0, s2, re, im = (part * part for part in parts)
    return jnp.concatenate(
        [s0[:, :128] + s0[:, 128:], s2[:, :128] + s2[:, 128:], re + im], axis=1
    )


def fine_frames(blocks, tapers):
    now, later = blocks[3:11, :], blocks[4:12, :]
    lane = lax.broadcasted_iota(jnp.int32, (8, 128), 1)
    frames = [now]
    for d in range(1, 4):
        keep = lane < 128 - 32 * d
        frames.append(
            jnp.concatenate(
                [
                    jnp.where(
                        keep,
                        roll(now[:, s : s + 128], -32 * d),
                        roll(later[:, s : s + 128], -32 * d),
                    )
                    for s in (0, 128)
                ],
                axis=1,
            )
        )
    return jnp.concatenate(frames, axis=0) * tapers[4:5, :]


def fine_spectrum(blocks, tapers, table):
    return rows_dot(
        fine_frames(blocks, tapers),
        table[FINE_HIGH : FINE_HIGH + 256, :],
        table[FINE_LOW : FINE_LOW + 256, :],
    )


def level_of(energy, bank):
    m = energy.shape[0]
    eh, el = split(energy)
    both = dot(jnp.concatenate([eh, el], axis=0), bank)
    both = both[:m] + both[m:]
    return jnp.sqrt(both + roll(both, MELS) + 1.0)


def energy_slope(level, target_level, valid, bank):
    m = level.shape[0]
    slope = jnp.where(valid, 1.0 - target_level / level, 0.0)
    sh, sl = split(slope)
    both = dot_nt(jnp.concatenate([sh, sl], axis=0), bank)
    return 2.0 * (both[:m] + both[m:])


def kernel(
    n_dp,
    n_tm,
    latent_hbm,
    target_hbm,
    up_hbm,
    inner_hbm,
    outer_hbm,
    out_hbm,
    dft_hbm,
    mels_hbm,
    tapers_hbm,
    grad_hbm,
    up_ref,
    inner_ref,
    outer_ref,
    out_ref,
    latent,
    halo,
    target_rows,
    up_k,
    inner_k,
    outer_k,
    out_k,
    table,
    mels,
    tapers,
    natural,
    target_blocks,
    wave_tiles,
    wave_blocks,
    frame_grads,
    grad_blocks,
    squares,
    packed,
    plane_rows,
    ring_rows,
    total,
    grad_out,
    load_sem,
    near_send,
    near_recv,
    far_send,
    far_recv,
    store_sem,
):
    dp = lax.axis_index("dp")
    tm = lax.axis_index("tm")
    n_z = n_tm // Y_HI
    n_plane = n_dp * Y_HI
    y_hi = tm // n_z
    z = lax.rem(tm, n_z)
    plane = y_hi * n_dp + dp
    right = lax.rem(tm + 1, n_tm)
    left = lax.rem(tm + n_tm - 1, n_tm)
    other = lax.rem(y_hi + 1, Y_HI) * n_z + z
    first = tm == 0
    last = tm == n_tm - 1

    barrier = pltpu.get_barrier_semaphore()

    def greet(device):
        pl.semaphore_signal(barrier, inc=1, device_id=device, device_id_type=MESH)

    @pl.loop(1, n_tm)
    def _(i):
        greet((dp, lax.rem(tm + i, n_tm)))

    @pl.loop(1, n_dp)
    def _(i):
        peer = lax.rem(dp + i, n_dp)
        greet((peer, tm))
        greet((peer, other))

    loads = [
        pltpu.make_async_copy(source, place, load_sem.at[i])
        for i, (source, place) in enumerate(
            [
                (latent_hbm.at[0], latent),
                (target_hbm, target_rows.at[1]),
                (up_hbm, up_k),
                (inner_hbm, inner_k),
                (outer_hbm, outer_k),
                (out_hbm, out_k),
                (dft_hbm, table),
                (mels_hbm, mels),
                (tapers_hbm, tapers),
            ]
        )
    ]
    for load in loads:
        load.start()
    frames = latent.shape[1]
    wide = frames + 128

    loads[2].wait()
    loads[3].wait()
    loads[4].wait()
    loads[5].wait()
    up_rows = up_k[...]
    up_all = jnp.concatenate([up_rows[r] for r in range(4)], axis=0)
    up_w = jnp.concatenate(
        [
            jnp.concatenate([up_rows[0], up_rows[2]], axis=1),
            jnp.concatenate([up_rows[1], up_rows[3]], axis=1),
        ],
        axis=0,
    )
    up_fwd = split(up_w)
    up_bwd = split(up_all.T)
    taps = jnp.concatenate(
        [inner_k[0], inner_k[1], inner_k[2], jnp.zeros((16, 32), F32)], axis=1
    )
    inner_w = jnp.concatenate([taps, roll(taps, 32)], axis=0)
    inner_fwd = split(inner_w)
    zero = jnp.zeros((16, 32), F32)
    k0, k1, k2 = inner_k[0], inner_k[1], inner_k[2]
    inner_t = jnp.concatenate(
        [
            jnp.concatenate([k1, k2], axis=1),
            jnp.concatenate([k0, k1], axis=1),
            jnp.concatenate([k2, zero], axis=1),
            jnp.concatenate([zero, k0], axis=1),
        ],
        axis=0,
    )
    inner_bwd = split(inner_t.T)
    outer_t = outer_k[...]
    outer_w = jnp.concatenate(
        [jnp.concatenate([outer_t, zero], axis=1), jnp.concatenate([zero, outer_t], axis=1)],
        axis=0,
    )
    outer_bwd = split(outer_w)
    outer_fwd = split(outer_w.T)
    pad = jnp.zeros((1, 32), F32)
    taps_out = out_k[...]
    out_w = jnp.concatenate(
        [
            jnp.concatenate([pad, taps_out], axis=0),
            jnp.concatenate([taps_out, pad], axis=0),
        ],
        axis=1,
    )
    out_w16 = jnp.concatenate([out_w, jnp.zeros((8, 64), F32)], axis=0)
    out_fwd = split(out_w16)
    out_bwd = split(out_w16.T)

    pl.semaphore_wait(barrier, n_tm - 1 + 2 * (n_dp - 1))

    def send(source, place, slot, device):
        copy = pltpu.make_async_remote_copy(
            src_ref=source,
            dst_ref=place,
            send_sem=near_send.at[slot],
            recv_sem=near_recv.at[slot],
            device_id=device,
            device_id_type=MESH,
        )
        copy.start()
        return copy

    near = [
        send(latent_hbm.at[0, :, pl.ds(frames - 128, 128)], halo.at[0], 0, (dp, right)),
        send(latent_hbm.at[0, :, pl.ds(0, 128)], halo.at[1], 1, (dp, left)),
        send(target_hbm, target_rows.at[0], 2, (dp, right)),
        send(target_hbm, target_rows.at[2], 3, (dp, left)),
    ]

    lane = lax.broadcasted_iota(jnp.int32, (1, wide), 1)
    inside = (
        (lane < frames)
        | ((lane < frames + 4) & jnp.logical_not(last))
        | ((lane >= wide - 4) & jnp.logical_not(first))
    )

    loads[0].wait()
    near[0].wait_recv()
    near[1].wait_recv()
    spot = lax.broadcasted_iota(jnp.int32, (64, 128), 1)
    rim = jnp.where(
        (spot < 4) & jnp.logical_not(last),
        halo[1],
        jnp.where((spot >= 124) & jnp.logical_not(first), halo[0], 0.0),
    )
    activated, slope_in = elu_and_slope(jnp.concatenate([latent[...], rim], axis=1))
    stacked = jnp.concatenate([activated, roll(activated, 1)], axis=0)
    upper = jnp.where(inside, weight_dot(up_fwd, stacked), 0.0)
    lifted, slope_upper = elu_and_slope(upper)
    even, odd = lifted[:32], lifted[32:]
    tapped = jnp.concatenate([roll(odd, 1), even, odd, roll(even, -1)], axis=0)
    hidden, slope_inner = elu_and_slope(weight_dot(inner_fwd, tapped))
    mixed = jnp.where(inside, upper + weight_dot(outer_fwd, hidden), 0.0)
    final, slope_mixed = elu_and_slope(mixed)
    taps_8 = weight_dot(out_fwd, final)[:8]
    row = lax.broadcasted_iota(jnp.int32, (8, wide), 0)
    moves = ((2, 0, 0), (1, 1, 2), (-1, 5, 6), (-2, 7, 7))
    aligned = taps_8
    for by, low, high in moves:
        aligned = jnp.where((row >= low) & (row <= high), roll(taps_8, by), aligned)
    aligned = aligned[:, :frames]
    aligned = aligned + roll(aligned, 4, 0)
    aligned = aligned + roll(aligned, 2, 0)
    is_even = lax.rem(row[:, :frames], 2) == 0
    swapped = roll(aligned, 1, 0)
    wave_even = jnp.where(is_even, aligned, swapped)
    wave_odd = jnp.where(is_even, swapped, aligned)
    tile = jnp.zeros((8, 128), F32)
    row_8 = row[:, :128]
    for b in range(4):
        tile = jnp.where(row_8 == b, wave_even[:, 128 * b : 128 * b + 128], tile)
        tile = jnp.where(row_8 == 4 + b, wave_odd[:, 128 * b : 128 * b + 128], tile)
    wave_tiles[1] = tile
    near += [
        send(wave_tiles.at[1], wave_tiles.at[0], 4, (dp, right)),
        send(wave_tiles.at[1], wave_tiles.at[2], 5, (dp, left)),
    ]

    for load in (loads[1], loads[6], loads[7], loads[8]):
        load.wait()
    near[2].wait_recv()
    near[3].wait_recv()
    natural[...] = jnp.zeros(natural.shape, F32)
    for s in range(3):
        for b in range(4):
            line = target_rows[s, :, 256 * b : 256 * b + 256]
            if s == 0:
                line = jnp.where(first, 0.0, line)
            if s == 2:
                line = jnp.where(last, 0.0, line)
            natural[4 * s + b : 4 * s + b + 1, :] = line
    nh, nl = split(natural[...])
    moved = dot(jnp.concatenate([nh, nl], axis=0), table[MOVE : MOVE + 256, :])
    target_blocks[...] = jnp.zeros(target_blocks.shape, F32)
    target_blocks[0:16, :] = moved[:16] + moved[16:]
    bank, bank_fine = mels[0:512, :], mels[512:640, :]
    target_coarse = level_of(coarse_energy(coarse_spectrum(target_blocks, tapers, table)), bank)
    s = fine_spectrum(target_blocks, tapers, table)
    s = s * s
    target_fine = level_of(s[:, :128] + s[:, 128:], bank_fine)

    wave_blocks[...] = jnp.zeros(wave_blocks.shape, F32)
    near[4].wait_recv()
    near[5].wait_recv()
    for s in range(3):
        for half in range(2):
            lines = wave_tiles[s, 4 * half : 4 * half + 4, :]
            if s == 0:
                lines = jnp.where(first, 0.0, lines)
            if s == 2:
                lines = jnp.where(last, 0.0, lines)
            wave_blocks[4 * s : 4 * s + 4, 128 * half : 128 * half + 128] = lines
    parts = coarse_spectrum(wave_blocks, tapers, table)
    level = level_of(coarse_energy(parts), bank)
    frame = lax.broadcasted_iota(jnp.int32, (16, 128), 0)
    index = 4 * tm + frame - 4
    valid = (frame < 9) & (index >= 0) & (index < 4 * n_tm)
    slope = energy_slope(level, target_coarse, valid, bank)
    s0, s2, re, im = parts
    twice = functools.partial(jnp.concatenate, axis=1)
    d0 = s0 * twice([slope[:, 0:128]] * 2)
    d2 = s2 * twice([slope[:, 128:256]] * 2)
    d_even = rows_dot(d0, table[HIGH : HIGH + 256, :], table[LOW : LOW + 256, :], dot_nt)
    d_odd = rows_dot(
        d2, table[HIGH + 256 : HIGH + 512, :], table[LOW + 256 : LOW + 512, :], dot_nt
    )
    d_cross = rows_dot(
        re * slope[:, 256:512],
        table[HIGH + 512 : HIGH + 1024, :],
        table[LOW + 512 : LOW + 1024, :],
        dot_nt,
    ) + rows_dot(
        im * slope[:, 256:512],
        table[HIGH + 1024 : HIGH + 1536, :],
        table[LOW + 1024 : LOW + 1536, :],
        dot_nt,
    )
    d_first, d_second = d_cross[:, :256], d_cross[:, 256:]
    both, apart = d_even + d_odd, d_even - d_odd
    for b, d in enumerate((both + d_first, apart + d_second, both - d_first, apart - d_second)):
        frame_grads[b] = d * tapers[b : b + 1, :]
    coarse = frame_grads[0, 3:11, :]
    for b in range(1, 4):
        coarse = coarse + frame_grads[b, 3 - b : 11 - b, :]

    spectrum = fine_spectrum(wave_blocks, tapers, table)
    s = spectrum * spectrum
    level = level_of(s[:, :128] + s[:, 128:], bank_fine)
    frame = lax.broadcasted_iota(jnp.int32, (32, 128), 0)
    index = 16 * tm + 4 * (lax.rem(frame, 8) - 1) + frame // 8
    valid = (index >= 0) & (index < 16 * n_tm)
    slope = energy_slope(level, target_fine, valid, bank_fine)
    d = rows_dot(
        spectrum * twice([slope] * 2),
        table[FINE_HIGH : FINE_HIGH + 256, :],
        table[FINE_LOW : FINE_LOW + 256, :],
        dot_nt,
    )
    d = d * tapers[4:5, :]
    lane_8 = lax.broadcasted_iota(jnp.int32, (8, 128), 1)
    fine = []
    for start in (0, 128):
        here = d[0:8, start : start + 128]
        after = jnp.zeros((8, 128), F32)
        for k in range(1, 4):
            moved = roll(d[8 * k : 8 * k + 8, start : start + 128], 32 * k)
            here = here + jnp.where(lane_8 >= 32 * k, moved, 0.0)
            after = after + jnp.where(lane_8 < 32 * k, moved, 0.0)
        fine.append(here + roll(after, 1, 0))
    fine = twice(fine)
    timed = 2.0 * (wave_blocks[3:11, :] - target_blocks[3:11, :])

    row_256 = lax.broadcasted_iota(jnp.int32, (8, 256), 0)
    own = (row_256 >= 1) & (row_256 <= 4)
    lane_1 = lax.broadcasted_iota(jnp.int32, (1, 128), 1)
    line = jnp.zeros((1, 128), F32)
    for i, member in enumerate((timed, coarse, fine)):
        kept = jnp.where(own, member * member, 0.0)
        line = jnp.where(lane_1 == i, jnp.sum(kept, keepdims=True), line)
    squares[tm] = line

    def far(source, place, slot, device):
        return pltpu.make_async_remote_copy(
            src_ref=source,
            dst_ref=place,
            send_sem=far_send.at[slot],
            recv_sem=far_recv.at[slot],
            device_id=device,
            device_id_type=MESH,
        )

    def arrived(ref, slot):
        pltpu.make_async_copy(ref, ref, far_recv.at[slot]).wait()

    def sent(ref, slot):
        pltpu.make_async_copy(ref, ref, far_send.at[slot]).wait()

    @pl.loop(1, n_tm)
    def _(i):
        far(squares.at[tm], squares.at[tm], 0, (dp, lax.rem(tm + i, n_tm))).start()

    grad_blocks[0] = timed
    grad_blocks[1] = coarse
    grad_blocks[2] = fine
    arrived(squares.at[pl.ds(0, n_tm - 1)], 0)
    sums = squares[0]
    for i in range(1, n_tm):
        sums = sums + squares[i]
    scale = lax.rsqrt(sums / (n_tm * 2.0 * frames) + 1e-06)
    balanced = jnp.zeros((8, 256), F32)
    for i, coeff in enumerate(COEFFS):
        balanced = balanced + grad_blocks[i] * (coeff * scale[:, i : i + 1])
    grad_blocks[0] = balanced

    spread = []
    even_8 = lax.rem(row_8, 2) == 0
    for b in range(5):
        r = b + 1
        even = jnp.broadcast_to(grad_blocks[0, r : r + 1, 0:128], (8, 128))
        odd = jnp.broadcast_to(grad_blocks[0, r : r + 1, 128:256], (8, 128))
        lines = jnp.where(even_8, even, odd)
        if b == 4:
            even = jnp.broadcast_to(grad_blocks[0, 0:1, 0:128], (8, 128))
            odd = jnp.broadcast_to(grad_blocks[0, 0:1, 128:256], (8, 128))
            lines = jnp.where(lane_8 < 64, lines, jnp.where(even_8, even, odd))
        spread.append(lines)
    wide_grad = jnp.where(inside, jnp.concatenate(spread, axis=1), 0.0)

    def shifted(x):
        result = x
        for by, low, high in moves:
            result = jnp.where((row >= low) & (row <= high), roll(x, -by), result)
        return jnp.concatenate([result, jnp.zeros_like(result)], axis=0)

    grad_final = weight_dot(out_bwd, shifted(wide_grad))
    owned = jnp.where(lane < frames, wide_grad, 0.0)
    out_rows = gram(shifted(owned), final)[:8]
    grad_mixed = jnp.where(inside, grad_final * slope_mixed, 0.0)
    outer_rows = gram(hidden[:, :frames], grad_mixed[:, :frames])
    grad_inner = weight_dot(outer_bwd, grad_mixed) * slope_inner
    inner_rows = gram(grad_inner[:, :frames], tapped[:, :frames])
    even, odd = grad_inner[:16], grad_inner[16:]
    around = jnp.concatenate([even, odd, roll(odd, 1), roll(even, -1)], axis=0)
    grad_lifted = weight_dot(inner_bwd, around)
    grad_upper = jnp.where(inside, grad_mixed + grad_lifted * slope_upper, 0.0)
    packed[0:64, :] = gram(grad_upper[:, :frames], stacked[:, :frames])
    taps = inner_rows[:16] + roll(inner_rows[16:], -32)
    pair = outer_rows[:16, :32] + outer_rows[16:, 32:]
    packed[64:80, :] = jnp.concatenate([taps[:, :96], pair], axis=1)
    taps_7 = out_rows[0:7, 32:64] + out_rows[1:8, 0:32]
    packed[80:88, :] = jnp.zeros((8, 128), F32)
    packed[80:87, 0:32] = taps_7

    for i in range(TILES):
        owner = (i * n_plane) // TILES
        chunk = packed.at[pl.ds(8 * i, 8)]
        mine = plane == owner

        @pl.when(mine)
        def _():
            plane_rows[plane] = chunk[...]

        @pl.when(jnp.logical_not(mine))
        def _():
            far(
                chunk, plane_rows.at[plane], 1, (owner % n_dp, (owner // n_dp) * n_z + z)
            ).start()

    after = jnp.concatenate([grad_upper, roll(grad_upper, -1)], axis=0)
    grad_out[...] = weight_dot(up_bwd, after[:, :frames]) * slope_in[:, :frames]
    store = pltpu.make_async_copy(grad_out, grad_hbm.at[0], store_sem)
    store.start()

    tile_index = (plane * TILES + n_plane - 1) // n_plane
    owns = (tile_index < TILES) & ((tile_index * n_plane) // TILES == plane)
    tile_rows = pl.ds(pl.multiple_of(8 * tile_index, 8), 8)

    @pl.when(owns)
    def _():
        arrived(plane_rows.at[pl.ds(0, n_plane - 1)], 1)
        chunk = plane_rows[0]
        for i in range(1, n_plane):
            chunk = chunk + plane_rows[i]
        ring_rows[z] = chunk

        @pl.loop(1, n_z)
        def _(i):
            peer = y_hi * n_z + lax.rem(z + i, n_z)
            far(ring_rows.at[z], ring_rows.at[z], 2, (dp, peer)).start()

        arrived(ring_rows.at[pl.ds(0, n_z - 1)], 2)
        chunk = ring_rows[0]
        for i in range(1, n_z):
            chunk = chunk + ring_rows[i]
        total[tile_rows, :] = chunk

        @pl.loop(1, n_plane)
        def _(i):
            peer = lax.rem(plane + i, n_plane)
            far(
                total.at[tile_rows],
                total.at[tile_rows],
                3,
                (lax.rem(peer, n_dp), (peer // n_dp) * n_z + z),
            ).start()

        arrived(total.at[pl.ds(0, 8 * (TILES - 1))], 3)

    @pl.when(jnp.logical_not(owns))
    def _():
        arrived(total.at[pl.ds(0, 8 * TILES)], 3)

    sums = total[...]
    square = jnp.sum(sums * sums, keepdims=True)
    factor = jnp.minimum(1.0, lax.rsqrt(square / PARAMS + 1e-06))
    sums = sums * factor
    up_ref[0] = sums[0:32, 0:64]
    up_ref[1] = sums[32:64, 0:64]
    up_ref[2] = sums[0:32, 64:128]
    up_ref[3] = sums[32:64, 64:128]
    for j in range(3):
        inner_ref[j] = sums[64:80, 32 * j : 32 * j + 32]
    outer_ref[...] = sums[64:80, 96:128]
    out_ref[...] = sums[80:87, 0:32]

    for copy in near:
        copy.wait_send()
    sent(squares.at[pl.ds(0, n_tm - 1)], 0)
    store.wait()

    @pl.when(owns)
    def _():
        sent(packed.at[pl.ds(0, 8 * (TILES - 1))], 1)
        sent(ring_rows.at[pl.ds(0, n_z - 1)], 2)
        sent(plane_rows.at[pl.ds(0, n_plane - 1)], 3)

    @pl.when(jnp.logical_not(owns))
    def _():
        sent(packed.at[pl.ds(0, 8 * TILES)], 1)


def local(n_dp, n_tm, latent, target, up_kernel, inner_kernel, outer_kernel, out_kernel):
    dft, mels, tapers = tables()
    frames = latent.shape[2]
    n_z = n_tm // Y_HI
    n_plane = n_dp * Y_HI
    shape = jax.ShapeDtypeStruct
    hbm = pl.BlockSpec(memory_space=pltpu.HBM)
    vmem = pl.BlockSpec(memory_space=pltpu.VMEM)
    results = pl.pallas_call(
        functools.partial(kernel, n_dp, n_tm),
        out_shape=(
            shape(latent.shape, F32),
            shape((4, 32, 64), F32),
            shape((3, 16, 32), F32),
            shape((16, 32), F32),
            shape((7, 32), F32),
        ),
        in_specs=[hbm] * 9,
        out_specs=(hbm, vmem, vmem, vmem, vmem),
        scratch_shapes=[
            pltpu.VMEM((64, frames), F32),
            pltpu.VMEM((2, 64, 128), F32),
            pltpu.VMEM((3, 1, 2 * frames), F32),
            pltpu.VMEM((4, 32, 64), F32),
            pltpu.VMEM((3, 16, 32), F32),
            pltpu.VMEM((16, 32), F32),
            pltpu.VMEM((7, 32), F32),
            pltpu.VMEM((ROWS, 256), BF16),
            pltpu.VMEM((640, 128), BF16),
            pltpu.VMEM((8, 256), F32),
            pltpu.VMEM((16, 256), F32),
            pltpu.VMEM((24, 256), F32),
            pltpu.VMEM((3, 8, 128), F32),
            pltpu.VMEM((24, 256), F32),
            pltpu.VMEM((4, 16, 256), F32),
            pltpu.VMEM((3, 8, 256), F32),
            pltpu.VMEM((n_tm, 1, 128), F32),
            pltpu.VMEM((8 * TILES, 128), F32),
            pltpu.VMEM((n_plane, 8, 128), F32),
            pltpu.VMEM((n_z, 8, 128), F32),
            pltpu.VMEM((8 * TILES, 128), F32),
            pltpu.VMEM((64, frames), F32),
            pltpu.SemaphoreType.DMA((9,)),
            pltpu.SemaphoreType.DMA((6,)),
            pltpu.SemaphoreType.DMA((6,)),
            pltpu.SemaphoreType.DMA((4,)),
            pltpu.SemaphoreType.DMA((4,)),
            pltpu.SemaphoreType.DMA,
        ],
        compiler_params=pltpu.CompilerParams(
            collective_id=0, has_side_effects=True, vmem_limit_bytes=32 * 1024 * 1024
        ),
    )(
        latent,
        target,
        up_kernel,
        inner_kernel,
        outer_kernel.T,
        out_kernel,
        jnp.asarray(dft),
        jnp.asarray(mels),
        jnp.asarray(tapers),
    )
    grad, up, inner, outer, out = results
    return grad, up, inner, outer.T, out


def solution(mesh):
    return jax.shard_map(
        functools.partial(local, mesh.shape["dp"], mesh.shape["tm"]),
        mesh=mesh,
        in_specs=(P("dp", None, "tm"), P("dp", "tm"), P(), P(), P(), P()),
        out_specs=(P("dp", None, "tm"), P(), P(), P(), P()),
        check_vma=False,
    )
```

```python
import functools

import jax
import jax.numpy as jnp
import ml_dtypes
import numpy as np
from jax import lax
from jax.experimental import pallas as pl
from jax.experimental.pallas import tpu as pltpu
from jax.sharding import PartitionSpec as P

F32 = jnp.float32
BF16 = jnp.bfloat16
MESH = pl.DeviceIdType.MESH
MELS = 64
COEFFS = (0.25, 0.5, 0.5)
PARAMS = 10464
Y_HI = 2
TILES = 11


def mel_bank(window):
    half = window // 2
    top = 2595.0 * np.log10(1.0 + 12000.0 / 700.0)
    points = (np.arange(MELS + 1) + 1.0) / (MELS + 2.0) * top
    centers = 700.0 * (np.power(10.0, points / 2595.0) - 1.0) / 12000.0 * half
    spacing = np.maximum(centers[1:] - centers[:-1], 1.0)
    places = np.arange(half)[:, None]
    return np.maximum(0.0, 1.0 - np.abs(places - centers[None, :MELS]) / spacing[None, :])


def halves(x):
    high = x.astype(ml_dtypes.bfloat16)
    low = (x - high.astype(np.float64)).astype(ml_dtypes.bfloat16)
    return high, low


@functools.cache
def tables():
    lane = np.arange(256)
    place = np.where(lane < 128, 2 * lane, 2 * (lane - 128) + 1)

    def waves(bins, window):
        angle = 2.0 * np.pi * ((place[:, None] * bins[None, :]) % window) / window
        return np.cos(angle), np.sin(angle)

    p = np.arange(128)
    cos0, sin0 = waves(4 * p, 1024)
    cos2, sin2 = waves(4 * p + 2, 1024)
    cos1, sin1 = waves(4 * p + 1, 1024)
    cos3, sin3 = waves(4 * p + 3, 1024)
    t0 = np.concatenate([cos0, -sin0], axis=1)
    t2 = np.concatenate([cos2, -sin2], axis=1)
    real = np.concatenate(
        [np.concatenate([cos1, cos3], axis=1), np.concatenate([-sin1, sin3], axis=1)], axis=0
    )
    imag = np.concatenate(
        [np.concatenate([-sin1, -sin3], axis=1), np.concatenate([-cos1, cos3], axis=1)], axis=0
    )
    cosf, sinf = waves(p, 256)
    fine = np.concatenate([cosf, -sinf], axis=1)
    high, low = halves(np.concatenate([t0, t2, real, imag], axis=0))
    fine_high, fine_low = halves(fine)
    move = np.zeros((256, 256))
    move[place, lane] = 1.0
    dft = np.concatenate(
        [high, low, fine_high, fine_low, move.astype(ml_dtypes.bfloat16)], axis=0
    )
    order = np.concatenate([4 * p, 4 * p + 2, 4 * p + 1, 4 * p + 3])
    mels = np.concatenate([mel_bank(1024)[order], mel_bank(256)], axis=0)
    mels = np.concatenate(halves(mels), axis=1)
    taper = 0.5 - 0.5 * np.cos(2.0 * np.pi * (np.arange(4)[:, None] * 256 + place) / 1024)
    taper_fine = 0.5 - 0.5 * np.cos(2.0 * np.pi * place[None, :] / 256)
    tapers = np.concatenate([taper, taper_fine, np.zeros((3, 256))], axis=0).astype(np.float32)
    return dft, mels, tapers


HIGH, LOW, FINE_HIGH, FINE_LOW, MOVE, ROWS = 0, 1536, 3072, 3328, 3584, 3840


def split(x):
    high = x.astype(BF16)
    return high, (x - high.astype(F32)).astype(BF16)


def dot(a, b):
    return lax.dot_general(a, b, (((1,), (0,)), ((), ())), preferred_element_type=F32)


def dot_nt(a, b):
    return lax.dot_general(a, b, (((1,), (1,)), ((), ())), preferred_element_type=F32)


def weight_dot(w, x):
    high, low = w
    m = high.shape[0]
    xh, xl = split(x)
    both = dot(jnp.concatenate([high, low], axis=0), xh)
    return both[:m] + both[m:] + dot(high, xl)


def rows_dot(x, high, low, product=dot):
    m = x.shape[0]
    xh, xl = split(x)
    both = product(jnp.concatenate([xh, xl], axis=0), high)
    return both[:m] + both[m:] + product(xh, low)


def gram(a, b):
    m = a.shape[0]
    ah, al = split(a)
    bh, bl = split(b)
    both = dot_nt(jnp.concatenate([ah, al], axis=0), bh)
    return both[:m] + both[m:] + dot_nt(ah, bl)


def elu_and_slope(x):
    slope = jnp.exp(jnp.minimum(x, 0.0))
    return jnp.maximum(x, 0.0) + (slope - 1.0), slope


def roll(x, by, axis=1):
    return pltpu.roll(x, by % x.shape[axis], axis)


def coarse_spectrum(blocks, tapers, table):
    x = [blocks[b : b + 16, :] * tapers[b : b + 1, :] for b in range(4)]
    even, odd = x[0] + x[2], x[1] + x[3]
    cross = jnp.concatenate([x[0] - x[2], x[1] - x[3]], axis=1)
    return (
        rows_dot(even + odd, table[HIGH : HIGH + 256, :], table[LOW : LOW + 256, :]),
        rows_dot(even - odd, table[HIGH + 256 : HIGH + 512, :], table[LOW + 256 : LOW + 512, :]),
        rows_dot(cross, table[HIGH + 512 : HIGH + 1024, :], table[LOW + 512 : LOW + 1024, :]),
        rows_dot(cross, table[HIGH + 1024 : HIGH + 1536, :], table[LOW + 1024 : LOW + 1536, :]),
    )


def coarse_energy(parts):
    s0, s2, re, im = (part * part for part in parts)
    return jnp.concatenate(
        [s0[:, :128] + s0[:, 128:], s2[:, :128] + s2[:, 128:], re + im], axis=1
    )


def fine_frames(blocks, tapers):
    now, later = blocks[3:11, :], blocks[4:12, :]
    lane = lax.broadcasted_iota(jnp.int32, (8, 128), 1)
    frames = [now]
    for d in range(1, 4):
        keep = lane < 128 - 32 * d
        frames.append(
            jnp.concatenate(
                [
                    jnp.where(
                        keep,
                        roll(now[:, s : s + 128], -32 * d),
                        roll(later[:, s : s + 128], -32 * d),
                    )
                    for s in (0, 128)
                ],
                axis=1,
            )
        )
    return jnp.concatenate(frames, axis=0) * tapers[4:5, :]


def fine_spectrum(blocks, tapers, table):
    return rows_dot(
        fine_frames(blocks, tapers),
        table[FINE_HIGH : FINE_HIGH + 256, :],
        table[FINE_LOW : FINE_LOW + 256, :],
    )


def level_of(energy, bank):
    m = energy.shape[0]
    eh, el = split(energy)
    both = dot(jnp.concatenate([eh, el], axis=0), bank)
    both = both[:m] + both[m:]
    return jnp.sqrt(both + roll(both, MELS) + 1.0)


def energy_slope(level, target_level, valid, bank):
    m = level.shape[0]
    slope = jnp.where(valid, 1.0 - target_level / level, 0.0)
    sh, sl = split(slope)
    both = dot_nt(jnp.concatenate([sh, sl], axis=0), bank)
    return 2.0 * (both[:m] + both[m:])


def kernel(
    n_dp,
    n_tm,
    latent_hbm,
    target_hbm,
    up_hbm,
    inner_hbm,
    outer_hbm,
    out_hbm,
    dft_hbm,
    mels_hbm,
    tapers_hbm,
    grad_out,
    total,
    latent,
    halo,
    target_rows,
    up_k,
    inner_k,
    outer_k,
    out_k,
    table,
    mels,
    tapers,
    natural,
    target_blocks,
    wave_tiles,
    wave_blocks,
    frame_grads,
    grad_blocks,
    squares,
    packed,
    plane_rows,
    ring_rows,
    load_sem,
    near_send,
    near_recv,
    far_send,
    far_recv,
):
    dp = lax.axis_index("dp")
    tm = lax.axis_index("tm")
    n_z = n_tm // Y_HI
    n_plane = n_dp * Y_HI
    y_hi = tm // n_z
    z = lax.rem(tm, n_z)
    plane = y_hi * n_dp + dp
    right = lax.rem(tm + 1, n_tm)
    left = lax.rem(tm + n_tm - 1, n_tm)
    other = lax.rem(y_hi + 1, Y_HI) * n_z + z
    first = tm == 0
    last = tm == n_tm - 1

    barrier = pltpu.get_barrier_semaphore()

    def greet(device):
        pl.semaphore_signal(barrier, inc=1, device_id=device, device_id_type=MESH)

    @pl.loop(1, n_tm)
    def _(i):
        greet((dp, lax.rem(tm + i, n_tm)))

    @pl.loop(1, n_dp)
    def _(i):
        peer = lax.rem(dp + i, n_dp)
        greet((peer, tm))
        greet((peer, other))

    loads = [
        pltpu.make_async_copy(source, place, load_sem.at[i])
        for i, (source, place) in enumerate(
            [
                (latent_hbm.at[0], latent),
                (target_hbm, target_rows.at[1]),
                (up_hbm, up_k),
                (inner_hbm, inner_k),
                (outer_hbm, outer_k),
                (out_hbm, out_k),
                (dft_hbm, table),
                (mels_hbm, mels),
                (tapers_hbm, tapers),
            ]
        )
    ]
    for load in loads:
        load.start()
    frames = latent.shape[1]
    wide = frames + 128

    loads[2].wait()
    loads[3].wait()
    loads[4].wait()
    loads[5].wait()
    up_rows = up_k[...]
    up_all = jnp.concatenate([up_rows[r] for r in range(4)], axis=0)
    up_w = jnp.concatenate(
        [
            jnp.concatenate([up_rows[0], up_rows[2]], axis=1),
            jnp.concatenate([up_rows[1], up_rows[3]], axis=1),
        ],
        axis=0,
    )
    up_fwd = split(up_w)
    up_bwd = split(up_all.T)
    taps = jnp.concatenate(
        [inner_k[0], inner_k[1], inner_k[2], jnp.zeros((16, 32), F32)], axis=1
    )
    inner_w = jnp.concatenate([taps, roll(taps, 32)], axis=0)
    inner_fwd = split(inner_w)
    zero = jnp.zeros((16, 32), F32)
    k0, k1, k2 = inner_k[0], inner_k[1], inner_k[2]
    inner_t = jnp.concatenate(
        [
            jnp.concatenate([k1, k2], axis=1),
            jnp.concatenate([k0, k1], axis=1),
            jnp.concatenate([k2, zero], axis=1),
            jnp.concatenate([zero, k0], axis=1),
        ],
        axis=0,
    )
    inner_bwd = split(inner_t.T)
    outer_t = outer_k[...]
    outer_w = jnp.concatenate(
        [jnp.concatenate([outer_t, zero], axis=1), jnp.concatenate([zero, outer_t], axis=1)],
        axis=0,
    )
    outer_bwd = split(outer_w)
    outer_fwd = split(outer_w.T)
    pad = jnp.zeros((1, 32), F32)
    taps_out = out_k[...]
    out_w = jnp.concatenate(
        [
            jnp.concatenate([pad, taps_out], axis=0),
            jnp.concatenate([taps_out, pad], axis=0),
        ],
        axis=1,
    )
    out_w16 = jnp.concatenate([out_w, jnp.zeros((8, 64), F32)], axis=0)
    out_fwd = split(out_w16)
    out_bwd = split(out_w16.T)

    pl.semaphore_wait(barrier, n_tm - 1 + 2 * (n_dp - 1))

    def send(source, place, slot, device):
        copy = pltpu.make_async_remote_copy(
            src_ref=source,
            dst_ref=place,
            send_sem=near_send.at[slot],
            recv_sem=near_recv.at[slot],
            device_id=device,
            device_id_type=MESH,
        )
        copy.start()
        return copy

    near = [
        send(latent_hbm.at[0, :, pl.ds(frames - 128, 128)], halo.at[0], 0, (dp, right)),
        send(latent_hbm.at[0, :, pl.ds(0, 128)], halo.at[1], 1, (dp, left)),
        send(target_hbm, target_rows.at[0], 2, (dp, right)),
        send(target_hbm, target_rows.at[2], 3, (dp, left)),
    ]

    lane = lax.broadcasted_iota(jnp.int32, (1, wide), 1)
    inside = (
        (lane < frames)
        | ((lane < frames + 4) & jnp.logical_not(last))
        | ((lane >= wide - 4) & jnp.logical_not(first))
    )

    loads[0].wait()
    near[0].wait_recv()
    near[1].wait_recv()
    spot = lax.broadcasted_iota(jnp.int32, (64, 128), 1)
    rim = jnp.where(
        (spot < 4) & jnp.logical_not(last),
        halo[1],
        jnp.where((spot >= 124) & jnp.logical_not(first), halo[0], 0.0),
    )
    activated, slope_in = elu_and_slope(jnp.concatenate([latent[...], rim], axis=1))
    stacked = jnp.concatenate([activated, roll(activated, 1)], axis=0)
    upper = jnp.where(inside, weight_dot(up_fwd, stacked), 0.0)
    lifted, slope_upper = elu_and_slope(upper)
    even, odd = lifted[:32], lifted[32:]
    tapped = jnp.concatenate([roll(odd, 1), even, odd, roll(even, -1)], axis=0)
    hidden, slope_inner = elu_and_slope(weight_dot(inner_fwd, tapped))
    mixed = jnp.where(inside, upper + weight_dot(outer_fwd, hidden), 0.0)
    final, slope_mixed = elu_and_slope(mixed)
    taps_8 = weight_dot(out_fwd, final)[:8]
    row = lax.broadcasted_iota(jnp.int32, (8, wide), 0)
    moves = ((2, 0, 0), (1, 1, 2), (-1, 5, 6), (-2, 7, 7))
    aligned = taps_8
    for by, low, high in moves:
        aligned = jnp.where((row >= low) & (row <= high), roll(taps_8, by), aligned)
    aligned = aligned[:, :frames]
    aligned = aligned + roll(aligned, 4, 0)
    aligned = aligned + roll(aligned, 2, 0)
    is_even = lax.rem(row[:, :frames], 2) == 0
    swapped = roll(aligned, 1, 0)
    wave_even = jnp.where(is_even, aligned, swapped)
    wave_odd = jnp.where(is_even, swapped, aligned)
    tile = jnp.zeros((8, 128), F32)
    row_8 = row[:, :128]
    for b in range(4):
        tile = jnp.where(row_8 == b, wave_even[:, 128 * b : 128 * b + 128], tile)
        tile = jnp.where(row_8 == 4 + b, wave_odd[:, 128 * b : 128 * b + 128], tile)
    wave_tiles[1] = tile
    near += [
        send(wave_tiles.at[1], wave_tiles.at[0], 4, (dp, right)),
        send(wave_tiles.at[1], wave_tiles.at[2], 5, (dp, left)),
    ]

    for load in (loads[1], loads[6], loads[7], loads[8]):
        load.wait()
    near[2].wait_recv()
    near[3].wait_recv()
    natural[...] = jnp.zeros(natural.shape, F32)
    for s in range(3):
        for b in range(4):
            line = target_rows[s, :, 256 * b : 256 * b + 256]
            if s == 0:
                line = jnp.where(first, 0.0, line)
            if s == 2:
                line = jnp.where(last, 0.0, line)
            natural[4 * s + b : 4 * s + b + 1, :] = line
    nh, nl = split(natural[...])
    moved = dot(jnp.concatenate([nh, nl], axis=0), table[MOVE : MOVE + 256, :])
    target_blocks[...] = jnp.zeros(target_blocks.shape, F32)
    target_blocks[0:16, :] = moved[:16] + moved[16:]
    bank, bank_fine = mels[0:512, :], mels[512:640, :]
    target_coarse = level_of(coarse_energy(coarse_spectrum(target_blocks, tapers, table)), bank)
    s = fine_spectrum(target_blocks, tapers, table)
    s = s * s
    target_fine = level_of(s[:, :128] + s[:, 128:], bank_fine)

    wave_blocks[...] = jnp.zeros(wave_blocks.shape, F32)
    near[4].wait_recv()
    near[5].wait_recv()
    for s in range(3):
        for half in range(2):
            lines = wave_tiles[s, 4 * half : 4 * half + 4, :]
            if s == 0:
                lines = jnp.where(first, 0.0, lines)
            if s == 2:
                lines = jnp.where(last, 0.0, lines)
            wave_blocks[4 * s : 4 * s + 4, 128 * half : 128 * half + 128] = lines
    parts = coarse_spectrum(wave_blocks, tapers, table)
    level = level_of(coarse_energy(parts), bank)
    frame = lax.broadcasted_iota(jnp.int32, (16, 128), 0)
    index = 4 * tm + frame - 4
    valid = (frame < 9) & (index >= 0) & (index < 4 * n_tm)
    slope = energy_slope(level, target_coarse, valid, bank)
    s0, s2, re, im = parts
    twice = functools.partial(jnp.concatenate, axis=1)
    d0 = s0 * twice([slope[:, 0:128]] * 2)
    d2 = s2 * twice([slope[:, 128:256]] * 2)
    d_even = rows_dot(d0, table[HIGH : HIGH + 256, :], table[LOW : LOW + 256, :], dot_nt)
    d_odd = rows_dot(
        d2, table[HIGH + 256 : HIGH + 512, :], table[LOW + 256 : LOW + 512, :], dot_nt
    )
    d_cross = rows_dot(
        re * slope[:, 256:512],
        table[HIGH + 512 : HIGH + 1024, :],
        table[LOW + 512 : LOW + 1024, :],
        dot_nt,
    ) + rows_dot(
        im * slope[:, 256:512],
        table[HIGH + 1024 : HIGH + 1536, :],
        table[LOW + 1024 : LOW + 1536, :],
        dot_nt,
    )
    d_first, d_second = d_cross[:, :256], d_cross[:, 256:]
    both, apart = d_even + d_odd, d_even - d_odd
    for b, d in enumerate((both + d_first, apart + d_second, both - d_first, apart - d_second)):
        frame_grads[b] = d * tapers[b : b + 1, :]
    coarse = frame_grads[0, 3:11, :]
    for b in range(1, 4):
        coarse = coarse + frame_grads[b, 3 - b : 11 - b, :]

    spectrum = fine_spectrum(wave_blocks, tapers, table)
    s = spectrum * spectrum
    level = level_of(s[:, :128] + s[:, 128:], bank_fine)
    frame = lax.broadcasted_iota(jnp.int32, (32, 128), 0)
    index = 16 * tm + 4 * (lax.rem(frame, 8) - 1) + frame // 8
    valid = (index >= 0) & (index < 16 * n_tm)
    slope = energy_slope(level, target_fine, valid, bank_fine)
    d = rows_dot(
        spectrum * twice([slope] * 2),
        table[FINE_HIGH : FINE_HIGH + 256, :],
        table[FINE_LOW : FINE_LOW + 256, :],
        dot_nt,
    )
    d = d * tapers[4:5, :]
    lane_8 = lax.broadcasted_iota(jnp.int32, (8, 128), 1)
    fine = []
    for start in (0, 128):
        here = d[0:8, start : start + 128]
        after = jnp.zeros((8, 128), F32)
        for k in range(1, 4):
            moved = roll(d[8 * k : 8 * k + 8, start : start + 128], 32 * k)
            here = here + jnp.where(lane_8 >= 32 * k, moved, 0.0)
            after = after + jnp.where(lane_8 < 32 * k, moved, 0.0)
        fine.append(here + roll(after, 1, 0))
    fine = twice(fine)
    timed = 2.0 * (wave_blocks[3:11, :] - target_blocks[3:11, :])

    row_256 = lax.broadcasted_iota(jnp.int32, (8, 256), 0)
    own = (row_256 >= 1) & (row_256 <= 4)
    lane_1 = lax.broadcasted_iota(jnp.int32, (1, 128), 1)
    line = jnp.zeros((1, 128), F32)
    for i, member in enumerate((timed, coarse, fine)):
        kept = jnp.where(own, member * member, 0.0)
        line = jnp.where(lane_1 == i, jnp.sum(kept, keepdims=True), line)
    squares[tm] = line

    def far(source, place, slot, device):
        return pltpu.make_async_remote_copy(
            src_ref=source,
            dst_ref=place,
            send_sem=far_send.at[slot],
            recv_sem=far_recv.at[slot],
            device_id=device,
            device_id_type=MESH,
        )

    def arrived(ref, slot):
        pltpu.make_async_copy(ref, ref, far_recv.at[slot]).wait()

    def sent(ref, slot):
        pltpu.make_async_copy(ref, ref, far_send.at[slot]).wait()

    @pl.loop(1, n_tm)
    def _(i):
        far(squares.at[tm], squares.at[tm], 0, (dp, lax.rem(tm + i, n_tm))).start()

    grad_blocks[0] = timed
    grad_blocks[1] = coarse
    grad_blocks[2] = fine
    arrived(squares.at[pl.ds(0, n_tm - 1)], 0)
    sums = squares[0]
    for i in range(1, n_tm):
        sums = sums + squares[i]
    scale = lax.rsqrt(sums / (n_tm * 2.0 * frames) + 1e-06)
    balanced = jnp.zeros((8, 256), F32)
    for i, coeff in enumerate(COEFFS):
        balanced = balanced + grad_blocks[i] * (coeff * scale[:, i : i + 1])
    grad_blocks[0] = balanced

    spread = []
    even_8 = lax.rem(row_8, 2) == 0
    for b in range(5):
        r = b + 1
        even = jnp.broadcast_to(grad_blocks[0, r : r + 1, 0:128], (8, 128))
        odd = jnp.broadcast_to(grad_blocks[0, r : r + 1, 128:256], (8, 128))
        lines = jnp.where(even_8, even, odd)
        if b == 4:
            even = jnp.broadcast_to(grad_blocks[0, 0:1, 0:128], (8, 128))
            odd = jnp.broadcast_to(grad_blocks[0, 0:1, 128:256], (8, 128))
            lines = jnp.where(lane_8 < 64, lines, jnp.where(even_8, even, odd))
        spread.append(lines)
    wide_grad = jnp.where(inside, jnp.concatenate(spread, axis=1), 0.0)

    def shifted(x):
        result = x
        for by, low, high in moves:
            result = jnp.where((row >= low) & (row <= high), roll(x, -by), result)
        return jnp.concatenate([result, jnp.zeros_like(result)], axis=0)

    grad_final = weight_dot(out_bwd, shifted(wide_grad))
    owned = jnp.where(lane < frames, wide_grad, 0.0)
    out_rows = gram(shifted(owned), final)[:8]
    grad_mixed = jnp.where(inside, grad_final * slope_mixed, 0.0)
    outer_rows = gram(hidden[:, :frames], grad_mixed[:, :frames])
    grad_inner = weight_dot(outer_bwd, grad_mixed) * slope_inner
    inner_rows = gram(grad_inner[:, :frames], tapped[:, :frames])
    even, odd = grad_inner[:16], grad_inner[16:]
    around = jnp.concatenate([even, odd, roll(odd, 1), roll(even, -1)], axis=0)
    grad_lifted = weight_dot(inner_bwd, around)
    grad_upper = jnp.where(inside, grad_mixed + grad_lifted * slope_upper, 0.0)
    packed[0:64, :] = gram(grad_upper[:, :frames], stacked[:, :frames])
    taps = inner_rows[:16] + roll(inner_rows[16:], -32)
    pair = outer_rows[:16, :32] + outer_rows[16:, 32:]
    packed[64:80, :] = jnp.concatenate([taps[:, :96], pair], axis=1)
    taps_7 = out_rows[0:7, 32:64] + out_rows[1:8, 0:32]
    packed[80:88, :] = jnp.zeros((8, 128), F32)
    packed[80:87, 0:32] = taps_7

    for i in range(TILES):
        owner = (i * n_plane) // TILES
        chunk = packed.at[pl.ds(8 * i, 8)]
        mine = plane == owner

        @pl.when(mine)
        def _():
            plane_rows[plane] = chunk[...]

        @pl.when(jnp.logical_not(mine))
        def _():
            far(
                chunk, plane_rows.at[plane], 1, (owner % n_dp, (owner // n_dp) * n_z + z)
            ).start()

    after = jnp.concatenate([grad_upper, roll(grad_upper, -1)], axis=0)
    grad_out[...] = weight_dot(up_bwd, after[:, :frames]) * slope_in[:, :frames]

    tile_index = (plane * TILES + n_plane - 1) // n_plane
    owns = (tile_index < TILES) & ((tile_index * n_plane) // TILES == plane)
    tile_rows = pl.ds(pl.multiple_of(8 * tile_index, 8), 8)

    @pl.when(owns)
    def _():
        arrived(plane_rows.at[pl.ds(0, n_plane - 1)], 1)
        chunk = plane_rows[0]
        for i in range(1, n_plane):
            chunk = chunk + plane_rows[i]
        ring_rows[z] = chunk

        @pl.loop(1, n_z)
        def _(i):
            peer = y_hi * n_z + lax.rem(z + i, n_z)
            far(ring_rows.at[z], ring_rows.at[z], 2, (dp, peer)).start()

        arrived(ring_rows.at[pl.ds(0, n_z - 1)], 2)
        chunk = ring_rows[0]
        for i in range(1, n_z):
            chunk = chunk + ring_rows[i]
        total[tile_rows, :] = chunk

        @pl.loop(1, n_plane)
        def _(i):
            peer = lax.rem(plane + i, n_plane)
            far(
                total.at[tile_rows],
                total.at[tile_rows],
                3,
                (lax.rem(peer, n_dp), (peer // n_dp) * n_z + z),
            ).start()

        arrived(total.at[pl.ds(0, 8 * (TILES - 1))], 3)

    @pl.when(jnp.logical_not(owns))
    def _():
        arrived(total.at[pl.ds(0, 8 * TILES)], 3)

    for copy in near:
        copy.wait_send()
    sent(squares.at[pl.ds(0, n_tm - 1)], 0)

    @pl.when(owns)
    def _():
        sent(packed.at[pl.ds(0, 8 * (TILES - 1))], 1)
        sent(ring_rows.at[pl.ds(0, n_z - 1)], 2)
        sent(plane_rows.at[pl.ds(0, n_plane - 1)], 3)

    @pl.when(jnp.logical_not(owns))
    def _():
        sent(packed.at[pl.ds(0, 8 * TILES)], 1)


def finish(grad_ref, total_ref, latent_ref, up_ref, inner_ref, outer_ref, out_ref):
    latent_ref[0] = grad_ref[...]
    sums = total_ref[...]
    square = jnp.sum(sums * sums, keepdims=True)
    factor = jnp.minimum(1.0, lax.rsqrt(square / PARAMS + 1e-06))
    sums = sums * factor
    up_ref[0] = sums[0:32, 0:64]
    up_ref[1] = sums[32:64, 0:64]
    up_ref[2] = sums[0:32, 64:128]
    up_ref[3] = sums[32:64, 64:128]
    for j in range(3):
        inner_ref[j] = sums[64:80, 32 * j : 32 * j + 32]
    outer_ref[...] = sums[64:80, 96:128]
    out_ref[...] = sums[80:87, 0:32]


def local(n_dp, n_tm, latent, target, up_kernel, inner_kernel, outer_kernel, out_kernel):
    dft, mels, tapers = tables()
    frames = latent.shape[2]
    n_z = n_tm // Y_HI
    n_plane = n_dp * Y_HI
    shape = jax.ShapeDtypeStruct
    hbm = pl.BlockSpec(memory_space=pltpu.HBM)
    vmem = pl.BlockSpec(memory_space=pltpu.VMEM)
    grad, total = pl.pallas_call(
        functools.partial(kernel, n_dp, n_tm),
        out_shape=(shape((64, frames), F32), shape((8 * TILES, 128), F32)),
        in_specs=[hbm] * 9,
        out_specs=(vmem, vmem),
        scratch_shapes=[
            pltpu.VMEM((64, frames), F32),
            pltpu.VMEM((2, 64, 128), F32),
            pltpu.VMEM((3, 1, 2 * frames), F32),
            pltpu.VMEM((4, 32, 64), F32),
            pltpu.VMEM((3, 16, 32), F32),
            pltpu.VMEM((16, 32), F32),
            pltpu.VMEM((7, 32), F32),
            pltpu.VMEM((ROWS, 256), BF16),
            pltpu.VMEM((640, 128), BF16),
            pltpu.VMEM((8, 256), F32),
            pltpu.VMEM((16, 256), F32),
            pltpu.VMEM((24, 256), F32),
            pltpu.VMEM((3, 8, 128), F32),
            pltpu.VMEM((24, 256), F32),
            pltpu.VMEM((4, 16, 256), F32),
            pltpu.VMEM((3, 8, 256), F32),
            pltpu.VMEM((n_tm, 1, 128), F32),
            pltpu.VMEM((8 * TILES, 128), F32),
            pltpu.VMEM((n_plane, 8, 128), F32),
            pltpu.VMEM((n_z, 8, 128), F32),
            pltpu.SemaphoreType.DMA((9,)),
            pltpu.SemaphoreType.DMA((6,)),
            pltpu.SemaphoreType.DMA((6,)),
            pltpu.SemaphoreType.DMA((4,)),
            pltpu.SemaphoreType.DMA((4,)),
        ],
        compiler_params=pltpu.CompilerParams(
            collective_id=0, has_side_effects=True, vmem_limit_bytes=60 * 1024 * 1024
        ),
    )(
        latent,
        target,
        up_kernel,
        inner_kernel,
        outer_kernel.T,
        out_kernel,
        jnp.asarray(dft),
        jnp.asarray(mels),
        jnp.asarray(tapers),
    )
    grad, up, inner, outer, out = pl.pallas_call(
        finish,
        out_shape=(
            shape(latent.shape, F32),
            shape((4, 32, 64), F32),
            shape((3, 16, 32), F32),
            shape((16, 32), F32),
            shape((7, 32), F32),
        ),
        in_specs=[vmem] * 2,
        out_specs=(vmem,) * 5,
    )(grad, total)
    return grad, up, inner, outer.T, out


def solution(mesh):
    return jax.shard_map(
        functools.partial(local, mesh.shape["dp"], mesh.shape["tm"]),
        mesh=mesh,
        in_specs=(P("dp", None, "tm"), P("dp", "tm"), P(), P(), P(), P()),
        out_specs=(P("dp", None, "tm"), P(), P(), P(), P()),
        check_vma=False,
    )
```

```python
import functools

import jax
import jax.numpy as jnp
import ml_dtypes
import numpy as np
from jax import lax
from jax.experimental import pallas as pl
from jax.experimental.pallas import tpu as pltpu
from jax.sharding import PartitionSpec as P

F32 = jnp.float32
BF16 = jnp.bfloat16
MESH = pl.DeviceIdType.MESH
MELS = 64
COEFFS = (0.25, 0.5, 0.5)
PARAMS = 10464
Y_HI = 2
TILES = 11


def mel_bank(window):
    half = window // 2
    top = 2595.0 * np.log10(1.0 + 12000.0 / 700.0)
    points = (np.arange(MELS + 1) + 1.0) / (MELS + 2.0) * top
    centers = 700.0 * (np.power(10.0, points / 2595.0) - 1.0) / 12000.0 * half
    spacing = np.maximum(centers[1:] - centers[:-1], 1.0)
    places = np.arange(half)[:, None]
    return np.maximum(0.0, 1.0 - np.abs(places - centers[None, :MELS]) / spacing[None, :])


def halves(x):
    high = x.astype(ml_dtypes.bfloat16)
    low = (x - high.astype(np.float64)).astype(ml_dtypes.bfloat16)
    return high, low


@functools.cache
def tables():
    lane = np.arange(256)
    place = np.where(lane < 128, 2 * lane, 2 * (lane - 128) + 1)

    def waves(bins, window):
        angle = 2.0 * np.pi * ((place[:, None] * bins[None, :]) % window) / window
        return np.cos(angle), np.sin(angle)

    p = np.arange(128)
    cos0, sin0 = waves(4 * p, 1024)
    cos2, sin2 = waves(4 * p + 2, 1024)
    cos1, sin1 = waves(4 * p + 1, 1024)
    cos3, sin3 = waves(4 * p + 3, 1024)
    t0 = np.concatenate([cos0, -sin0], axis=1)
    t2 = np.concatenate([cos2, -sin2], axis=1)
    real = np.concatenate(
        [np.concatenate([cos1, cos3], axis=1), np.concatenate([-sin1, sin3], axis=1)], axis=0
    )
    imag = np.concatenate(
        [np.concatenate([-sin1, -sin3], axis=1), np.concatenate([-cos1, cos3], axis=1)], axis=0
    )
    cosf, sinf = waves(p, 256)
    fine = np.concatenate([cosf, -sinf], axis=1)
    high, low = halves(np.concatenate([t0, t2, real, imag], axis=0))
    fine_high, fine_low = halves(fine)
    move = np.zeros((256, 256))
    move[place, lane] = 1.0
    dft = np.concatenate(
        [high, low, fine_high, fine_low, move.astype(ml_dtypes.bfloat16)], axis=0
    )
    order = np.concatenate([4 * p, 4 * p + 2, 4 * p + 1, 4 * p + 3])
    mels = np.concatenate([mel_bank(1024)[order], mel_bank(256)], axis=0)
    mels = np.concatenate(halves(mels), axis=1)
    taper = 0.5 - 0.5 * np.cos(2.0 * np.pi * (np.arange(4)[:, None] * 256 + place) / 1024)
    taper_fine = 0.5 - 0.5 * np.cos(2.0 * np.pi * place[None, :] / 256)
    tapers = np.concatenate([taper, taper_fine, np.zeros((3, 256))], axis=0).astype(np.float32)
    return dft, mels, tapers


HIGH, LOW, FINE_HIGH, FINE_LOW, MOVE, ROWS = 0, 1536, 3072, 3328, 3584, 3840


def split(x):
    high = x.astype(BF16)
    return high, (x - high.astype(F32)).astype(BF16)


def dot(a, b):
    return lax.dot_general(a, b, (((1,), (0,)), ((), ())), preferred_element_type=F32)


def dot_nt(a, b):
    return lax.dot_general(a, b, (((1,), (1,)), ((), ())), preferred_element_type=F32)


def weight_dot(w, x):
    high, low = w
    m = high.shape[0]
    xh, xl = split(x)
    both = dot(jnp.concatenate([high, low], axis=0), xh)
    return both[:m] + both[m:] + dot(high, xl)


def rows_dot(x, high, low, product=dot):
    m = x.shape[0]
    xh, xl = split(x)
    both = product(jnp.concatenate([xh, xl], axis=0), high)
    return both[:m] + both[m:] + product(xh, low)


def gram(a, b):
    m = a.shape[0]
    ah, al = split(a)
    bh, bl = split(b)
    both = dot_nt(jnp.concatenate([ah, al], axis=0), bh)
    return both[:m] + both[m:] + dot_nt(ah, bl)


def elu_and_slope(x):
    slope = jnp.exp(jnp.minimum(x, 0.0))
    return jnp.maximum(x, 0.0) + (slope - 1.0), slope


def roll(x, by, axis=1):
    return pltpu.roll(x, by % x.shape[axis], axis)


def coarse_spectrum(blocks, tapers, table):
    x = [blocks[b : b + 16, :] * tapers[b : b + 1, :] for b in range(4)]
    even, odd = x[0] + x[2], x[1] + x[3]
    cross = jnp.concatenate([x[0] - x[2], x[1] - x[3]], axis=1)
    return (
        rows_dot(even + odd, table[HIGH : HIGH + 256, :], table[LOW : LOW + 256, :]),
        rows_dot(even - odd, table[HIGH + 256 : HIGH + 512, :], table[LOW + 256 : LOW + 512, :]),
        rows_dot(cross, table[HIGH + 512 : HIGH + 1024, :], table[LOW + 512 : LOW + 1024, :]),
        rows_dot(cross, table[HIGH + 1024 : HIGH + 1536, :], table[LOW + 1024 : LOW + 1536, :]),
    )


def coarse_energy(parts):
    s0, s2, re, im = (part * part for part in parts)
    return jnp.concatenate(
        [s0[:, :128] + s0[:, 128:], s2[:, :128] + s2[:, 128:], re + im], axis=1
    )


def fine_frames(blocks, tapers):
    now, later = blocks[3:11, :], blocks[4:12, :]
    lane = lax.broadcasted_iota(jnp.int32, (8, 128), 1)
    frames = [now]
    for d in range(1, 4):
        keep = lane < 128 - 32 * d
        frames.append(
            jnp.concatenate(
                [
                    jnp.where(
                        keep,
                        roll(now[:, s : s + 128], -32 * d),
                        roll(later[:, s : s + 128], -32 * d),
                    )
                    for s in (0, 128)
                ],
                axis=1,
            )
        )
    return jnp.concatenate(frames, axis=0) * tapers[4:5, :]


def fine_spectrum(blocks, tapers, table):
    return rows_dot(
        fine_frames(blocks, tapers),
        table[FINE_HIGH : FINE_HIGH + 256, :],
        table[FINE_LOW : FINE_LOW + 256, :],
    )


def level_of(energy, bank):
    m = energy.shape[0]
    eh, el = split(energy)
    both = dot(jnp.concatenate([eh, el], axis=0), bank)
    both = both[:m] + both[m:]
    return jnp.sqrt(both + roll(both, MELS) + 1.0)


def energy_slope(level, target_level, valid, bank):
    m = level.shape[0]
    slope = jnp.where(valid, 1.0 - target_level / level, 0.0)
    sh, sl = split(slope)
    both = dot_nt(jnp.concatenate([sh, sl], axis=0), bank)
    return 2.0 * (both[:m] + both[m:])


def kernel(
    n_dp,
    n_tm,
    latent_hbm,
    target_hbm,
    up_hbm,
    inner_hbm,
    outer_hbm,
    out_hbm,
    dft_hbm,
    mels_hbm,
    tapers_hbm,
    grad_out,
    total,
    latent,
    halo,
    target_rows,
    up_k,
    inner_k,
    outer_k,
    out_k,
    table,
    mels,
    tapers,
    natural,
    target_blocks,
    wave_tiles,
    wave_blocks,
    frame_grads,
    grad_blocks,
    squares,
    packed,
    packed_rows,
    grad_rows,
    plane_rows,
    ring_rows,
    load_sem,
    near_send,
    near_recv,
    far_send,
    far_recv,
):
    dp = lax.axis_index("dp")
    tm = lax.axis_index("tm")
    n_z = n_tm // Y_HI
    n_plane = n_dp * Y_HI
    y_hi = tm // n_z
    z = lax.rem(tm, n_z)
    plane = y_hi * n_dp + dp
    right = lax.rem(tm + 1, n_tm)
    left = lax.rem(tm + n_tm - 1, n_tm)
    other = lax.rem(y_hi + 1, Y_HI) * n_z + z
    first = tm == 0
    last = tm == n_tm - 1

    barrier = pltpu.get_barrier_semaphore()

    def owner_of(index):
        return (index * n_plane) // TILES

    def tile_of(member):
        return (member * TILES + n_plane - 1) // n_plane

    def is_owner(member):
        index = tile_of(member)
        return (index < TILES) & (owner_of(index) == member)

    def along_z(i):
        half = (i + 1) // 2
        return lax.rem(z + n_z // 2 + half - 2 * half * lax.rem(i, 2) + n_z, n_z)

    def in_plane(visit):
        core, x, y_lo = lax.rem(dp, 2), lax.rem(dp // 2, 4), dp // 8
        for dx in (2, 1, 3, 0):

            @pl.loop(0, 8 if dx else 7)
            def _(i):
                bits = 7 - i
                y = lax.rem(y_hi + bits // 4, 2)
                y_in = lax.rem(y_lo + lax.rem(bits // 2, 2), 2)
                side = lax.rem(core + lax.rem(bits, 2), 2)
                visit(y * n_dp + y_in * 8 + lax.rem(x + dx, 4) * 2 + side)

    def member_id(member):
        return (lax.rem(member, n_dp), (member // n_dp) * n_z + z)

    owns = is_owner(plane)
    partner = lax.rem(y_hi + 1, Y_HI) * n_dp + dp

    def greet(device):
        pl.semaphore_signal(barrier, inc=1, device_id=device, device_id_type=MESH)

    @pl.loop(0, n_z - 1)
    def _(i):
        greet((dp, y_hi * n_z + along_z(i)))
        greet((dp, other - z + along_z(i)))

    greet((dp, other))

    def greet_member(member):
        @pl.when((owns | is_owner(member)) & (member != partner))
        def _():
            greet(member_id(member))

    in_plane(greet_member)
    greeted = jnp.where(owns, n_plane - 2, TILES - jnp.where(is_owner(partner), 1, 0))

    loads = [
        pltpu.make_async_copy(source, place, load_sem.at[i])
        for i, (source, place) in enumerate(
            [
                (latent_hbm.at[0], latent),
                (target_hbm, target_rows.at[1]),
                (up_hbm, up_k),
                (inner_hbm, inner_k),
                (outer_hbm, outer_k),
                (out_hbm, out_k),
                (dft_hbm, table),
                (mels_hbm, mels),
                (tapers_hbm, tapers),
            ]
        )
    ]
    for load in loads:
        load.start()
    frames = latent.shape[1]
    wide = frames + 128

    loads[2].wait()
    loads[3].wait()
    loads[4].wait()
    loads[5].wait()
    up_rows = up_k[...]
    up_all = jnp.concatenate([up_rows[r] for r in range(4)], axis=0)
    up_w = jnp.concatenate(
        [
            jnp.concatenate([up_rows[0], up_rows[2]], axis=1),
            jnp.concatenate([up_rows[1], up_rows[3]], axis=1),
        ],
        axis=0,
    )
    up_fwd = split(up_w)
    up_bwd = split(up_all.T)
    taps = jnp.concatenate(
        [inner_k[0], inner_k[1], inner_k[2], jnp.zeros((16, 32), F32)], axis=1
    )
    inner_w = jnp.concatenate([taps, roll(taps, 32)], axis=0)
    inner_fwd = split(inner_w)
    zero = jnp.zeros((16, 32), F32)
    k0, k1, k2 = inner_k[0], inner_k[1], inner_k[2]
    inner_t = jnp.concatenate(
        [
            jnp.concatenate([k1, k2], axis=1),
            jnp.concatenate([k0, k1], axis=1),
            jnp.concatenate([k2, zero], axis=1),
            jnp.concatenate([zero, k0], axis=1),
        ],
        axis=0,
    )
    inner_bwd = split(inner_t.T)
    outer_t = outer_k[...]
    outer_w = jnp.concatenate(
        [jnp.concatenate([outer_t, zero], axis=1), jnp.concatenate([zero, outer_t], axis=1)],
        axis=0,
    )
    outer_bwd = split(outer_w)
    outer_fwd = split(outer_w.T)
    pad = jnp.zeros((1, 32), F32)
    taps_out = out_k[...]
    out_w = jnp.concatenate(
        [
            jnp.concatenate([pad, taps_out], axis=0),
            jnp.concatenate([taps_out, pad], axis=0),
        ],
        axis=1,
    )
    out_w16 = jnp.concatenate([out_w, jnp.zeros((8, 64), F32)], axis=0)
    out_fwd = split(out_w16)
    out_bwd = split(out_w16.T)

    loads[0].wait()
    lane_8 = lax.broadcasted_iota(jnp.int32, (8, 128), 1)
    lent = jnp.zeros((8, 128), F32)
    for g in range(8):
        start = latent[8 * g : 8 * g + 8, 0:128]
        end = latent[8 * g : 8 * g + 8, frames - 128 : frames]
        lent = jnp.where(lane_8 // 4 == g, roll(start, 4 * g), lent)
        lent = jnp.where(lane_8 // 4 == 16 + g, roll(end, 4 * g - 60), lent)
    halo[1] = lent

    pl.semaphore_wait(barrier, n_tm - 1 + greeted)

    def send(source, place, slot, device):
        copy = pltpu.make_async_remote_copy(
            src_ref=source,
            dst_ref=place,
            send_sem=near_send.at[slot],
            recv_sem=near_recv.at[slot],
            device_id=device,
            device_id_type=MESH,
        )
        copy.start()
        return copy

    near = [
        send(halo.at[1], halo.at[0], 0, (dp, right)),
        send(halo.at[1], halo.at[2], 1, (dp, left)),
        send(target_hbm, target_rows.at[0], 2, (dp, right)),
        send(target_hbm, target_rows.at[2], 3, (dp, left)),
    ]

    lane = lax.broadcasted_iota(jnp.int32, (1, wide), 1)
    inside = (
        (lane < frames)
        | ((lane < frames + 4) & jnp.logical_not(last))
        | ((lane >= wide - 4) & jnp.logical_not(first))
    )

    near[0].wait_recv()
    near[1].wait_recv()
    before, behind = halo[0], halo[2]
    rim = []
    for g in range(8):
        tile = jnp.where((lane_8 < 4) & jnp.logical_not(last), roll(behind, -4 * g), 0.0)
        rim.append(
            jnp.where((lane_8 >= 124) & jnp.logical_not(first), roll(before, 60 - 4 * g), tile)
        )
    rim = jnp.concatenate(rim, axis=0)
    activated, slope_in = elu_and_slope(jnp.concatenate([latent[...], rim], axis=1))
    stacked = jnp.concatenate([activated, roll(activated, 1)], axis=0)
    upper = jnp.where(inside, weight_dot(up_fwd, stacked), 0.0)
    lifted, slope_upper = elu_and_slope(upper)
    even, odd = lifted[:32], lifted[32:]
    tapped = jnp.concatenate([roll(odd, 1), even, odd, roll(even, -1)], axis=0)
    hidden, slope_inner = elu_and_slope(weight_dot(inner_fwd, tapped))
    mixed = jnp.where(inside, upper + weight_dot(outer_fwd, hidden), 0.0)
    final, slope_mixed = elu_and_slope(mixed)
    taps_8 = weight_dot(out_fwd, final)[:8]
    row = lax.broadcasted_iota(jnp.int32, (8, wide), 0)
    moves = ((2, 0, 0), (1, 1, 2), (-1, 5, 6), (-2, 7, 7))
    aligned = taps_8
    for by, low, high in moves:
        aligned = jnp.where((row >= low) & (row <= high), roll(taps_8, by), aligned)
    aligned = aligned[:, :frames]
    aligned = aligned + roll(aligned, 4, 0)
    aligned = aligned + roll(aligned, 2, 0)
    is_even = lax.rem(row[:, :frames], 2) == 0
    swapped = roll(aligned, 1, 0)
    wave_even = jnp.where(is_even, aligned, swapped)
    wave_odd = jnp.where(is_even, swapped, aligned)
    tile = jnp.zeros((8, 128), F32)
    row_8 = row[:, :128]
    for b in range(4):
        tile = jnp.where(row_8 == b, wave_even[:, 128 * b : 128 * b + 128], tile)
        tile = jnp.where(row_8 == 4 + b, wave_odd[:, 128 * b : 128 * b + 128], tile)
    wave_tiles[1] = tile
    near += [
        send(wave_tiles.at[1], wave_tiles.at[0], 4, (dp, right)),
        send(wave_tiles.at[1], wave_tiles.at[2], 5, (dp, left)),
    ]

    for load in (loads[1], loads[6], loads[7], loads[8]):
        load.wait()
    near[2].wait_recv()
    near[3].wait_recv()
    natural[...] = jnp.zeros(natural.shape, F32)
    for s in range(3):
        for b in range(4):
            line = target_rows[s, :, 256 * b : 256 * b + 256]
            if s == 0:
                line = jnp.where(first, 0.0, line)
            if s == 2:
                line = jnp.where(last, 0.0, line)
            natural[4 * s + b : 4 * s + b + 1, :] = line
    nh, nl = split(natural[...])
    moved = dot(jnp.concatenate([nh, nl], axis=0), table[MOVE : MOVE + 256, :])
    target_blocks[...] = jnp.zeros(target_blocks.shape, F32)
    target_blocks[0:16, :] = moved[:16] + moved[16:]
    bank, bank_fine = mels[0:512, :], mels[512:640, :]
    target_coarse = level_of(coarse_energy(coarse_spectrum(target_blocks, tapers, table)), bank)
    s = fine_spectrum(target_blocks, tapers, table)
    s = s * s
    target_fine = level_of(s[:, :128] + s[:, 128:], bank_fine)

    wave_blocks[...] = jnp.zeros(wave_blocks.shape, F32)
    near[4].wait_recv()
    near[5].wait_recv()
    for s in range(3):
        for half in range(2):
            lines = wave_tiles[s, 4 * half : 4 * half + 4, :]
            if s == 0:
                lines = jnp.where(first, 0.0, lines)
            if s == 2:
                lines = jnp.where(last, 0.0, lines)
            wave_blocks[4 * s : 4 * s + 4, 128 * half : 128 * half + 128] = lines
    parts = coarse_spectrum(wave_blocks, tapers, table)
    level = level_of(coarse_energy(parts), bank)
    frame = lax.broadcasted_iota(jnp.int32, (16, 128), 0)
    index = 4 * tm + frame - 4
    valid = (frame < 9) & (index >= 0) & (index < 4 * n_tm)
    slope = energy_slope(level, target_coarse, valid, bank)
    s0, s2, re, im = parts
    twice = functools.partial(jnp.concatenate, axis=1)
    d0 = s0 * twice([slope[:, 0:128]] * 2)
    d2 = s2 * twice([slope[:, 128:256]] * 2)
    d_even = rows_dot(d0, table[HIGH : HIGH + 256, :], table[LOW : LOW + 256, :], dot_nt)
    d_odd = rows_dot(
        d2, table[HIGH + 256 : HIGH + 512, :], table[LOW + 256 : LOW + 512, :], dot_nt
    )
    d_cross = rows_dot(
        re * slope[:, 256:512],
        table[HIGH + 512 : HIGH + 1024, :],
        table[LOW + 512 : LOW + 1024, :],
        dot_nt,
    ) + rows_dot(
        im * slope[:, 256:512],
        table[HIGH + 1024 : HIGH + 1536, :],
        table[LOW + 1024 : LOW + 1536, :],
        dot_nt,
    )
    d_first, d_second = d_cross[:, :256], d_cross[:, 256:]
    both, apart = d_even + d_odd, d_even - d_odd
    for b, d in enumerate((both + d_first, apart + d_second, both - d_first, apart - d_second)):
        frame_grads[b] = d * tapers[b : b + 1, :]
    coarse = frame_grads[0, 3:11, :]
    for b in range(1, 4):
        coarse = coarse + frame_grads[b, 3 - b : 11 - b, :]

    spectrum = fine_spectrum(wave_blocks, tapers, table)
    s = spectrum * spectrum
    level = level_of(s[:, :128] + s[:, 128:], bank_fine)
    frame = lax.broadcasted_iota(jnp.int32, (32, 128), 0)
    index = 16 * tm + 4 * (lax.rem(frame, 8) - 1) + frame // 8
    valid = (index >= 0) & (index < 16 * n_tm)
    slope = energy_slope(level, target_fine, valid, bank_fine)
    d = rows_dot(
        spectrum * twice([slope] * 2),
        table[FINE_HIGH : FINE_HIGH + 256, :],
        table[FINE_LOW : FINE_LOW + 256, :],
        dot_nt,
    )
    d = d * tapers[4:5, :]
    fine = []
    for start in (0, 128):
        here = d[0:8, start : start + 128]
        after = jnp.zeros((8, 128), F32)
        for k in range(1, 4):
            moved = roll(d[8 * k : 8 * k + 8, start : start + 128], 32 * k)
            here = here + jnp.where(lane_8 >= 32 * k, moved, 0.0)
            after = after + jnp.where(lane_8 < 32 * k, moved, 0.0)
        fine.append(here + roll(after, 1, 0))
    fine = twice(fine)
    timed = 2.0 * (wave_blocks[3:11, :] - target_blocks[3:11, :])

    row_256 = lax.broadcasted_iota(jnp.int32, (8, 256), 0)
    own = (row_256 >= 1) & (row_256 <= 4)
    lane_1 = lax.broadcasted_iota(jnp.int32, (1, 128), 1)
    line = jnp.zeros((1, 128), F32)
    for i, member in enumerate((timed, coarse, fine)):
        kept = jnp.where(own, member * member, 0.0)
        line = jnp.where(lane_1 == i, jnp.sum(kept, keepdims=True), line)
    squares[tm] = line

    def far(source, place, slot, device):
        return pltpu.make_async_remote_copy(
            src_ref=source,
            dst_ref=place,
            send_sem=far_send.at[slot],
            recv_sem=far_recv.at[slot],
            device_id=device,
            device_id_type=MESH,
        )

    def arrived(ref, slot):
        pltpu.make_async_copy(ref, ref, far_recv.at[slot]).wait()

    def sent(ref, slot):
        pltpu.make_async_copy(ref, ref, far_send.at[slot]).wait()

    @pl.loop(0, n_z - 1)
    def _(i):
        far(squares.at[tm], squares.at[tm], 0, (dp, other - z + along_z(i))).start()
        far(squares.at[tm], squares.at[tm], 0, (dp, y_hi * n_z + along_z(i))).start()

    far(squares.at[tm], squares.at[tm], 0, (dp, other)).start()

    grad_blocks[0] = timed
    grad_blocks[1] = coarse
    grad_blocks[2] = fine
    even_8 = lax.rem(row_8, 2) == 0

    def shifted(x):
        result = x
        for by, low, high in moves:
            result = jnp.where((row >= low) & (row <= high), roll(x, -by), result)
        return jnp.concatenate([result, jnp.zeros_like(result)], axis=0)

    for i in range(3):
        spread = []
        for b in range(5):
            r = b + 1
            even = jnp.broadcast_to(grad_blocks[i, r : r + 1, 0:128], (8, 128))
            odd = jnp.broadcast_to(grad_blocks[i, r : r + 1, 128:256], (8, 128))
            lines = jnp.where(even_8, even, odd)
            if b == 4:
                even = jnp.broadcast_to(grad_blocks[i, 0:1, 0:128], (8, 128))
                odd = jnp.broadcast_to(grad_blocks[i, 0:1, 128:256], (8, 128))
                lines = jnp.where(lane_8 < 64, lines, jnp.where(even_8, even, odd))
            spread.append(lines)
        wide_grad = jnp.where(inside, jnp.concatenate(spread, axis=1), 0.0)
        grad_final = weight_dot(out_bwd, shifted(wide_grad))
        owned = jnp.where(lane < frames, wide_grad, 0.0)
        out_rows = gram(shifted(owned), final)[:8]
        grad_mixed = jnp.where(inside, grad_final * slope_mixed, 0.0)
        outer_rows = gram(hidden[:, :frames], grad_mixed[:, :frames])
        grad_inner = weight_dot(outer_bwd, grad_mixed) * slope_inner
        inner_rows = gram(grad_inner[:, :frames], tapped[:, :frames])
        even, odd = grad_inner[:16], grad_inner[16:]
        around = jnp.concatenate([even, odd, roll(odd, 1), roll(even, -1)], axis=0)
        grad_lifted = weight_dot(inner_bwd, around)
        grad_upper = jnp.where(inside, grad_mixed + grad_lifted * slope_upper, 0.0)
        packed_rows[i, 0:64, :] = gram(grad_upper[:, :frames], stacked[:, :frames])
        taps = inner_rows[:16] + roll(inner_rows[16:], -32)
        pair = outer_rows[:16, :32] + outer_rows[16:, 32:]
        packed_rows[i, 64:80, :] = jnp.concatenate([taps[:, :96], pair], axis=1)
        taps_7 = out_rows[0:7, 32:64] + out_rows[1:8, 0:32]
        packed_rows[i, 80:88, :] = jnp.zeros((8, 128), F32)
        packed_rows[i, 80:87, 0:32] = taps_7
        after = jnp.concatenate([grad_upper, roll(grad_upper, -1)], axis=0)
        grad_rows[i] = weight_dot(up_bwd, after[:, :frames]) * slope_in[:, :frames]

    arrived(squares.at[pl.ds(0, n_tm - 1)], 0)
    sums = squares[0]
    for i in range(1, n_tm):
        sums = sums + squares[i]
    scale = lax.rsqrt(sums / (n_tm * 2.0 * frames) + 1e-06)
    scales = [coeff * scale[:, i : i + 1] for i, coeff in enumerate(COEFFS)]

    def combined(rows):
        return scales[0] * rows[0] + scales[1] * rows[1] + scales[2] * rows[2]

    packed[...] = combined(packed_rows)

    for i in range(TILES):
        owner = owner_of(i)
        chunk = packed.at[pl.ds(8 * i, 8)]
        mine = plane == owner

        @pl.when(mine)
        def _():
            plane_rows[plane] = chunk[...]

        @pl.when(jnp.logical_not(mine))
        def _():
            far(
                chunk, plane_rows.at[plane], 1, (owner % n_dp, (owner // n_dp) * n_z + z)
            ).start()

    grad_out[...] = combined(grad_rows)

    tile_index = tile_of(plane)
    tile_rows = pl.ds(pl.multiple_of(8 * tile_index, 8), 8)

    @pl.when(owns)
    def _():
        arrived(plane_rows.at[pl.ds(0, n_plane - 1)], 1)
        chunk = plane_rows[0]
        for i in range(1, n_plane):
            chunk = chunk + plane_rows[i]
        ring_rows[z] = chunk

        @pl.loop(0, n_z - 1)
        def _(i):
            far(ring_rows.at[z], ring_rows.at[z], 2, (dp, y_hi * n_z + along_z(i))).start()

        arrived(ring_rows.at[pl.ds(0, n_z - 1)], 2)
        chunk = ring_rows[0]
        for i in range(1, n_z):
            chunk = chunk + ring_rows[i]
        total[tile_rows, :] = chunk

        def give(member):
            far(total.at[tile_rows], total.at[tile_rows], 3, member_id(member)).start()

        in_plane(give)
        arrived(total.at[pl.ds(0, 8 * (TILES - 1))], 3)

    @pl.when(jnp.logical_not(owns))
    def _():
        arrived(total.at[pl.ds(0, 8 * TILES)], 3)

    for copy in near:
        copy.wait_send()
    sent(squares.at[pl.ds(0, n_tm - 1)], 0)

    @pl.when(owns)
    def _():
        sent(packed.at[pl.ds(0, 8 * (TILES - 1))], 1)
        sent(ring_rows.at[pl.ds(0, n_z - 1)], 2)
        sent(plane_rows.at[pl.ds(0, n_plane - 1)], 3)

    @pl.when(jnp.logical_not(owns))
    def _():
        sent(packed.at[pl.ds(0, 8 * TILES)], 1)


def finish(grad_ref, total_ref, latent_ref, up_ref, inner_ref, outer_ref, out_ref):
    latent_ref[0] = grad_ref[...]
    sums = total_ref[...]
    square = jnp.sum(sums * sums, keepdims=True)
    factor = jnp.minimum(1.0, lax.rsqrt(square / PARAMS + 1e-06))
    sums = sums * factor
    up_ref[0] = sums[0:32, 0:64]
    up_ref[1] = sums[32:64, 0:64]
    up_ref[2] = sums[0:32, 64:128]
    up_ref[3] = sums[32:64, 64:128]
    for j in range(3):
        inner_ref[j] = sums[64:80, 32 * j : 32 * j + 32]
    outer_ref[...] = sums[64:80, 96:128]
    out_ref[...] = sums[80:87, 0:32]


def local(n_dp, n_tm, latent, target, up_kernel, inner_kernel, outer_kernel, out_kernel):
    dft, mels, tapers = tables()
    frames = latent.shape[2]
    n_z = n_tm // Y_HI
    n_plane = n_dp * Y_HI
    shape = jax.ShapeDtypeStruct
    hbm = pl.BlockSpec(memory_space=pltpu.HBM)
    vmem = pl.BlockSpec(memory_space=pltpu.VMEM)
    grad, total = pl.pallas_call(
        functools.partial(kernel, n_dp, n_tm),
        out_shape=(shape((64, frames), F32), shape((8 * TILES, 128), F32)),
        in_specs=[hbm] * 9,
        out_specs=(vmem, vmem),
        scratch_shapes=[
            pltpu.VMEM((64, frames), F32),
            pltpu.VMEM((3, 8, 128), F32),
            pltpu.VMEM((3, 1, 2 * frames), F32),
            pltpu.VMEM((4, 32, 64), F32),
            pltpu.VMEM((3, 16, 32), F32),
            pltpu.VMEM((16, 32), F32),
            pltpu.VMEM((7, 32), F32),
            pltpu.VMEM((ROWS, 256), BF16),
            pltpu.VMEM((640, 128), BF16),
            pltpu.VMEM((8, 256), F32),
            pltpu.VMEM((16, 256), F32),
            pltpu.VMEM((24, 256), F32),
            pltpu.VMEM((3, 8, 128), F32),
            pltpu.VMEM((24, 256), F32),
            pltpu.VMEM((4, 16, 256), F32),
            pltpu.VMEM((3, 8, 256), F32),
            pltpu.VMEM((n_tm, 1, 128), F32),
            pltpu.VMEM((8 * TILES, 128), F32),
            pltpu.VMEM((3, 8 * TILES, 128), F32),
            pltpu.VMEM((3, 64, frames), F32),
            pltpu.VMEM((n_plane, 8, 128), F32),
            pltpu.VMEM((n_z, 8, 128), F32),
            pltpu.SemaphoreType.DMA((9,)),
            pltpu.SemaphoreType.DMA((6,)),
            pltpu.SemaphoreType.DMA((6,)),
            pltpu.SemaphoreType.DMA((4,)),
            pltpu.SemaphoreType.DMA((4,)),
        ],
        compiler_params=pltpu.CompilerParams(
            collective_id=0, has_side_effects=True, vmem_limit_bytes=60 * 1024 * 1024
        ),
    )(
        latent,
        target,
        up_kernel,
        inner_kernel,
        outer_kernel.T,
        out_kernel,
        jnp.asarray(dft),
        jnp.asarray(mels),
        jnp.asarray(tapers),
    )
    grad, up, inner, outer, out = pl.pallas_call(
        finish,
        out_shape=(
            shape(latent.shape, F32),
            shape((4, 32, 64), F32),
            shape((3, 16, 32), F32),
            shape((16, 32), F32),
            shape((7, 32), F32),
        ),
        in_specs=[vmem] * 2,
        out_specs=(vmem,) * 5,
    )(grad, total)
    return grad, up, inner, outer.T, out


def solution(mesh):
    return jax.shard_map(
        functools.partial(local, mesh.shape["dp"], mesh.shape["tm"]),
        mesh=mesh,
        in_specs=(P("dp", None, "tm"), P("dp", "tm"), P(), P(), P(), P()),
        out_specs=(P("dp", None, "tm"), P(), P(), P(), P()),
        check_vma=False,
    )
```

```python
import functools

import jax
import jax.numpy as jnp
import ml_dtypes
import numpy as np
from jax import lax
from jax.experimental import pallas as pl
from jax.experimental.pallas import tpu as pltpu
from jax.sharding import PartitionSpec as P

F32 = jnp.float32
BF16 = jnp.bfloat16
MESH = pl.DeviceIdType.MESH
MELS = 64
COEFFS = (0.25, 0.5, 0.5)
PARAMS = 10464
Y_HI = 2
TILES = 11


def mel_bank(window):
    half = window // 2
    top = 2595.0 * np.log10(1.0 + 12000.0 / 700.0)
    points = (np.arange(MELS + 1) + 1.0) / (MELS + 2.0) * top
    centers = 700.0 * (np.power(10.0, points / 2595.0) - 1.0) / 12000.0 * half
    spacing = np.maximum(centers[1:] - centers[:-1], 1.0)
    places = np.arange(half)[:, None]
    return np.maximum(0.0, 1.0 - np.abs(places - centers[None, :MELS]) / spacing[None, :])


def halves(x):
    high = x.astype(ml_dtypes.bfloat16)
    low = (x - high.astype(np.float64)).astype(ml_dtypes.bfloat16)
    return high, low


@functools.cache
def tables():
    lane = np.arange(256)
    place = np.where(lane < 128, 2 * lane, 2 * (lane - 128) + 1)

    def waves(bins, window):
        angle = 2.0 * np.pi * ((place[:, None] * bins[None, :]) % window) / window
        return np.cos(angle), np.sin(angle)

    p = np.arange(128)
    cos0, sin0 = waves(4 * p, 1024)
    cos2, sin2 = waves(4 * p + 2, 1024)
    cos1, sin1 = waves(4 * p + 1, 1024)
    cos3, sin3 = waves(4 * p + 3, 1024)
    t0 = np.concatenate([cos0, -sin0], axis=1)
    t2 = np.concatenate([cos2, -sin2], axis=1)
    real = np.concatenate(
        [np.concatenate([cos1, cos3], axis=1), np.concatenate([-sin1, sin3], axis=1)], axis=0
    )
    imag = np.concatenate(
        [np.concatenate([-sin1, -sin3], axis=1), np.concatenate([-cos1, cos3], axis=1)], axis=0
    )
    cosf, sinf = waves(p, 256)
    fine = np.concatenate([cosf, -sinf], axis=1)
    high, low = halves(np.concatenate([t0, t2, real, imag], axis=0))
    fine_high, fine_low = halves(fine)
    move = np.zeros((256, 256))
    move[place, lane] = 1.0
    dft = np.concatenate(
        [high, low, fine_high, fine_low, move.astype(ml_dtypes.bfloat16)], axis=0
    )
    order = np.concatenate([4 * p, 4 * p + 2, 4 * p + 1, 4 * p + 3])
    mels = np.concatenate([mel_bank(1024)[order], mel_bank(256)], axis=0)
    mels = np.concatenate(halves(mels), axis=1)
    taper = 0.5 - 0.5 * np.cos(2.0 * np.pi * (np.arange(4)[:, None] * 256 + place) / 1024)
    taper_fine = 0.5 - 0.5 * np.cos(2.0 * np.pi * place[None, :] / 256)
    tapers = np.concatenate([taper, taper_fine, np.zeros((3, 256))], axis=0).astype(np.float32)
    return dft, mels, tapers


HIGH, LOW, FINE_HIGH, FINE_LOW, MOVE, ROWS = 0, 1536, 3072, 3328, 3584, 3840


def split(x):
    high = x.astype(BF16)
    return high, (x - high.astype(F32)).astype(BF16)


def dot(a, b):
    return lax.dot_general(a, b, (((1,), (0,)), ((), ())), preferred_element_type=F32)


def dot_nt(a, b):
    return lax.dot_general(a, b, (((1,), (1,)), ((), ())), preferred_element_type=F32)


def weight_dot(w, x):
    high, low = w
    m = high.shape[0]
    xh, xl = split(x)
    both = dot(jnp.concatenate([high, low], axis=0), xh)
    return both[:m] + both[m:] + dot(high, xl)


def rows_dot(x, high, low, product=dot):
    m = x.shape[0]
    xh, xl = split(x)
    both = product(jnp.concatenate([xh, xl], axis=0), high)
    return both[:m] + both[m:] + product(xh, low)


def gram(a, b):
    m = a.shape[0]
    ah, al = split(a)
    bh, bl = split(b)
    both = dot_nt(jnp.concatenate([ah, al], axis=0), bh)
    return both[:m] + both[m:] + dot_nt(ah, bl)


def elu_and_slope(x):
    slope = jnp.exp(jnp.minimum(x, 0.0))
    return jnp.maximum(x, 0.0) + (slope - 1.0), slope


def roll(x, by, axis=1):
    return pltpu.roll(x, by % x.shape[axis], axis)


def coarse_spectrum(blocks, tapers, table):
    x = [blocks[b : b + 16, :] * tapers[b : b + 1, :] for b in range(4)]
    even, odd = x[0] + x[2], x[1] + x[3]
    cross = jnp.concatenate([x[0] - x[2], x[1] - x[3]], axis=1)
    return (
        rows_dot(even + odd, table[HIGH : HIGH + 256, :], table[LOW : LOW + 256, :]),
        rows_dot(even - odd, table[HIGH + 256 : HIGH + 512, :], table[LOW + 256 : LOW + 512, :]),
        rows_dot(cross, table[HIGH + 512 : HIGH + 1024, :], table[LOW + 512 : LOW + 1024, :]),
        rows_dot(cross, table[HIGH + 1024 : HIGH + 1536, :], table[LOW + 1024 : LOW + 1536, :]),
    )


def coarse_energy(parts):
    s0, s2, re, im = (part * part for part in parts)
    return jnp.concatenate(
        [s0[:, :128] + s0[:, 128:], s2[:, :128] + s2[:, 128:], re + im], axis=1
    )


def fine_frames(blocks, tapers):
    now, later = blocks[3:11, :], blocks[4:12, :]
    lane = lax.broadcasted_iota(jnp.int32, (8, 128), 1)
    frames = [now]
    for d in range(1, 4):
        keep = lane < 128 - 32 * d
        frames.append(
            jnp.concatenate(
                [
                    jnp.where(
                        keep,
                        roll(now[:, s : s + 128], -32 * d),
                        roll(later[:, s : s + 128], -32 * d),
                    )
                    for s in (0, 128)
                ],
                axis=1,
            )
        )
    return jnp.concatenate(frames, axis=0) * tapers[4:5, :]


def fine_spectrum(blocks, tapers, table):
    return rows_dot(
        fine_frames(blocks, tapers),
        table[FINE_HIGH : FINE_HIGH + 256, :],
        table[FINE_LOW : FINE_LOW + 256, :],
    )


def level_of(energy, bank):
    m = energy.shape[0]
    eh, el = split(energy)
    both = dot(jnp.concatenate([eh, el], axis=0), bank)
    both = both[:m] + both[m:]
    return jnp.sqrt(both + roll(both, MELS) + 1.0)


def energy_slope(level, target_level, valid, bank):
    m = level.shape[0]
    slope = jnp.where(valid, 1.0 - target_level / level, 0.0)
    sh, sl = split(slope)
    both = dot_nt(jnp.concatenate([sh, sl], axis=0), bank)
    return 2.0 * (both[:m] + both[m:])


def kernel(
    n_dp,
    n_tm,
    latent_hbm,
    target_hbm,
    up_hbm,
    inner_hbm,
    outer_hbm,
    out_hbm,
    dft_hbm,
    mels_hbm,
    tapers_hbm,
    grad_out,
    total,
    latent,
    halo,
    target_rows,
    up_k,
    inner_k,
    outer_k,
    out_k,
    table,
    mels,
    tapers,
    natural,
    target_blocks,
    wave_tiles,
    wave_blocks,
    frame_grads,
    grad_blocks,
    squares,
    packed_rows,
    grad_rows,
    halves_own,
    plane_halves,
    plane_rows,
    ring_rows,
    load_sem,
    near_send,
    near_recv,
    far_send,
    far_recv,
):
    dp = lax.axis_index("dp")
    tm = lax.axis_index("tm")
    n_z = n_tm // Y_HI
    n_plane = n_dp * Y_HI
    y_hi = tm // n_z
    z = lax.rem(tm, n_z)
    plane = y_hi * n_dp + dp
    right = lax.rem(tm + 1, n_tm)
    left = lax.rem(tm + n_tm - 1, n_tm)
    other = lax.rem(y_hi + 1, Y_HI) * n_z + z
    first = tm == 0
    last = tm == n_tm - 1

    barrier = pltpu.get_barrier_semaphore()

    def owner_of(index):
        return (index * n_plane) // TILES

    def tile_of(member):
        return (member * TILES + n_plane - 1) // n_plane

    def is_owner(member):
        index = tile_of(member)
        return (index < TILES) & (owner_of(index) == member)

    def along_z(i):
        half = (i + 1) // 2
        return lax.rem(z + n_z // 2 + half - 2 * half * lax.rem(i, 2) + n_z, n_z)

    def in_plane(visit):
        core, x, y_lo = lax.rem(dp, 2), lax.rem(dp // 2, 4), dp // 8
        for dx in (2, 1, 3, 0):

            @pl.loop(0, 8 if dx else 7)
            def _(i):
                bits = 7 - i
                y = lax.rem(y_hi + bits // 4, 2)
                y_in = lax.rem(y_lo + lax.rem(bits // 2, 2), 2)
                side = lax.rem(core + lax.rem(bits, 2), 2)
                visit(y * n_dp + y_in * 8 + lax.rem(x + dx, 4) * 2 + side)

    def member_id(member):
        return (lax.rem(member, n_dp), (member // n_dp) * n_z + z)

    owns = is_owner(plane)
    partner = lax.rem(y_hi + 1, Y_HI) * n_dp + dp

    def greet(device):
        pl.semaphore_signal(barrier, inc=1, device_id=device, device_id_type=MESH)

    @pl.loop(0, n_z - 1)
    def _(i):
        greet((dp, y_hi * n_z + along_z(i)))

    greet((dp, other))

    @pl.when(z == n_z - 1)
    def _():
        greet((dp, right))

    @pl.when(z == 0)
    def _():
        greet((dp, left))

    def greet_member(member):
        @pl.when((owns | is_owner(member)) & (member != partner))
        def _():
            greet(member_id(member))

    in_plane(greet_member)
    greeted = n_z + jnp.where((z == 0) | (z == n_z - 1), 1, 0)
    greeted += jnp.where(owns, n_plane - 2, TILES - jnp.where(is_owner(partner), 1, 0))

    loads = [
        pltpu.make_async_copy(source, place, load_sem.at[i])
        for i, (source, place) in enumerate(
            [
                (latent_hbm.at[0], latent),
                (target_hbm, target_rows.at[1]),
                (up_hbm, up_k),
                (inner_hbm, inner_k),
                (outer_hbm, outer_k),
                (out_hbm, out_k),
                (dft_hbm, table),
                (mels_hbm, mels),
                (tapers_hbm, tapers),
            ]
        )
    ]
    for load in loads:
        load.start()
    frames = latent.shape[1]
    wide = frames + 128

    loads[2].wait()
    loads[3].wait()
    loads[4].wait()
    loads[5].wait()
    up_rows = up_k[...]
    up_all = jnp.concatenate([up_rows[r] for r in range(4)], axis=0)
    up_w = jnp.concatenate(
        [
            jnp.concatenate([up_rows[0], up_rows[2]], axis=1),
            jnp.concatenate([up_rows[1], up_rows[3]], axis=1),
        ],
        axis=0,
    )
    up_fwd = split(up_w)
    up_bwd = split(up_all.T)
    taps = jnp.concatenate(
        [inner_k[0], inner_k[1], inner_k[2], jnp.zeros((16, 32), F32)], axis=1
    )
    inner_w = jnp.concatenate([taps, roll(taps, 32)], axis=0)
    inner_fwd = split(inner_w)
    zero = jnp.zeros((16, 32), F32)
    k0, k1, k2 = inner_k[0], inner_k[1], inner_k[2]
    inner_t = jnp.concatenate(
        [
            jnp.concatenate([k1, k2], axis=1),
            jnp.concatenate([k0, k1], axis=1),
            jnp.concatenate([k2, zero], axis=1),
            jnp.concatenate([zero, k0], axis=1),
        ],
        axis=0,
    )
    inner_bwd = split(inner_t.T)
    outer_t = outer_k[...]
    outer_w = jnp.concatenate(
        [jnp.concatenate([outer_t, zero], axis=1), jnp.concatenate([zero, outer_t], axis=1)],
        axis=0,
    )
    outer_bwd = split(outer_w)
    outer_fwd = split(outer_w.T)
    pad = jnp.zeros((1, 32), F32)
    taps_out = out_k[...]
    out_w = jnp.concatenate(
        [
            jnp.concatenate([pad, taps_out], axis=0),
            jnp.concatenate([taps_out, pad], axis=0),
        ],
        axis=1,
    )
    out_w16 = jnp.concatenate([out_w, jnp.zeros((8, 64), F32)], axis=0)
    out_fwd = split(out_w16)
    out_bwd = split(out_w16.T)

    loads[0].wait()
    lane_8 = lax.broadcasted_iota(jnp.int32, (8, 128), 1)
    lent = jnp.zeros((8, 128), F32)
    for g in range(8):
        start = latent[8 * g : 8 * g + 8, 0:128]
        end = latent[8 * g : 8 * g + 8, frames - 128 : frames]
        lent = jnp.where(lane_8 // 4 == g, roll(start, 4 * g), lent)
        lent = jnp.where(lane_8 // 4 == 16 + g, roll(end, 4 * g - 60), lent)
    halo[1] = lent

    pl.semaphore_wait(barrier, greeted)

    def send(source, place, slot, device):
        copy = pltpu.make_async_remote_copy(
            src_ref=source,
            dst_ref=place,
            send_sem=near_send.at[slot],
            recv_sem=near_recv.at[slot],
            device_id=device,
            device_id_type=MESH,
        )
        copy.start()
        return copy

    near = [
        send(halo.at[1], halo.at[0], 0, (dp, right)),
        send(halo.at[1], halo.at[2], 1, (dp, left)),
        send(target_hbm, target_rows.at[0], 2, (dp, right)),
        send(target_hbm, target_rows.at[2], 3, (dp, left)),
    ]

    lane = lax.broadcasted_iota(jnp.int32, (1, wide), 1)
    inside = (
        (lane < frames)
        | ((lane < frames + 4) & jnp.logical_not(last))
        | ((lane >= wide - 4) & jnp.logical_not(first))
    )

    near[0].wait_recv()
    near[1].wait_recv()
    before, behind = halo[0], halo[2]
    rim = []
    for g in range(8):
        tile = jnp.where((lane_8 < 4) & jnp.logical_not(last), roll(behind, -4 * g), 0.0)
        rim.append(
            jnp.where((lane_8 >= 124) & jnp.logical_not(first), roll(before, 60 - 4 * g), tile)
        )
    rim = jnp.concatenate(rim, axis=0)
    activated, slope_in = elu_and_slope(jnp.concatenate([latent[...], rim], axis=1))
    stacked = jnp.concatenate([activated, roll(activated, 1)], axis=0)
    upper = jnp.where(inside, weight_dot(up_fwd, stacked), 0.0)
    lifted, slope_upper = elu_and_slope(upper)
    even, odd = lifted[:32], lifted[32:]
    tapped = jnp.concatenate([roll(odd, 1), even, odd, roll(even, -1)], axis=0)
    hidden, slope_inner = elu_and_slope(weight_dot(inner_fwd, tapped))
    mixed = jnp.where(inside, upper + weight_dot(outer_fwd, hidden), 0.0)
    final, slope_mixed = elu_and_slope(mixed)
    taps_8 = weight_dot(out_fwd, final)[:8]
    row = lax.broadcasted_iota(jnp.int32, (8, wide), 0)
    moves = ((2, 0, 0), (1, 1, 2), (-1, 5, 6), (-2, 7, 7))
    aligned = taps_8
    for by, low, high in moves:
        aligned = jnp.where((row >= low) & (row <= high), roll(taps_8, by), aligned)
    aligned = aligned[:, :frames]
    aligned = aligned + roll(aligned, 4, 0)
    aligned = aligned + roll(aligned, 2, 0)
    is_even = lax.rem(row[:, :frames], 2) == 0
    swapped = roll(aligned, 1, 0)
    wave_even = jnp.where(is_even, aligned, swapped)
    wave_odd = jnp.where(is_even, swapped, aligned)
    tile = jnp.zeros((8, 128), F32)
    row_8 = row[:, :128]
    for b in range(4):
        tile = jnp.where(row_8 == b, wave_even[:, 128 * b : 128 * b + 128], tile)
        tile = jnp.where(row_8 == 4 + b, wave_odd[:, 128 * b : 128 * b + 128], tile)
    wave_tiles[1] = tile
    near += [
        send(wave_tiles.at[1], wave_tiles.at[0], 4, (dp, right)),
        send(wave_tiles.at[1], wave_tiles.at[2], 5, (dp, left)),
    ]

    for load in (loads[1], loads[6], loads[7], loads[8]):
        load.wait()
    near[2].wait_recv()
    near[3].wait_recv()
    natural[...] = jnp.zeros(natural.shape, F32)
    for s in range(3):
        for b in range(4):
            line = target_rows[s, :, 256 * b : 256 * b + 256]
            if s == 0:
                line = jnp.where(first, 0.0, line)
            if s == 2:
                line = jnp.where(last, 0.0, line)
            natural[4 * s + b : 4 * s + b + 1, :] = line
    nh, nl = split(natural[...])
    moved = dot(jnp.concatenate([nh, nl], axis=0), table[MOVE : MOVE + 256, :])
    target_blocks[...] = jnp.zeros(target_blocks.shape, F32)
    target_blocks[0:16, :] = moved[:16] + moved[16:]
    bank, bank_fine = mels[0:512, :], mels[512:640, :]
    target_coarse = level_of(coarse_energy(coarse_spectrum(target_blocks, tapers, table)), bank)
    s = fine_spectrum(target_blocks, tapers, table)
    s = s * s
    target_fine = level_of(s[:, :128] + s[:, 128:], bank_fine)

    wave_blocks[...] = jnp.zeros(wave_blocks.shape, F32)
    near[4].wait_recv()
    near[5].wait_recv()
    for s in range(3):
        for half in range(2):
            lines = wave_tiles[s, 4 * half : 4 * half + 4, :]
            if s == 0:
                lines = jnp.where(first, 0.0, lines)
            if s == 2:
                lines = jnp.where(last, 0.0, lines)
            wave_blocks[4 * s : 4 * s + 4, 128 * half : 128 * half + 128] = lines
    parts = coarse_spectrum(wave_blocks, tapers, table)
    level = level_of(coarse_energy(parts), bank)
    frame = lax.broadcasted_iota(jnp.int32, (16, 128), 0)
    index = 4 * tm + frame - 4
    valid = (frame < 9) & (index >= 0) & (index < 4 * n_tm)
    slope = energy_slope(level, target_coarse, valid, bank)
    s0, s2, re, im = parts
    twice = functools.partial(jnp.concatenate, axis=1)
    d0 = s0 * twice([slope[:, 0:128]] * 2)
    d2 = s2 * twice([slope[:, 128:256]] * 2)
    d_even = rows_dot(d0, table[HIGH : HIGH + 256, :], table[LOW : LOW + 256, :], dot_nt)
    d_odd = rows_dot(
        d2, table[HIGH + 256 : HIGH + 512, :], table[LOW + 256 : LOW + 512, :], dot_nt
    )
    d_cross = rows_dot(
        re * slope[:, 256:512],
        table[HIGH + 512 : HIGH + 1024, :],
        table[LOW + 512 : LOW + 1024, :],
        dot_nt,
    ) + rows_dot(
        im * slope[:, 256:512],
        table[HIGH + 1024 : HIGH + 1536, :],
        table[LOW + 1024 : LOW + 1536, :],
        dot_nt,
    )
    d_first, d_second = d_cross[:, :256], d_cross[:, 256:]
    both, apart = d_even + d_odd, d_even - d_odd
    for b, d in enumerate((both + d_first, apart + d_second, both - d_first, apart - d_second)):
        frame_grads[b] = d * tapers[b : b + 1, :]
    coarse = frame_grads[0, 3:11, :]
    for b in range(1, 4):
        coarse = coarse + frame_grads[b, 3 - b : 11 - b, :]

    spectrum = fine_spectrum(wave_blocks, tapers, table)
    s = spectrum * spectrum
    level = level_of(s[:, :128] + s[:, 128:], bank_fine)
    frame = lax.broadcasted_iota(jnp.int32, (32, 128), 0)
    index = 16 * tm + 4 * (lax.rem(frame, 8) - 1) + frame // 8
    valid = (index >= 0) & (index < 16 * n_tm)
    slope = energy_slope(level, target_fine, valid, bank_fine)
    d = rows_dot(
        spectrum * twice([slope] * 2),
        table[FINE_HIGH : FINE_HIGH + 256, :],
        table[FINE_LOW : FINE_LOW + 256, :],
        dot_nt,
    )
    d = d * tapers[4:5, :]
    fine = []
    for start in (0, 128):
        here = d[0:8, start : start + 128]
        after = jnp.zeros((8, 128), F32)
        for k in range(1, 4):
            moved = roll(d[8 * k : 8 * k + 8, start : start + 128], 32 * k)
            here = here + jnp.where(lane_8 >= 32 * k, moved, 0.0)
            after = after + jnp.where(lane_8 < 32 * k, moved, 0.0)
        fine.append(here + roll(after, 1, 0))
    fine = twice(fine)
    timed = 2.0 * (wave_blocks[3:11, :] - target_blocks[3:11, :])

    row_256 = lax.broadcasted_iota(jnp.int32, (8, 256), 0)
    own = (row_256 >= 1) & (row_256 <= 4)
    lane_1 = lax.broadcasted_iota(jnp.int32, (1, 128), 1)
    line = jnp.zeros((1, 128), F32)
    for i, member in enumerate((timed, coarse, fine)):
        kept = jnp.where(own, member * member, 0.0)
        line = jnp.where(lane_1 == i, jnp.sum(kept, keepdims=True), line)
    squares[z] = line

    def far(source, place, slot, device):
        return pltpu.make_async_remote_copy(
            src_ref=source,
            dst_ref=place,
            send_sem=far_send.at[slot],
            recv_sem=far_recv.at[slot],
            device_id=device,
            device_id_type=MESH,
        )

    def arrived(ref, slot):
        pltpu.make_async_copy(ref, ref, far_recv.at[slot]).wait()

    def sent(ref, slot):
        pltpu.make_async_copy(ref, ref, far_send.at[slot]).wait()

    @pl.loop(0, n_z - 1)
    def _(i):
        far(squares.at[z], squares.at[z], 0, (dp, y_hi * n_z + along_z(i))).start()

    grad_blocks[0] = timed
    grad_blocks[1] = coarse
    grad_blocks[2] = fine
    even_8 = lax.rem(row_8, 2) == 0

    def shifted(x):
        result = x
        for by, low, high in moves:
            result = jnp.where((row >= low) & (row <= high), roll(x, -by), result)
        return jnp.concatenate([result, jnp.zeros_like(result)], axis=0)

    for i in range(3):
        spread = []
        for b in range(5):
            r = b + 1
            even = jnp.broadcast_to(grad_blocks[i, r : r + 1, 0:128], (8, 128))
            odd = jnp.broadcast_to(grad_blocks[i, r : r + 1, 128:256], (8, 128))
            lines = jnp.where(even_8, even, odd)
            if b == 4:
                even = jnp.broadcast_to(grad_blocks[i, 0:1, 0:128], (8, 128))
                odd = jnp.broadcast_to(grad_blocks[i, 0:1, 128:256], (8, 128))
                lines = jnp.where(lane_8 < 64, lines, jnp.where(even_8, even, odd))
            spread.append(lines)
        wide_grad = jnp.where(inside, jnp.concatenate(spread, axis=1), 0.0)
        grad_final = weight_dot(out_bwd, shifted(wide_grad))
        owned = jnp.where(lane < frames, wide_grad, 0.0)
        out_rows = gram(shifted(owned), final)[:8]
        grad_mixed = jnp.where(inside, grad_final * slope_mixed, 0.0)
        outer_rows = gram(hidden[:, :frames], grad_mixed[:, :frames])
        grad_inner = weight_dot(outer_bwd, grad_mixed) * slope_inner
        inner_rows = gram(grad_inner[:, :frames], tapped[:, :frames])
        even, odd = grad_inner[:16], grad_inner[16:]
        around = jnp.concatenate([even, odd, roll(odd, 1), roll(even, -1)], axis=0)
        grad_lifted = weight_dot(inner_bwd, around)
        grad_upper = jnp.where(inside, grad_mixed + grad_lifted * slope_upper, 0.0)
        packed_rows[i, 0:64, :] = gram(grad_upper[:, :frames], stacked[:, :frames])
        taps = inner_rows[:16] + roll(inner_rows[16:], -32)
        pair = outer_rows[:16, :32] + outer_rows[16:, 32:]
        packed_rows[i, 64:80, :] = jnp.concatenate([taps[:, :96], pair], axis=1)
        taps_7 = out_rows[0:7, 32:64] + out_rows[1:8, 0:32]
        packed_rows[i, 80:88, :] = jnp.zeros((8, 128), F32)
        packed_rows[i, 80:87, 0:32] = taps_7
        after = jnp.concatenate([grad_upper, roll(grad_upper, -1)], axis=0)
        grad_rows[i] = weight_dot(up_bwd, after[:, :frames]) * slope_in[:, :frames]

    for i in range(TILES):
        owner = owner_of(i)
        chunk = packed_rows.at[:, pl.ds(8 * i, 8)]
        mine = plane == owner

        @pl.when(mine)
        def _():
            plane_rows[plane] = chunk[...]

        @pl.when(jnp.logical_not(mine))
        def _():
            far(chunk, plane_rows.at[plane], 1, member_id(owner)).start()

    arrived(squares.at[pl.ds(0, n_z - 1)], 0)
    sums = squares[0]
    for i in range(1, n_z):
        sums = sums + squares[i]
    halves_own[0] = sums
    for i in range(TILES):
        owner = owner_of(i)
        mine = plane == owner

        @pl.when(mine)
        def _():
            plane_halves[plane] = sums

        @pl.when(jnp.logical_not(mine))
        def _():
            far(halves_own.at[0], plane_halves.at[plane], 4, member_id(owner)).start()

    far(halves_own.at[0], halves_own.at[1], 5, (dp, other)).start()

    def scales_of(sums):
        coeffs = jnp.where(lane_1 == 0, COEFFS[0], jnp.where(lane_1 == 1, COEFFS[1], COEFFS[2]))
        return coeffs * lax.rsqrt(sums / (n_tm * 2.0 * frames) + 1e-06)

    arrived(halves_own.at[1], 5)
    scales = scales_of(halves_own[0] + halves_own[1])
    grad_out[...] = (
        scales[:, 0:1] * grad_rows[0] + scales[:, 1:2] * grad_rows[1] + scales[:, 2:3] * grad_rows[2]
    )

    tile_index = tile_of(plane)
    tile_rows = pl.ds(pl.multiple_of(8 * tile_index, 8), 8)

    @pl.when(owns)
    def _():
        arrived(plane_rows.at[pl.ds(0, n_plane - 1)], 1)
        arrived(plane_halves.at[pl.ds(0, n_plane - 1)], 4)
        chunk = jnp.zeros((8, 128), F32)
        for c in range(n_dp):
            scales = scales_of(plane_halves[c] + plane_halves[n_dp + c])
            for i in range(3):
                both = plane_rows[c, i] + plane_rows[n_dp + c, i]
                chunk = chunk + scales[:, i : i + 1] * both
        ring_rows[z] = chunk

        @pl.loop(0, n_z - 1)
        def _(i):
            far(ring_rows.at[z], ring_rows.at[z], 2, (dp, y_hi * n_z + along_z(i))).start()

        arrived(ring_rows.at[pl.ds(0, n_z - 1)], 2)
        chunk = ring_rows[0]
        for i in range(1, n_z):
            chunk = chunk + ring_rows[i]
        total[tile_rows, :] = chunk

        def give(member):
            far(total.at[tile_rows], total.at[tile_rows], 3, member_id(member)).start()

        in_plane(give)
        arrived(total.at[pl.ds(0, 8 * (TILES - 1))], 3)

    @pl.when(jnp.logical_not(owns))
    def _():
        arrived(total.at[pl.ds(0, 8 * TILES)], 3)

    for copy in near:
        copy.wait_send()
    sent(squares.at[pl.ds(0, n_z - 1)], 0)
    sent(halves_own.at[0], 5)

    @pl.when(owns)
    def _():
        sent(plane_rows.at[pl.ds(0, TILES - 1)], 1)
        sent(plane_halves.at[pl.ds(0, TILES - 1)], 4)
        sent(ring_rows.at[pl.ds(0, n_z - 1)], 2)
        sent(plane_rows.at[pl.ds(0, n_plane - 1), 0], 3)

    @pl.when(jnp.logical_not(owns))
    def _():
        sent(plane_rows.at[pl.ds(0, TILES)], 1)
        sent(plane_halves.at[pl.ds(0, TILES)], 4)


def finish(grad_ref, total_ref, latent_ref, up_ref, inner_ref, outer_ref, out_ref, store_sem):
    store = pltpu.make_async_copy(grad_ref, latent_ref.at[0], store_sem)
    store.start()
    sums = total_ref[...]
    square = jnp.sum(sums * sums, keepdims=True)
    factor = jnp.minimum(1.0, lax.rsqrt(square / PARAMS + 1e-06))
    sums = sums * factor
    up_ref[0] = sums[0:32, 0:64]
    up_ref[1] = sums[32:64, 0:64]
    up_ref[2] = sums[0:32, 64:128]
    up_ref[3] = sums[32:64, 64:128]
    for j in range(3):
        inner_ref[j] = sums[64:80, 32 * j : 32 * j + 32]
    outer_ref[...] = sums[64:80, 96:128]
    out_ref[...] = sums[80:87, 0:32]
    store.wait()


def local(n_dp, n_tm, latent, target, up_kernel, inner_kernel, outer_kernel, out_kernel):
    dft, mels, tapers = tables()
    frames = latent.shape[2]
    n_z = n_tm // Y_HI
    n_plane = n_dp * Y_HI
    shape = jax.ShapeDtypeStruct
    hbm = pl.BlockSpec(memory_space=pltpu.HBM)
    vmem = pl.BlockSpec(memory_space=pltpu.VMEM)
    grad, total = pl.pallas_call(
        functools.partial(kernel, n_dp, n_tm),
        out_shape=(pltpu.VMEM((64, frames), F32), pltpu.VMEM((8 * TILES, 128), F32)),
        in_specs=[hbm] * 9,
        out_specs=(vmem, vmem),
        scratch_shapes=[
            pltpu.VMEM((64, frames), F32),
            pltpu.VMEM((3, 8, 128), F32),
            pltpu.VMEM((3, 1, 2 * frames), F32),
            pltpu.VMEM((4, 32, 64), F32),
            pltpu.VMEM((3, 16, 32), F32),
            pltpu.VMEM((16, 32), F32),
            pltpu.VMEM((7, 32), F32),
            pltpu.VMEM((ROWS, 256), BF16),
            pltpu.VMEM((640, 128), BF16),
            pltpu.VMEM((8, 256), F32),
            pltpu.VMEM((16, 256), F32),
            pltpu.VMEM((24, 256), F32),
            pltpu.VMEM((3, 8, 128), F32),
            pltpu.VMEM((24, 256), F32),
            pltpu.VMEM((4, 16, 256), F32),
            pltpu.VMEM((3, 8, 256), F32),
            pltpu.VMEM((n_z, 1, 128), F32),
            pltpu.VMEM((3, 8 * TILES, 128), F32),
            pltpu.VMEM((3, 64, frames), F32),
            pltpu.VMEM((2, 1, 128), F32),
            pltpu.VMEM((n_plane, 1, 128), F32),
            pltpu.VMEM((n_plane, 3, 8, 128), F32),
            pltpu.VMEM((n_z, 8, 128), F32),
            pltpu.SemaphoreType.DMA((9,)),
            pltpu.SemaphoreType.DMA((6,)),
            pltpu.SemaphoreType.DMA((6,)),
            pltpu.SemaphoreType.DMA((6,)),
            pltpu.SemaphoreType.DMA((6,)),
        ],
        compiler_params=pltpu.CompilerParams(
            collective_id=0, has_side_effects=True, vmem_limit_bytes=32 * 1024 * 1024
        ),
    )(
        *(
            pltpu.with_memory_space_constraint(x, pltpu.HBM)
            for x in (
                latent,
                target,
                up_kernel,
                inner_kernel,
                outer_kernel.T,
                out_kernel,
                jnp.asarray(dft),
                jnp.asarray(mels),
                jnp.asarray(tapers),
            )
        )
    )
    grad, up, inner, outer, out = pl.pallas_call(
        finish,
        out_shape=(
            shape(latent.shape, F32),
            shape((4, 32, 64), F32),
            shape((3, 16, 32), F32),
            shape((16, 32), F32),
            shape((7, 32), F32),
        ),
        in_specs=[vmem] * 2,
        out_specs=(hbm, vmem, vmem, vmem, vmem),
        scratch_shapes=[pltpu.SemaphoreType.DMA],
    )(*(pltpu.with_memory_space_constraint(x, pltpu.VMEM) for x in (grad, total)))
    return grad, up, inner, outer.T, out


def solution(mesh):
    return jax.shard_map(
        functools.partial(local, mesh.shape["dp"], mesh.shape["tm"]),
        mesh=mesh,
        in_specs=(P("dp", None, "tm"), P("dp", "tm"), P(), P(), P(), P()),
        out_specs=(P("dp", None, "tm"), P(), P(), P(), P()),
        check_vma=False,
    )
```

```python
import functools

import jax
import jax.numpy as jnp
import ml_dtypes
import numpy as np
from jax import lax
from jax.experimental import pallas as pl
from jax.experimental.pallas import tpu as pltpu
from jax.sharding import PartitionSpec as P

F32 = jnp.float32
BF16 = jnp.bfloat16
MESH = pl.DeviceIdType.MESH
MELS = 64
COEFFS = (0.25, 0.5, 0.5)
PARAMS = 10464
Y_HI = 2
TILES = 11


def mel_bank(window):
    half = window // 2
    top = 2595.0 * np.log10(1.0 + 12000.0 / 700.0)
    points = (np.arange(MELS + 1) + 1.0) / (MELS + 2.0) * top
    centers = 700.0 * (np.power(10.0, points / 2595.0) - 1.0) / 12000.0 * half
    spacing = np.maximum(centers[1:] - centers[:-1], 1.0)
    places = np.arange(half)[:, None]
    return np.maximum(0.0, 1.0 - np.abs(places - centers[None, :MELS]) / spacing[None, :])


def halves(x):
    high = x.astype(ml_dtypes.bfloat16)
    low = (x - high.astype(np.float64)).astype(ml_dtypes.bfloat16)
    return high, low


@functools.cache
def tables():
    lane = np.arange(256)
    place = np.where(lane < 128, 2 * lane, 2 * (lane - 128) + 1)

    def waves(bins, window):
        angle = 2.0 * np.pi * ((place[:, None] * bins[None, :]) % window) / window
        return np.cos(angle), np.sin(angle)

    p = np.arange(128)
    cos0, sin0 = waves(4 * p, 1024)
    cos2, sin2 = waves(4 * p + 2, 1024)
    cos1, sin1 = waves(4 * p + 1, 1024)
    cos3, sin3 = waves(4 * p + 3, 1024)
    t0 = np.concatenate([cos0, -sin0], axis=1)
    t2 = np.concatenate([cos2, -sin2], axis=1)
    real = np.concatenate(
        [np.concatenate([cos1, cos3], axis=1), np.concatenate([-sin1, sin3], axis=1)], axis=0
    )
    imag = np.concatenate(
        [np.concatenate([-sin1, -sin3], axis=1), np.concatenate([-cos1, cos3], axis=1)], axis=0
    )
    cosf, sinf = waves(p, 256)
    fine = np.concatenate([cosf, -sinf], axis=1)
    high, low = halves(np.concatenate([t0, t2, real, imag], axis=0))
    fine_high, fine_low = halves(fine)
    move = np.zeros((256, 256))
    move[place, lane] = 1.0
    dft = np.concatenate(
        [high, low, fine_high, fine_low, move.astype(ml_dtypes.bfloat16)], axis=0
    )
    order = np.concatenate([4 * p, 4 * p + 2, 4 * p + 1, 4 * p + 3])
    mels = np.concatenate([mel_bank(1024)[order], mel_bank(256)], axis=0)
    mels = np.concatenate(halves(mels), axis=1)
    taper = 0.5 - 0.5 * np.cos(2.0 * np.pi * (np.arange(4)[:, None] * 256 + place) / 1024)
    taper_fine = 0.5 - 0.5 * np.cos(2.0 * np.pi * place[None, :] / 256)
    tapers = np.concatenate([taper, taper_fine, np.zeros((3, 256))], axis=0).astype(np.float32)
    return dft, mels, tapers


HIGH, LOW, FINE_HIGH, FINE_LOW, MOVE, ROWS = 0, 1536, 3072, 3328, 3584, 3840


def split(x):
    high = x.astype(BF16)
    return high, (x - high.astype(F32)).astype(BF16)


def dot(a, b):
    return lax.dot_general(a, b, (((1,), (0,)), ((), ())), preferred_element_type=F32)


def dot_nt(a, b):
    return lax.dot_general(a, b, (((1,), (1,)), ((), ())), preferred_element_type=F32)


def weight_dot(w, x):
    high, low = w
    m = high.shape[0]
    xh, xl = split(x)
    both = dot(jnp.concatenate([high, low], axis=0), xh)
    return both[:m] + both[m:] + dot(high, xl)


def rows_dot(x, high, low, product=dot):
    m = x.shape[0]
    xh, xl = split(x)
    both = product(jnp.concatenate([xh, xl], axis=0), high)
    return both[:m] + both[m:] + product(xh, low)


def gram(a, b):
    m = a.shape[0]
    ah, al = split(a)
    bh, bl = split(b)
    both = dot_nt(jnp.concatenate([ah, al], axis=0), bh)
    return both[:m] + both[m:] + dot_nt(ah, bl)


def elu_and_slope(x):
    slope = jnp.exp(jnp.minimum(x, 0.0))
    return jnp.maximum(x, 0.0) + (slope - 1.0), slope


def roll(x, by, axis=1):
    return pltpu.roll(x, by % x.shape[axis], axis)


def coarse_spectrum(blocks, tapers, table):
    x = [blocks[b : b + 16, :] * tapers[b : b + 1, :] for b in range(4)]
    even, odd = x[0] + x[2], x[1] + x[3]
    cross = jnp.concatenate([x[0] - x[2], x[1] - x[3]], axis=1)
    return (
        rows_dot(even + odd, table[HIGH : HIGH + 256, :], table[LOW : LOW + 256, :]),
        rows_dot(even - odd, table[HIGH + 256 : HIGH + 512, :], table[LOW + 256 : LOW + 512, :]),
        rows_dot(cross, table[HIGH + 512 : HIGH + 1024, :], table[LOW + 512 : LOW + 1024, :]),
        rows_dot(cross, table[HIGH + 1024 : HIGH + 1536, :], table[LOW + 1024 : LOW + 1536, :]),
    )


def coarse_energy(parts):
    s0, s2, re, im = (part * part for part in parts)
    return jnp.concatenate(
        [s0[:, :128] + s0[:, 128:], s2[:, :128] + s2[:, 128:], re + im], axis=1
    )


def fine_frames(blocks, tapers):
    now, later = blocks[3:11, :], blocks[4:12, :]
    lane = lax.broadcasted_iota(jnp.int32, (8, 128), 1)
    frames = [now]
    for d in range(1, 4):
        keep = lane < 128 - 32 * d
        frames.append(
            jnp.concatenate(
                [
                    jnp.where(
                        keep,
                        roll(now[:, s : s + 128], -32 * d),
                        roll(later[:, s : s + 128], -32 * d),
                    )
                    for s in (0, 128)
                ],
                axis=1,
            )
        )
    return jnp.concatenate(frames, axis=0) * tapers[4:5, :]


def fine_spectrum(blocks, tapers, table):
    return rows_dot(
        fine_frames(blocks, tapers),
        table[FINE_HIGH : FINE_HIGH + 256, :],
        table[FINE_LOW : FINE_LOW + 256, :],
    )


def level_of(energy, bank):
    m = energy.shape[0]
    eh, el = split(energy)
    both = dot(jnp.concatenate([eh, el], axis=0), bank)
    both = both[:m] + both[m:]
    return jnp.sqrt(both + roll(both, MELS) + 1.0)


def energy_slope(level, target_level, valid, bank):
    m = level.shape[0]
    slope = jnp.where(valid, 1.0 - target_level / level, 0.0)
    sh, sl = split(slope)
    both = dot_nt(jnp.concatenate([sh, sl], axis=0), bank)
    return 2.0 * (both[:m] + both[m:])


def kernel(
    n_dp,
    n_tm,
    latent_hbm,
    target_hbm,
    up_hbm,
    inner_hbm,
    outer_hbm,
    out_hbm,
    dft_hbm,
    mels_hbm,
    tapers_hbm,
    grad_out,
    total,
    latent,
    halo,
    target_rows,
    up_k,
    inner_k,
    outer_k,
    out_k,
    table,
    mels,
    tapers,
    natural,
    target_blocks,
    wave_tiles,
    wave_blocks,
    frame_grads,
    grad_blocks,
    squares,
    window,
    packed_rows,
    grad_rows,
    halves_own,
    plane_halves,
    plane_rows,
    ring_rows,
    load_sem,
    near_send,
    near_recv,
    far_send,
    far_recv,
):
    dp = lax.axis_index("dp")
    tm = lax.axis_index("tm")
    n_z = n_tm // Y_HI
    n_plane = n_dp * Y_HI
    y_hi = tm // n_z
    z = lax.rem(tm, n_z)
    plane = y_hi * n_dp + dp
    right = lax.rem(tm + 1, n_tm)
    left = lax.rem(tm + n_tm - 1, n_tm)
    other = lax.rem(y_hi + 1, Y_HI) * n_z + z
    first = tm == 0
    last = tm == n_tm - 1

    loads = [
        pltpu.make_async_copy(source, place, load_sem.at[i])
        for i, (source, place) in enumerate(
            [
                (latent_hbm.at[0], latent),
                (target_hbm, target_rows.at[1]),
                (up_hbm, up_k),
                (inner_hbm, inner_k),
                (outer_hbm, outer_k),
                (out_hbm, out_k),
                (dft_hbm, table),
                (mels_hbm, mels),
                (tapers_hbm, tapers),
            ]
        )
    ]
    for load in loads:
        load.start()
    frames = latent.shape[1]
    wide = frames + 128

    barrier = pltpu.get_barrier_semaphore()

    def owner_of(index):
        return (index * n_plane) // TILES

    def tile_of(member):
        return (member * TILES + n_plane - 1) // n_plane

    def is_owner(member):
        index = tile_of(member)
        return (index < TILES) & (owner_of(index) == member)

    def along_z(i):
        half = (i + 1) // 2
        return lax.rem(z + n_z // 2 + half - 2 * half * lax.rem(i, 2) + n_z, n_z)

    def in_plane(visit):
        core, x, y_lo = lax.rem(dp, 2), lax.rem(dp // 2, 4), dp // 8
        for dx in (2, 1, 3, 0):

            @pl.loop(0, 8 if dx else 7)
            def _(i):
                bits = 7 - i
                y = lax.rem(y_hi + bits // 4, 2)
                y_in = lax.rem(y_lo + lax.rem(bits // 2, 2), 2)
                side = lax.rem(core + lax.rem(bits, 2), 2)
                visit(y * n_dp + y_in * 8 + lax.rem(x + dx, 4) * 2 + side)

    def member_id(member):
        return (lax.rem(member, n_dp), (member // n_dp) * n_z + z)

    owns = is_owner(plane)
    partner = lax.rem(y_hi + 1, Y_HI) * n_dp + dp

    def greet(device):
        pl.semaphore_signal(barrier, inc=1, device_id=device, device_id_type=MESH)

    reach = n_z // 4

    def beside(i):
        step = reach - i // 2
        ahead = z + n_z + step - 2 * step * lax.rem(i, 2)
        return (dp, y_hi * n_z + lax.rem(ahead, n_z))

    @pl.loop(0, 2 * reach)
    def _(i):
        greet(beside(i))

    greet((dp, other))

    @pl.when(z == n_z - 1)
    def _():
        greet((dp, right))

    @pl.when(z == 0)
    def _():
        greet((dp, left))

    for i in range(TILES):
        owner = owner_of(i)

        @pl.when((plane != owner) & (partner != owner))
        def _():
            greet(member_id(owner))

    @pl.when(owns)
    def _():
        def greet_member(member):
            @pl.when(jnp.logical_not(is_owner(member)) & (member != partner))
            def _():
                greet(member_id(member))

        in_plane(greet_member)

    greeted = 2 * reach + 1 + jnp.where((z == 0) | (z == n_z - 1), 1, 0)
    greeted += jnp.where(owns, n_plane - 2, TILES - jnp.where(is_owner(partner), 1, 0))

    loads[0].wait()
    lane_8 = lax.broadcasted_iota(jnp.int32, (8, 128), 1)
    lent = jnp.zeros((8, 128), F32)
    for g in range(8):
        start = latent[8 * g : 8 * g + 8, 0:128]
        end = latent[8 * g : 8 * g + 8, frames - 128 : frames]
        lent = jnp.where(lane_8 // 4 == g, roll(start, 4 * g), lent)
        lent = jnp.where(lane_8 // 4 == 16 + g, roll(end, 4 * g - 60), lent)
    halo[1] = lent

    pl.semaphore_wait(barrier, greeted)

    def send(source, place, slot, device):
        copy = pltpu.make_async_remote_copy(
            src_ref=source,
            dst_ref=place,
            send_sem=near_send.at[slot],
            recv_sem=near_recv.at[slot],
            device_id=device,
            device_id_type=MESH,
        )
        copy.start()
        return copy

    near = [
        send(halo.at[1], halo.at[0], 0, (dp, right)),
        send(halo.at[1], halo.at[2], 1, (dp, left)),
        send(target_hbm, target_rows.at[0], 2, (dp, right)),
        send(target_hbm, target_rows.at[2], 3, (dp, left)),
    ]

    loads[2].wait()
    loads[3].wait()
    loads[4].wait()
    loads[5].wait()
    up_rows = up_k[...]
    up_all = jnp.concatenate([up_rows[r] for r in range(4)], axis=0)
    up_w = jnp.concatenate(
        [
            jnp.concatenate([up_rows[0], up_rows[2]], axis=1),
            jnp.concatenate([up_rows[1], up_rows[3]], axis=1),
        ],
        axis=0,
    )
    up_fwd = split(up_w)
    up_bwd = split(up_all.T)
    taps = jnp.concatenate(
        [inner_k[0], inner_k[1], inner_k[2], jnp.zeros((16, 32), F32)], axis=1
    )
    inner_w = jnp.concatenate([taps, roll(taps, 32)], axis=0)
    inner_fwd = split(inner_w)
    zero = jnp.zeros((16, 32), F32)
    k0, k1, k2 = inner_k[0], inner_k[1], inner_k[2]
    inner_t = jnp.concatenate(
        [
            jnp.concatenate([k1, k2], axis=1),
            jnp.concatenate([k0, k1], axis=1),
            jnp.concatenate([k2, zero], axis=1),
            jnp.concatenate([zero, k0], axis=1),
        ],
        axis=0,
    )
    inner_bwd = split(inner_t.T)
    outer_t = outer_k[...]
    outer_w = jnp.concatenate(
        [jnp.concatenate([outer_t, zero], axis=1), jnp.concatenate([zero, outer_t], axis=1)],
        axis=0,
    )
    outer_bwd = split(outer_w)
    outer_fwd = split(outer_w.T)
    pad = jnp.zeros((1, 32), F32)
    taps_out = out_k[...]
    out_w = jnp.concatenate(
        [
            jnp.concatenate([pad, taps_out], axis=0),
            jnp.concatenate([taps_out, pad], axis=0),
        ],
        axis=1,
    )
    out_w16 = jnp.concatenate([out_w, jnp.zeros((8, 64), F32)], axis=0)
    out_fwd = split(out_w16)
    out_bwd = split(out_w16.T)

    lane = lax.broadcasted_iota(jnp.int32, (1, wide), 1)
    inside = (
        (lane < frames)
        | ((lane < frames + 4) & jnp.logical_not(last))
        | ((lane >= wide - 4) & jnp.logical_not(first))
    )

    near[0].wait_recv()
    near[1].wait_recv()
    before, behind = halo[0], halo[2]
    rim = []
    for g in range(8):
        tile = jnp.where((lane_8 < 4) & jnp.logical_not(last), roll(behind, -4 * g), 0.0)
        rim.append(
            jnp.where((lane_8 >= 124) & jnp.logical_not(first), roll(before, 60 - 4 * g), tile)
        )
    rim = jnp.concatenate(rim, axis=0)
    activated, slope_in = elu_and_slope(jnp.concatenate([latent[...], rim], axis=1))
    stacked = jnp.concatenate([activated, roll(activated, 1)], axis=0)
    upper = jnp.where(inside, weight_dot(up_fwd, stacked), 0.0)
    lifted, slope_upper = elu_and_slope(upper)
    even, odd = lifted[:32], lifted[32:]
    tapped = jnp.concatenate([roll(odd, 1), even, odd, roll(even, -1)], axis=0)
    hidden, slope_inner = elu_and_slope(weight_dot(inner_fwd, tapped))
    mixed = jnp.where(inside, upper + weight_dot(outer_fwd, hidden), 0.0)
    final, slope_mixed = elu_and_slope(mixed)
    taps_8 = weight_dot(out_fwd, final)[:8]
    row = lax.broadcasted_iota(jnp.int32, (8, wide), 0)
    moves = ((2, 0, 0), (1, 1, 2), (-1, 5, 6), (-2, 7, 7))
    aligned = taps_8
    for by, low, high in moves:
        aligned = jnp.where((row >= low) & (row <= high), roll(taps_8, by), aligned)
    aligned = aligned[:, :frames]
    aligned = aligned + roll(aligned, 4, 0)
    aligned = aligned + roll(aligned, 2, 0)
    is_even = lax.rem(row[:, :frames], 2) == 0
    swapped = roll(aligned, 1, 0)
    wave_even = jnp.where(is_even, aligned, swapped)
    wave_odd = jnp.where(is_even, swapped, aligned)
    tile = jnp.zeros((8, 128), F32)
    row_8 = row[:, :128]
    for b in range(4):
        tile = jnp.where(row_8 == b, wave_even[:, 128 * b : 128 * b + 128], tile)
        tile = jnp.where(row_8 == 4 + b, wave_odd[:, 128 * b : 128 * b + 128], tile)
    wave_tiles[1] = tile
    near += [
        send(wave_tiles.at[1], wave_tiles.at[0], 4, (dp, right)),
        send(wave_tiles.at[1], wave_tiles.at[2], 5, (dp, left)),
    ]

    for load in (loads[1], loads[6], loads[7], loads[8]):
        load.wait()
    near[2].wait_recv()
    near[3].wait_recv()
    natural[...] = jnp.zeros(natural.shape, F32)
    for s in range(3):
        for b in range(4):
            line = target_rows[s, :, 256 * b : 256 * b + 256]
            if s == 0:
                line = jnp.where(first, 0.0, line)
            if s == 2:
                line = jnp.where(last, 0.0, line)
            natural[4 * s + b : 4 * s + b + 1, :] = line
    nh, nl = split(natural[...])
    moved = dot(jnp.concatenate([nh, nl], axis=0), table[MOVE : MOVE + 256, :])
    target_blocks[...] = jnp.zeros(target_blocks.shape, F32)
    target_blocks[0:16, :] = moved[:16] + moved[16:]
    bank, bank_fine = mels[0:512, :], mels[512:640, :]
    target_coarse = level_of(coarse_energy(coarse_spectrum(target_blocks, tapers, table)), bank)
    s = fine_spectrum(target_blocks, tapers, table)
    s = s * s
    target_fine = level_of(s[:, :128] + s[:, 128:], bank_fine)

    wave_blocks[...] = jnp.zeros(wave_blocks.shape, F32)
    near[4].wait_recv()
    near[5].wait_recv()
    for s in range(3):
        for half in range(2):
            lines = wave_tiles[s, 4 * half : 4 * half + 4, :]
            if s == 0:
                lines = jnp.where(first, 0.0, lines)
            if s == 2:
                lines = jnp.where(last, 0.0, lines)
            wave_blocks[4 * s : 4 * s + 4, 128 * half : 128 * half + 128] = lines
    parts = coarse_spectrum(wave_blocks, tapers, table)
    level = level_of(coarse_energy(parts), bank)
    frame = lax.broadcasted_iota(jnp.int32, (16, 128), 0)
    index = 4 * tm + frame - 4
    valid = (frame < 9) & (index >= 0) & (index < 4 * n_tm)
    slope = energy_slope(level, target_coarse, valid, bank)
    s0, s2, re, im = parts
    twice = functools.partial(jnp.concatenate, axis=1)
    d0 = s0 * twice([slope[:, 0:128]] * 2)
    d2 = s2 * twice([slope[:, 128:256]] * 2)
    d_even = rows_dot(d0, table[HIGH : HIGH + 256, :], table[LOW : LOW + 256, :], dot_nt)
    d_odd = rows_dot(
        d2, table[HIGH + 256 : HIGH + 512, :], table[LOW + 256 : LOW + 512, :], dot_nt
    )
    d_cross = rows_dot(
        re * slope[:, 256:512],
        table[HIGH + 512 : HIGH + 1024, :],
        table[LOW + 512 : LOW + 1024, :],
        dot_nt,
    ) + rows_dot(
        im * slope[:, 256:512],
        table[HIGH + 1024 : HIGH + 1536, :],
        table[LOW + 1024 : LOW + 1536, :],
        dot_nt,
    )
    d_first, d_second = d_cross[:, :256], d_cross[:, 256:]
    both, apart = d_even + d_odd, d_even - d_odd
    for b, d in enumerate((both + d_first, apart + d_second, both - d_first, apart - d_second)):
        frame_grads[b] = d * tapers[b : b + 1, :]
    coarse = frame_grads[0, 3:11, :]
    for b in range(1, 4):
        coarse = coarse + frame_grads[b, 3 - b : 11 - b, :]

    spectrum = fine_spectrum(wave_blocks, tapers, table)
    s = spectrum * spectrum
    level = level_of(s[:, :128] + s[:, 128:], bank_fine)
    frame = lax.broadcasted_iota(jnp.int32, (32, 128), 0)
    index = 16 * tm + 4 * (lax.rem(frame, 8) - 1) + frame // 8
    valid = (index >= 0) & (index < 16 * n_tm)
    slope = energy_slope(level, target_fine, valid, bank_fine)
    d = rows_dot(
        spectrum * twice([slope] * 2),
        table[FINE_HIGH : FINE_HIGH + 256, :],
        table[FINE_LOW : FINE_LOW + 256, :],
        dot_nt,
    )
    d = d * tapers[4:5, :]
    fine = []
    for start in (0, 128):
        here = d[0:8, start : start + 128]
        after = jnp.zeros((8, 128), F32)
        for k in range(1, 4):
            moved = roll(d[8 * k : 8 * k + 8, start : start + 128], 32 * k)
            here = here + jnp.where(lane_8 >= 32 * k, moved, 0.0)
            after = after + jnp.where(lane_8 < 32 * k, moved, 0.0)
        fine.append(here + roll(after, 1, 0))
    fine = twice(fine)
    timed = 2.0 * (wave_blocks[3:11, :] - target_blocks[3:11, :])

    row_256 = lax.broadcasted_iota(jnp.int32, (8, 256), 0)
    own = (row_256 >= 1) & (row_256 <= 4)
    lane_1 = lax.broadcasted_iota(jnp.int32, (1, 128), 1)
    line = jnp.zeros((1, 128), F32)
    for i, member in enumerate((timed, coarse, fine)):
        kept = jnp.where(own, member * member, 0.0)
        line = jnp.where(lane_1 == i, jnp.sum(kept, keepdims=True), line)
    squares[z] = line

    def far(source, place, slot, device):
        return pltpu.make_async_remote_copy(
            src_ref=source,
            dst_ref=place,
            send_sem=far_send.at[slot],
            recv_sem=far_recv.at[slot],
            device_id=device,
            device_id_type=MESH,
        )

    def arrived(ref, slot):
        pltpu.make_async_copy(ref, ref, far_recv.at[slot]).wait()

    def sent(ref, slot):
        pltpu.make_async_copy(ref, ref, far_send.at[slot]).wait()

    @pl.loop(0, 2 * reach)
    def _(i):
        far(squares.at[z], squares.at[z], 0, beside(i)).start()

    grad_blocks[0] = timed
    grad_blocks[1] = coarse
    grad_blocks[2] = fine
    even_8 = lax.rem(row_8, 2) == 0

    def shifted(x):
        result = x
        for by, low, high in moves:
            result = jnp.where((row >= low) & (row <= high), roll(x, -by), result)
        return jnp.concatenate([result, jnp.zeros_like(result)], axis=0)

    for i in range(3):
        spread = []
        for b in range(5):
            r = b + 1
            even = jnp.broadcast_to(grad_blocks[i, r : r + 1, 0:128], (8, 128))
            odd = jnp.broadcast_to(grad_blocks[i, r : r + 1, 128:256], (8, 128))
            lines = jnp.where(even_8, even, odd)
            if b == 4:
                even = jnp.broadcast_to(grad_blocks[i, 0:1, 0:128], (8, 128))
                odd = jnp.broadcast_to(grad_blocks[i, 0:1, 128:256], (8, 128))
                lines = jnp.where(lane_8 < 64, lines, jnp.where(even_8, even, odd))
            spread.append(lines)
        wide_grad = jnp.where(inside, jnp.concatenate(spread, axis=1), 0.0)
        grad_final = weight_dot(out_bwd, shifted(wide_grad))
        owned = jnp.where(lane < frames, wide_grad, 0.0)
        out_rows = gram(shifted(owned), final)[:8]
        grad_mixed = jnp.where(inside, grad_final * slope_mixed, 0.0)
        outer_rows = gram(hidden[:, :frames], grad_mixed[:, :frames])
        grad_inner = weight_dot(outer_bwd, grad_mixed) * slope_inner
        inner_rows = gram(grad_inner[:, :frames], tapped[:, :frames])
        even, odd = grad_inner[:16], grad_inner[16:]
        around = jnp.concatenate([even, odd, roll(odd, 1), roll(even, -1)], axis=0)
        grad_lifted = weight_dot(inner_bwd, around)
        grad_upper = jnp.where(inside, grad_mixed + grad_lifted * slope_upper, 0.0)
        packed_rows[i, 0:64, :] = gram(grad_upper[:, :frames], stacked[:, :frames])
        taps = inner_rows[:16] + roll(inner_rows[16:], -32)
        pair = outer_rows[:16, :32] + outer_rows[16:, 32:]
        packed_rows[i, 64:80, :] = jnp.concatenate([taps[:, :96], pair], axis=1)
        taps_7 = out_rows[0:7, 32:64] + out_rows[1:8, 0:32]
        packed_rows[i, 80:88, :] = jnp.zeros((8, 128), F32)
        packed_rows[i, 80:87, 0:32] = taps_7
        after = jnp.concatenate([grad_upper, roll(grad_upper, -1)], axis=0)
        grad_rows[i] = weight_dot(up_bwd, after[:, :frames]) * slope_in[:, :frames]

    for i in range(TILES):
        owner = owner_of(i)
        chunk = packed_rows.at[:, pl.ds(8 * i, 8)]
        mine = plane == owner

        @pl.when(mine)
        def _():
            plane_rows[plane] = chunk[...]

        @pl.when(jnp.logical_not(mine))
        def _():
            far(chunk, plane_rows.at[plane], 1, member_id(owner)).start()

    arrived(squares.at[pl.ds(0, 2 * reach)], 0)

    def added(first, count):
        row = squares[lax.rem(z + n_z + first, n_z)]
        for k in range(1, count):
            row = row + squares[lax.rem(z + n_z + first + k, n_z)]
        return row

    ahead, back = added(1, reach), added(1 - reach, reach - 1)
    window[0] = ahead
    window[1] = back
    below, above = (
        (dp, y_hi * n_z + lax.rem(z + n_z - reach, n_z)),
        (dp, y_hi * n_z + lax.rem(z + reach, n_z)),
    )
    far(window.at[0], window.at[2], 6, below).start()
    far(window.at[1], window.at[3], 7, above).start()
    sums = squares[z] + added(-reach, 1) + back + ahead
    arrived(window.at[2], 6)
    arrived(window.at[3], 7)
    sums = sums + window[2] + window[3]
    halves_own[0] = sums
    for i in range(TILES):
        owner = owner_of(i)
        mine = plane == owner

        @pl.when(mine)
        def _():
            plane_halves[plane] = sums

        @pl.when(jnp.logical_not(mine))
        def _():
            far(halves_own.at[0], plane_halves.at[plane], 4, member_id(owner)).start()

    far(halves_own.at[0], halves_own.at[1], 5, (dp, other)).start()

    def scales_of(sums):
        coeffs = jnp.where(lane_1 == 0, COEFFS[0], jnp.where(lane_1 == 1, COEFFS[1], COEFFS[2]))
        return coeffs * lax.rsqrt(sums / (n_tm * 2.0 * frames) + 1e-06)

    arrived(halves_own.at[1], 5)
    scales = scales_of(halves_own[0] + halves_own[1])
    grad_out[...] = (
        scales[:, 0:1] * grad_rows[0] + scales[:, 1:2] * grad_rows[1] + scales[:, 2:3] * grad_rows[2]
    )

    tile_index = tile_of(plane)
    tile_rows = pl.ds(pl.multiple_of(8 * tile_index, 8), 8)

    @pl.when(owns)
    def _():
        arrived(plane_rows.at[pl.ds(0, n_plane - 1)], 1)
        arrived(plane_halves.at[pl.ds(0, n_plane - 1)], 4)
        chunk = jnp.zeros((8, 128), F32)
        for c in range(n_dp):
            scales = scales_of(plane_halves[c] + plane_halves[n_dp + c])
            for i in range(3):
                both = plane_rows[c, i] + plane_rows[n_dp + c, i]
                chunk = chunk + scales[:, i : i + 1] * both
        ring_rows[z] = chunk

        @pl.loop(0, n_z - 1)
        def _(i):
            far(ring_rows.at[z], ring_rows.at[z], 2, (dp, y_hi * n_z + along_z(i))).start()

        arrived(ring_rows.at[pl.ds(0, n_z - 1)], 2)
        chunk = ring_rows[0]
        for i in range(1, n_z):
            chunk = chunk + ring_rows[i]
        total[tile_rows, :] = chunk

        def give(member):
            far(total.at[tile_rows], total.at[tile_rows], 3, member_id(member)).start()

        in_plane(give)
        arrived(total.at[pl.ds(0, 8 * (TILES - 1))], 3)

    @pl.when(jnp.logical_not(owns))
    def _():
        arrived(total.at[pl.ds(0, 8 * TILES)], 3)

    for copy in near:
        copy.wait_send()
    sent(squares.at[pl.ds(0, 2 * reach)], 0)
    sent(window.at[0], 6)
    sent(window.at[1], 7)
    sent(halves_own.at[0], 5)

    @pl.when(owns)
    def _():
        sent(plane_rows.at[pl.ds(0, TILES - 1)], 1)
        sent(plane_halves.at[pl.ds(0, TILES - 1)], 4)
        sent(ring_rows.at[pl.ds(0, n_z - 1)], 2)
        sent(plane_rows.at[pl.ds(0, n_plane - 1), 0], 3)

    @pl.when(jnp.logical_not(owns))
    def _():
        sent(plane_rows.at[pl.ds(0, TILES)], 1)
        sent(plane_halves.at[pl.ds(0, TILES)], 4)


def finish(grad_ref, total_ref, latent_ref, up_ref, inner_ref, outer_ref, out_ref, store_sem):
    store = pltpu.make_async_copy(grad_ref, latent_ref.at[0], store_sem)
    store.start()
    sums = total_ref[...]
    square = jnp.sum(sums * sums, keepdims=True)
    factor = jnp.minimum(1.0, lax.rsqrt(square / PARAMS + 1e-06))
    sums = sums * factor
    up_ref[0] = sums[0:32, 0:64]
    up_ref[1] = sums[32:64, 0:64]
    up_ref[2] = sums[0:32, 64:128]
    up_ref[3] = sums[32:64, 64:128]
    for j in range(3):
        inner_ref[j] = sums[64:80, 32 * j : 32 * j + 32]
    outer_ref[...] = sums[64:80, 96:128]
    out_ref[...] = sums[80:87, 0:32]
    store.wait()


def local(n_dp, n_tm, latent, target, up_kernel, inner_kernel, outer_kernel, out_kernel):
    dft, mels, tapers = tables()
    frames = latent.shape[2]
    n_z = n_tm // Y_HI
    n_plane = n_dp * Y_HI
    shape = jax.ShapeDtypeStruct
    hbm = pl.BlockSpec(memory_space=pltpu.HBM)
    vmem = pl.BlockSpec(memory_space=pltpu.VMEM)
    grad, total = pl.pallas_call(
        functools.partial(kernel, n_dp, n_tm),
        out_shape=(pltpu.VMEM((64, frames), F32), pltpu.VMEM((8 * TILES, 128), F32)),
        in_specs=[hbm] * 9,
        out_specs=(vmem, vmem),
        scratch_shapes=[
            pltpu.VMEM((64, frames), F32),
            pltpu.VMEM((3, 8, 128), F32),
            pltpu.VMEM((3, 1, 2 * frames), F32),
            pltpu.VMEM((4, 32, 64), F32),
            pltpu.VMEM((3, 16, 32), F32),
            pltpu.VMEM((16, 32), F32),
            pltpu.VMEM((7, 32), F32),
            pltpu.VMEM((ROWS, 256), BF16),
            pltpu.VMEM((640, 128), BF16),
            pltpu.VMEM((8, 256), F32),
            pltpu.VMEM((16, 256), F32),
            pltpu.VMEM((24, 256), F32),
            pltpu.VMEM((3, 8, 128), F32),
            pltpu.VMEM((24, 256), F32),
            pltpu.VMEM((4, 16, 256), F32),
            pltpu.VMEM((3, 8, 256), F32),
            pltpu.VMEM((n_z, 1, 128), F32),
            pltpu.VMEM((4, 1, 128), F32),
            pltpu.VMEM((3, 8 * TILES, 128), F32),
            pltpu.VMEM((3, 64, frames), F32),
            pltpu.VMEM((2, 1, 128), F32),
            pltpu.VMEM((n_plane, 1, 128), F32),
            pltpu.VMEM((n_plane, 3, 8, 128), F32),
            pltpu.VMEM((n_z, 8, 128), F32),
            pltpu.SemaphoreType.DMA((9,)),
            pltpu.SemaphoreType.DMA((6,)),
            pltpu.SemaphoreType.DMA((6,)),
            pltpu.SemaphoreType.DMA((8,)),
            pltpu.SemaphoreType.DMA((8,)),
        ],
        compiler_params=pltpu.CompilerParams(
            collective_id=0, has_side_effects=True, vmem_limit_bytes=32 * 1024 * 1024
        ),
    )(
        *(
            pltpu.with_memory_space_constraint(x, pltpu.HBM)
            for x in (
                latent,
                target,
                up_kernel,
                inner_kernel,
                outer_kernel.T,
                out_kernel,
                jnp.asarray(dft),
                jnp.asarray(mels),
                jnp.asarray(tapers),
            )
        )
    )
    grad, up, inner, outer, out = pl.pallas_call(
        finish,
        out_shape=(
            shape(latent.shape, F32),
            shape((4, 32, 64), F32),
            shape((3, 16, 32), F32),
            shape((16, 32), F32),
            shape((7, 32), F32),
        ),
        in_specs=[vmem] * 2,
        out_specs=(hbm, vmem, vmem, vmem, vmem),
        scratch_shapes=[pltpu.SemaphoreType.DMA],
    )(*(pltpu.with_memory_space_constraint(x, pltpu.VMEM) for x in (grad, total)))
    return grad, up, inner, outer.T, out


def solution(mesh):
    return jax.shard_map(
        functools.partial(local, mesh.shape["dp"], mesh.shape["tm"]),
        mesh=mesh,
        in_specs=(P("dp", None, "tm"), P("dp", "tm"), P(), P(), P(), P()),
        out_specs=(P("dp", None, "tm"), P(), P(), P(), P()),
        check_vma=False,
    )
```

```python
import functools

import jax
import jax.numpy as jnp
import ml_dtypes
import numpy as np
from jax import lax
from jax.experimental import pallas as pl
from jax.experimental.pallas import tpu as pltpu
from jax.sharding import PartitionSpec as P

F32 = jnp.float32
BF16 = jnp.bfloat16
MESH = pl.DeviceIdType.MESH
MELS = 64
COEFFS = (0.25, 0.5, 0.5)
PARAMS = 10464
Y_HI = 2
TILES = 11


def mel_bank(window):
    half = window // 2
    top = 2595.0 * np.log10(1.0 + 12000.0 / 700.0)
    points = (np.arange(MELS + 1) + 1.0) / (MELS + 2.0) * top
    centers = 700.0 * (np.power(10.0, points / 2595.0) - 1.0) / 12000.0 * half
    spacing = np.maximum(centers[1:] - centers[:-1], 1.0)
    places = np.arange(half)[:, None]
    return np.maximum(0.0, 1.0 - np.abs(places - centers[None, :MELS]) / spacing[None, :])


def halves(x):
    high = x.astype(ml_dtypes.bfloat16)
    low = (x - high.astype(np.float64)).astype(ml_dtypes.bfloat16)
    return high, low


@functools.cache
def tables():
    lane = np.arange(256)
    place = np.where(lane < 128, 2 * lane, 2 * (lane - 128) + 1)

    def waves(bins, window):
        angle = 2.0 * np.pi * ((place[:, None] * bins[None, :]) % window) / window
        return np.cos(angle), np.sin(angle)

    p = np.arange(128)
    cos0, sin0 = waves(4 * p, 1024)
    cos2, sin2 = waves(4 * p + 2, 1024)
    cos1, sin1 = waves(4 * p + 1, 1024)
    cos3, sin3 = waves(4 * p + 3, 1024)
    t0 = np.concatenate([cos0, -sin0], axis=1)
    t2 = np.concatenate([cos2, -sin2], axis=1)
    real = np.concatenate(
        [np.concatenate([cos1, cos3], axis=1), np.concatenate([-sin1, sin3], axis=1)], axis=0
    )
    imag = np.concatenate(
        [np.concatenate([-sin1, -sin3], axis=1), np.concatenate([-cos1, cos3], axis=1)], axis=0
    )
    cosf, sinf = waves(p, 256)
    fine = np.concatenate([cosf, -sinf], axis=1)
    high, low = halves(np.concatenate([t0, t2, real, imag], axis=0))
    fine_high, fine_low = halves(fine)
    move = np.zeros((256, 256))
    move[place, lane] = 1.0
    dft = np.concatenate(
        [high, low, fine_high, fine_low, move.astype(ml_dtypes.bfloat16)], axis=0
    )
    order = np.concatenate([4 * p, 4 * p + 2, 4 * p + 1, 4 * p + 3])
    mels = np.concatenate([mel_bank(1024)[order], mel_bank(256)], axis=0)
    mels = np.concatenate(halves(mels), axis=1)
    taper = 0.5 - 0.5 * np.cos(2.0 * np.pi * (np.arange(4)[:, None] * 256 + place) / 1024)
    taper_fine = 0.5 - 0.5 * np.cos(2.0 * np.pi * place[None, :] / 256)
    tapers = np.concatenate([taper, taper_fine, np.zeros((3, 256))], axis=0).astype(np.float32)
    return dft, mels, tapers


HIGH, LOW, FINE_HIGH, FINE_LOW, MOVE, ROWS = 0, 1536, 3072, 3328, 3584, 3840


def split(x):
    high = x.astype(BF16)
    return high, (x - high.astype(F32)).astype(BF16)


def dot(a, b):
    return lax.dot_general(a, b, (((1,), (0,)), ((), ())), preferred_element_type=F32)


def dot_nt(a, b):
    return lax.dot_general(a, b, (((1,), (1,)), ((), ())), preferred_element_type=F32)


def weight_dot(w, x):
    high, low = w
    m = high.shape[0]
    xh, xl = split(x)
    both = dot(jnp.concatenate([high, low], axis=0), xh)
    return both[:m] + both[m:] + dot(high, xl)


def rows_dot(x, high, low, product=dot):
    m = x.shape[0]
    xh, xl = split(x)
    both = product(jnp.concatenate([xh, xl], axis=0), high)
    return both[:m] + both[m:] + product(xh, low)


def gram(a, b):
    m = a.shape[0]
    ah, al = split(a)
    bh, bl = split(b)
    both = dot_nt(jnp.concatenate([ah, al], axis=0), bh)
    return both[:m] + both[m:] + dot_nt(ah, bl)


def elu_and_slope(x):
    slope = jnp.exp(jnp.minimum(x, 0.0))
    return jnp.maximum(x, 0.0) + (slope - 1.0), slope


def roll(x, by, axis=1):
    return pltpu.roll(x, by % x.shape[axis], axis)


def coarse_spectrum(blocks, tapers, table):
    x = [blocks[b : b + 16, :] * tapers[b : b + 1, :] for b in range(4)]
    even, odd = x[0] + x[2], x[1] + x[3]
    cross = jnp.concatenate([x[0] - x[2], x[1] - x[3]], axis=1)
    return (
        rows_dot(even + odd, table[HIGH : HIGH + 256, :], table[LOW : LOW + 256, :]),
        rows_dot(even - odd, table[HIGH + 256 : HIGH + 512, :], table[LOW + 256 : LOW + 512, :]),
        rows_dot(cross, table[HIGH + 512 : HIGH + 1024, :], table[LOW + 512 : LOW + 1024, :]),
        rows_dot(cross, table[HIGH + 1024 : HIGH + 1536, :], table[LOW + 1024 : LOW + 1536, :]),
    )


def coarse_energy(parts):
    s0, s2, re, im = (part * part for part in parts)
    return jnp.concatenate(
        [s0[:, :128] + s0[:, 128:], s2[:, :128] + s2[:, 128:], re + im], axis=1
    )


def fine_frames(blocks, tapers):
    now, later = blocks[3:11, :], blocks[4:12, :]
    lane = lax.broadcasted_iota(jnp.int32, (8, 128), 1)
    frames = [now]
    for d in range(1, 4):
        keep = lane < 128 - 32 * d
        frames.append(
            jnp.concatenate(
                [
                    jnp.where(
                        keep,
                        roll(now[:, s : s + 128], -32 * d),
                        roll(later[:, s : s + 128], -32 * d),
                    )
                    for s in (0, 128)
                ],
                axis=1,
            )
        )
    return jnp.concatenate(frames, axis=0) * tapers[4:5, :]


def fine_spectrum(blocks, tapers, table):
    return rows_dot(
        fine_frames(blocks, tapers),
        table[FINE_HIGH : FINE_HIGH + 256, :],
        table[FINE_LOW : FINE_LOW + 256, :],
    )


def level_of(energy, bank):
    m = energy.shape[0]
    eh, el = split(energy)
    both = dot(jnp.concatenate([eh, el], axis=0), bank)
    both = both[:m] + both[m:]
    return jnp.sqrt(both + roll(both, MELS) + 1.0)


def energy_slope(level, target_level, valid, bank):
    m = level.shape[0]
    slope = jnp.where(valid, 1.0 - target_level / level, 0.0)
    sh, sl = split(slope)
    both = dot_nt(jnp.concatenate([sh, sl], axis=0), bank)
    return 2.0 * (both[:m] + both[m:])


def kernel(
    n_dp,
    n_tm,
    latent_hbm,
    target_hbm,
    up_hbm,
    inner_hbm,
    outer_hbm,
    out_hbm,
    dft_hbm,
    mels_hbm,
    tapers_hbm,
    grad_out,
    total,
    latent,
    halo,
    target_rows,
    up_k,
    inner_k,
    outer_k,
    out_k,
    table,
    mels,
    tapers,
    natural,
    target_blocks,
    wave_tiles,
    wave_blocks,
    frame_grads,
    grad_blocks,
    squares,
    packed_rows,
    grad_rows,
    halves_own,
    plane_halves,
    plane_rows,
    ring_rows,
    load_sem,
    near_send,
    near_recv,
    far_send,
    far_recv,
    known_sem,
    ready_sem,
):
    dp = lax.axis_index("dp")
    tm = lax.axis_index("tm")
    n_z = n_tm // Y_HI
    n_plane = n_dp * Y_HI
    y_hi = tm // n_z
    z = lax.rem(tm, n_z)
    plane = y_hi * n_dp + dp
    right = lax.rem(tm + 1, n_tm)
    left = lax.rem(tm + n_tm - 1, n_tm)
    other = lax.rem(y_hi + 1, Y_HI) * n_z + z
    first = tm == 0
    last = tm == n_tm - 1

    loads = [
        pltpu.make_async_copy(source, place, load_sem.at[i])
        for i, (source, place) in enumerate(
            [
                (latent_hbm.at[0], latent),
                (target_hbm, target_rows.at[1]),
                (up_hbm, up_k),
                (inner_hbm, inner_k),
                (outer_hbm, outer_k),
                (out_hbm, out_k),
                (dft_hbm, table),
                (mels_hbm, mels),
                (tapers_hbm, tapers),
            ]
        )
    ]
    for load in loads:
        load.start()
    frames = latent.shape[1]
    wide = frames + 128

    barrier = pltpu.get_barrier_semaphore()

    def owner_of(index):
        return (index * n_plane) // TILES

    def tile_of(member):
        return (member * TILES + n_plane - 1) // n_plane

    def is_owner(member):
        index = tile_of(member)
        return (index < TILES) & (owner_of(index) == member)

    def along_z(i):
        half = (i + 1) // 2
        return lax.rem(z + n_z // 2 + half - 2 * half * lax.rem(i, 2) + n_z, n_z)

    def in_plane(visit):
        core, x, y_lo = lax.rem(dp, 2), lax.rem(dp // 2, 4), dp // 8
        for dx in (2, 1, 3, 0):

            @pl.loop(0, 8 if dx else 7)
            def _(i):
                bits = 7 - i
                y = lax.rem(y_hi + bits // 4, 2)
                y_in = lax.rem(y_lo + lax.rem(bits // 2, 2), 2)
                side = lax.rem(core + lax.rem(bits, 2), 2)
                visit(y * n_dp + y_in * 8 + lax.rem(x + dx, 4) * 2 + side)

    def member_id(member):
        return (lax.rem(member, n_dp), (member // n_dp) * n_z + z)

    owns = is_owner(plane)
    partner = lax.rem(y_hi + 1, Y_HI) * n_dp + dp

    def greet(device):
        pl.semaphore_signal(barrier, inc=1, device_id=device, device_id_type=MESH)

    reach = n_z // 4

    def beside(i):
        step = reach - i // 2
        ahead = z + n_z + step - 2 * step * lax.rem(i, 2)
        return (dp, y_hi * n_z + lax.rem(ahead, n_z))

    @pl.loop(0, 2 * reach)
    def _(i):
        greet(beside(i))

    greet((dp, other))

    @pl.when(z == n_z - 1)
    def _():
        greet((dp, right))

    @pl.when(z == 0)
    def _():
        greet((dp, left))

    for i in range(TILES):
        owner = owner_of(i)

        @pl.when((plane != owner) & (partner != owner))
        def _():
            greet(member_id(owner))

    greeted = 2 * reach + 1 + jnp.where((z == 0) | (z == n_z - 1), 1, 0)
    greeted += jnp.where(owns, n_plane - 2, 0)

    loads[0].wait()
    lane_8 = lax.broadcasted_iota(jnp.int32, (8, 128), 1)
    lent = jnp.zeros((8, 128), F32)
    for g in range(8):
        start = latent[8 * g : 8 * g + 8, 0:128]
        end = latent[8 * g : 8 * g + 8, frames - 128 : frames]
        lent = jnp.where(lane_8 // 4 == g, roll(start, 4 * g), lent)
        lent = jnp.where(lane_8 // 4 == 16 + g, roll(end, 4 * g - 60), lent)
    halo[1] = lent

    pl.semaphore_wait(barrier, greeted)

    def send(source, place, slot, device):
        copy = pltpu.make_async_remote_copy(
            src_ref=source,
            dst_ref=place,
            send_sem=near_send.at[slot],
            recv_sem=near_recv.at[slot],
            device_id=device,
            device_id_type=MESH,
        )
        copy.start()
        return copy

    near = [
        send(halo.at[1], halo.at[0], 0, (dp, right)),
        send(halo.at[1], halo.at[2], 1, (dp, left)),
        send(target_hbm, target_rows.at[0], 2, (dp, right)),
        send(target_hbm, target_rows.at[2], 3, (dp, left)),
    ]

    def tell(semaphore, device):
        pl.semaphore_signal(semaphore, inc=1, device_id=device, device_id_type=MESH)

    below = (dp, y_hi * n_z + lax.rem(z + n_z - reach, n_z))
    above = (dp, y_hi * n_z + lax.rem(z + reach, n_z))
    tell(known_sem, below)
    tell(known_sem, above)

    @pl.when(owns)
    def _():
        in_plane(lambda member: tell(ready_sem, member_id(member)))

    loads[2].wait()
    loads[3].wait()
    loads[4].wait()
    loads[5].wait()
    up_rows = up_k[...]
    up_all = jnp.concatenate([up_rows[r] for r in range(4)], axis=0)
    up_w = jnp.concatenate(
        [
            jnp.concatenate([up_rows[0], up_rows[2]], axis=1),
            jnp.concatenate([up_rows[1], up_rows[3]], axis=1),
        ],
        axis=0,
    )
    up_fwd = split(up_w)
    up_bwd = split(up_all.T)
    taps = jnp.concatenate(
        [inner_k[0], inner_k[1], inner_k[2], jnp.zeros((16, 32), F32)], axis=1
    )
    inner_w = jnp.concatenate([taps, roll(taps, 32)], axis=0)
    inner_fwd = split(inner_w)
    zero = jnp.zeros((16, 32), F32)
    k0, k1, k2 = inner_k[0], inner_k[1], inner_k[2]
    inner_t = jnp.concatenate(
        [
            jnp.concatenate([k1, k2], axis=1),
            jnp.concatenate([k0, k1], axis=1),
            jnp.concatenate([k2, zero], axis=1),
            jnp.concatenate([zero, k0], axis=1),
        ],
        axis=0,
    )
    inner_bwd = split(inner_t.T)
    outer_t = outer_k[...]
    outer_w = jnp.concatenate(
        [jnp.concatenate([outer_t, zero], axis=1), jnp.concatenate([zero, outer_t], axis=1)],
        axis=0,
    )
    outer_bwd = split(outer_w)
    outer_fwd = split(outer_w.T)
    pad = jnp.zeros((1, 32), F32)
    taps_out = out_k[...]
    out_w = jnp.concatenate(
        [
            jnp.concatenate([pad, taps_out], axis=0),
            jnp.concatenate([taps_out, pad], axis=0),
        ],
        axis=1,
    )
    out_w16 = jnp.concatenate([out_w, jnp.zeros((8, 64), F32)], axis=0)
    out_fwd = split(out_w16)
    out_bwd = split(out_w16.T)

    lane = lax.broadcasted_iota(jnp.int32, (1, wide), 1)
    inside = (
        (lane < frames)
        | ((lane < frames + 4) & jnp.logical_not(last))
        | ((lane >= wide - 4) & jnp.logical_not(first))
    )

    near[0].wait_recv()
    near[1].wait_recv()
    before, behind = halo[0], halo[2]
    rim = []
    for g in range(8):
        tile = jnp.where((lane_8 < 4) & jnp.logical_not(last), roll(behind, -4 * g), 0.0)
        rim.append(
            jnp.where((lane_8 >= 124) & jnp.logical_not(first), roll(before, 60 - 4 * g), tile)
        )
    rim = jnp.concatenate(rim, axis=0)
    activated, slope_in = elu_and_slope(jnp.concatenate([latent[...], rim], axis=1))
    stacked = jnp.concatenate([activated, roll(activated, 1)], axis=0)
    upper = jnp.where(inside, weight_dot(up_fwd, stacked), 0.0)
    lifted, slope_upper = elu_and_slope(upper)
    even, odd = lifted[:32], lifted[32:]
    tapped = jnp.concatenate([roll(odd, 1), even, odd, roll(even, -1)], axis=0)
    hidden, slope_inner = elu_and_slope(weight_dot(inner_fwd, tapped))
    mixed = jnp.where(inside, upper + weight_dot(outer_fwd, hidden), 0.0)
    final, slope_mixed = elu_and_slope(mixed)
    taps_8 = weight_dot(out_fwd, final)[:8]
    row = lax.broadcasted_iota(jnp.int32, (8, wide), 0)
    moves = ((2, 0, 0), (1, 1, 2), (-1, 5, 6), (-2, 7, 7))
    aligned = taps_8
    for by, low, high in moves:
        aligned = jnp.where((row >= low) & (row <= high), roll(taps_8, by), aligned)
    aligned = aligned[:, :frames]
    aligned = aligned + roll(aligned, 4, 0)
    aligned = aligned + roll(aligned, 2, 0)
    is_even = lax.rem(row[:, :frames], 2) == 0
    swapped = roll(aligned, 1, 0)
    wave_even = jnp.where(is_even, aligned, swapped)
    wave_odd = jnp.where(is_even, swapped, aligned)
    tile = jnp.zeros((8, 128), F32)
    row_8 = row[:, :128]
    for b in range(4):
        tile = jnp.where(row_8 == b, wave_even[:, 128 * b : 128 * b + 128], tile)
        tile = jnp.where(row_8 == 4 + b, wave_odd[:, 128 * b : 128 * b + 128], tile)
    wave_tiles[1] = tile
    near += [
        send(wave_tiles.at[1], wave_tiles.at[0], 4, (dp, right)),
        send(wave_tiles.at[1], wave_tiles.at[2], 5, (dp, left)),
    ]

    for load in (loads[1], loads[6], loads[7], loads[8]):
        load.wait()
    near[2].wait_recv()
    near[3].wait_recv()
    natural[...] = jnp.zeros(natural.shape, F32)
    for s in range(3):
        for b in range(4):
            line = target_rows[s, :, 256 * b : 256 * b + 256]
            if s == 0:
                line = jnp.where(first, 0.0, line)
            if s == 2:
                line = jnp.where(last, 0.0, line)
            natural[4 * s + b : 4 * s + b + 1, :] = line
    nh, nl = split(natural[...])
    moved = dot(jnp.concatenate([nh, nl], axis=0), table[MOVE : MOVE + 256, :])
    target_blocks[...] = jnp.zeros(target_blocks.shape, F32)
    target_blocks[0:16, :] = moved[:16] + moved[16:]
    bank, bank_fine = mels[0:512, :], mels[512:640, :]
    target_coarse = level_of(coarse_energy(coarse_spectrum(target_blocks, tapers, table)), bank)
    s = fine_spectrum(target_blocks, tapers, table)
    s = s * s
    target_fine = level_of(s[:, :128] + s[:, 128:], bank_fine)

    wave_blocks[...] = jnp.zeros(wave_blocks.shape, F32)
    near[4].wait_recv()
    near[5].wait_recv()
    for s in range(3):
        for half in range(2):
            lines = wave_tiles[s, 4 * half : 4 * half + 4, :]
            if s == 0:
                lines = jnp.where(first, 0.0, lines)
            if s == 2:
                lines = jnp.where(last, 0.0, lines)
            wave_blocks[4 * s : 4 * s + 4, 128 * half : 128 * half + 128] = lines
    parts = coarse_spectrum(wave_blocks, tapers, table)
    level = level_of(coarse_energy(parts), bank)
    frame = lax.broadcasted_iota(jnp.int32, (16, 128), 0)
    index = 4 * tm + frame - 4
    valid = (frame < 9) & (index >= 0) & (index < 4 * n_tm)
    slope = energy_slope(level, target_coarse, valid, bank)
    s0, s2, re, im = parts
    twice = functools.partial(jnp.concatenate, axis=1)
    d0 = s0 * twice([slope[:, 0:128]] * 2)
    d2 = s2 * twice([slope[:, 128:256]] * 2)
    d_even = rows_dot(d0, table[HIGH : HIGH + 256, :], table[LOW : LOW + 256, :], dot_nt)
    d_odd = rows_dot(
        d2, table[HIGH + 256 : HIGH + 512, :], table[LOW + 256 : LOW + 512, :], dot_nt
    )
    d_cross = rows_dot(
        re * slope[:, 256:512],
        table[HIGH + 512 : HIGH + 1024, :],
        table[LOW + 512 : LOW + 1024, :],
        dot_nt,
    ) + rows_dot(
        im * slope[:, 256:512],
        table[HIGH + 1024 : HIGH + 1536, :],
        table[LOW + 1024 : LOW + 1536, :],
        dot_nt,
    )
    d_first, d_second = d_cross[:, :256], d_cross[:, 256:]
    both, apart = d_even + d_odd, d_even - d_odd
    for b, d in enumerate((both + d_first, apart + d_second, both - d_first, apart - d_second)):
        frame_grads[b] = d * tapers[b : b + 1, :]
    coarse = frame_grads[0, 3:11, :]
    for b in range(1, 4):
        coarse = coarse + frame_grads[b, 3 - b : 11 - b, :]

    spectrum = fine_spectrum(wave_blocks, tapers, table)
    s = spectrum * spectrum
    level = level_of(s[:, :128] + s[:, 128:], bank_fine)
    frame = lax.broadcasted_iota(jnp.int32, (32, 128), 0)
    index = 16 * tm + 4 * (lax.rem(frame, 8) - 1) + frame // 8
    valid = (index >= 0) & (index < 16 * n_tm)
    slope = energy_slope(level, target_fine, valid, bank_fine)
    d = rows_dot(
        spectrum * twice([slope] * 2),
        table[FINE_HIGH : FINE_HIGH + 256, :],
        table[FINE_LOW : FINE_LOW + 256, :],
        dot_nt,
    )
    d = d * tapers[4:5, :]
    fine = []
    for start in (0, 128):
        here = d[0:8, start : start + 128]
        after = jnp.zeros((8, 128), F32)
        for k in range(1, 4):
            moved = roll(d[8 * k : 8 * k + 8, start : start + 128], 32 * k)
            here = here + jnp.where(lane_8 >= 32 * k, moved, 0.0)
            after = after + jnp.where(lane_8 < 32 * k, moved, 0.0)
        fine.append(here + roll(after, 1, 0))
    fine = twice(fine)
    timed = 2.0 * (wave_blocks[3:11, :] - target_blocks[3:11, :])

    row_256 = lax.broadcasted_iota(jnp.int32, (8, 256), 0)
    own = (row_256 >= 1) & (row_256 <= 4)
    lane_1 = lax.broadcasted_iota(jnp.int32, (1, 128), 1)
    line = jnp.zeros((1, 128), F32)
    for i, member in enumerate((timed, coarse, fine)):
        kept = jnp.where(own, member * member, 0.0)
        line = jnp.where(lane_1 == i, jnp.sum(kept, keepdims=True), line)
    squares[z] = line

    def far(source, place, slot, device):
        return pltpu.make_async_remote_copy(
            src_ref=source,
            dst_ref=place,
            send_sem=far_send.at[slot],
            recv_sem=far_recv.at[slot],
            device_id=device,
            device_id_type=MESH,
        )

    def arrived(ref, slot):
        pltpu.make_async_copy(ref, ref, far_recv.at[slot]).wait()

    def sent(ref, slot):
        pltpu.make_async_copy(ref, ref, far_send.at[slot]).wait()

    pl.semaphore_wait(known_sem, 2)

    @pl.loop(0, n_z - 1)
    def _(i):
        far(squares.at[z], squares.at[z], 0, (dp, y_hi * n_z + along_z(i))).start()

    grad_blocks[0] = timed
    grad_blocks[1] = coarse
    grad_blocks[2] = fine
    even_8 = lax.rem(row_8, 2) == 0

    def shifted(x):
        result = x
        for by, low, high in moves:
            result = jnp.where((row >= low) & (row <= high), roll(x, -by), result)
        return jnp.concatenate([result, jnp.zeros_like(result)], axis=0)

    for i in range(3):
        spread = []
        for b in range(5):
            r = b + 1
            even = jnp.broadcast_to(grad_blocks[i, r : r + 1, 0:128], (8, 128))
            odd = jnp.broadcast_to(grad_blocks[i, r : r + 1, 128:256], (8, 128))
            lines = jnp.where(even_8, even, odd)
            if b == 4:
                even = jnp.broadcast_to(grad_blocks[i, 0:1, 0:128], (8, 128))
                odd = jnp.broadcast_to(grad_blocks[i, 0:1, 128:256], (8, 128))
                lines = jnp.where(lane_8 < 64, lines, jnp.where(even_8, even, odd))
            spread.append(lines)
        wide_grad = jnp.where(inside, jnp.concatenate(spread, axis=1), 0.0)
        grad_final = weight_dot(out_bwd, shifted(wide_grad))
        owned = jnp.where(lane < frames, wide_grad, 0.0)
        out_rows = gram(shifted(owned), final)[:8]
        grad_mixed = jnp.where(inside, grad_final * slope_mixed, 0.0)
        outer_rows = gram(hidden[:, :frames], grad_mixed[:, :frames])
        grad_inner = weight_dot(outer_bwd, grad_mixed) * slope_inner
        inner_rows = gram(grad_inner[:, :frames], tapped[:, :frames])
        even, odd = grad_inner[:16], grad_inner[16:]
        around = jnp.concatenate([even, odd, roll(odd, 1), roll(even, -1)], axis=0)
        grad_lifted = weight_dot(inner_bwd, around)
        grad_upper = jnp.where(inside, grad_mixed + grad_lifted * slope_upper, 0.0)
        packed_rows[i, 0:64, :] = gram(grad_upper[:, :frames], stacked[:, :frames])
        taps = inner_rows[:16] + roll(inner_rows[16:], -32)
        pair = outer_rows[:16, :32] + outer_rows[16:, 32:]
        packed_rows[i, 64:80, :] = jnp.concatenate([taps[:, :96], pair], axis=1)
        taps_7 = out_rows[0:7, 32:64] + out_rows[1:8, 0:32]
        packed_rows[i, 80:88, :] = jnp.zeros((8, 128), F32)
        packed_rows[i, 80:87, 0:32] = taps_7
        after = jnp.concatenate([grad_upper, roll(grad_upper, -1)], axis=0)
        grad_rows[i] = weight_dot(up_bwd, after[:, :frames]) * slope_in[:, :frames]

    pl.semaphore_wait(ready_sem, jnp.where(owns, TILES - 1, TILES))
    for i in range(TILES):
        owner = owner_of(i)
        chunk = packed_rows.at[:, pl.ds(8 * i, 8)]
        mine = plane == owner

        @pl.when(mine)
        def _():
            plane_rows[plane] = chunk[...]

        @pl.when(jnp.logical_not(mine))
        def _():
            far(chunk, plane_rows.at[plane], 1, member_id(owner)).start()

    arrived(squares.at[pl.ds(0, n_z - 1)], 0)
    sums = squares[0]
    for i in range(1, n_z):
        sums = sums + squares[i]
    halves_own[0] = sums
    for i in range(TILES):
        owner = owner_of(i)
        mine = plane == owner

        @pl.when(mine)
        def _():
            plane_halves[plane] = sums

        @pl.when(jnp.logical_not(mine))
        def _():
            far(halves_own.at[0], plane_halves.at[plane], 4, member_id(owner)).start()

    far(halves_own.at[0], halves_own.at[1], 5, (dp, other)).start()

    def scales_of(sums):
        coeffs = jnp.where(lane_1 == 0, COEFFS[0], jnp.where(lane_1 == 1, COEFFS[1], COEFFS[2]))
        return coeffs * lax.rsqrt(sums / (n_tm * 2.0 * frames) + 1e-06)

    arrived(halves_own.at[1], 5)
    scales = scales_of(halves_own[0] + halves_own[1])
    grad_out[...] = (
        scales[:, 0:1] * grad_rows[0] + scales[:, 1:2] * grad_rows[1] + scales[:, 2:3] * grad_rows[2]
    )

    tile_index = tile_of(plane)
    tile_rows = pl.ds(pl.multiple_of(8 * tile_index, 8), 8)

    @pl.when(owns)
    def _():
        arrived(plane_rows.at[pl.ds(0, n_plane - 1)], 1)
        arrived(plane_halves.at[pl.ds(0, n_plane - 1)], 4)
        chunk = jnp.zeros((8, 128), F32)
        for c in range(n_dp):
            scales = scales_of(plane_halves[c] + plane_halves[n_dp + c])
            for i in range(3):
                both = plane_rows[c, i] + plane_rows[n_dp + c, i]
                chunk = chunk + scales[:, i : i + 1] * both
        ring_rows[z] = chunk

        @pl.loop(0, n_z - 1)
        def _(i):
            far(ring_rows.at[z], ring_rows.at[z], 2, (dp, y_hi * n_z + along_z(i))).start()

        arrived(ring_rows.at[pl.ds(0, n_z - 1)], 2)
        chunk = ring_rows[0]
        for i in range(1, n_z):
            chunk = chunk + ring_rows[i]
        total[tile_rows, :] = chunk

        def give(member):
            far(total.at[tile_rows], total.at[tile_rows], 3, member_id(member)).start()

        in_plane(give)
        arrived(total.at[pl.ds(0, 8 * (TILES - 1))], 3)

    @pl.when(jnp.logical_not(owns))
    def _():
        arrived(total.at[pl.ds(0, 8 * TILES)], 3)

    for copy in near:
        copy.wait_send()
    sent(squares.at[pl.ds(0, n_z - 1)], 0)
    sent(halves_own.at[0], 5)

    @pl.when(owns)
    def _():
        sent(plane_rows.at[pl.ds(0, TILES - 1)], 1)
        sent(plane_halves.at[pl.ds(0, TILES - 1)], 4)
        sent(ring_rows.at[pl.ds(0, n_z - 1)], 2)
        sent(plane_rows.at[pl.ds(0, n_plane - 1), 0], 3)

    @pl.when(jnp.logical_not(owns))
    def _():
        sent(plane_rows.at[pl.ds(0, TILES)], 1)
        sent(plane_halves.at[pl.ds(0, TILES)], 4)


def finish(grad_ref, total_ref, latent_ref, up_ref, inner_ref, outer_ref, out_ref, store_sem):
    store = pltpu.make_async_copy(grad_ref, latent_ref.at[0], store_sem)
    store.start()
    sums = total_ref[...]
    square = jnp.sum(sums * sums, keepdims=True)
    factor = jnp.minimum(1.0, lax.rsqrt(square / PARAMS + 1e-06))
    sums = sums * factor
    up_ref[0] = sums[0:32, 0:64]
    up_ref[1] = sums[32:64, 0:64]
    up_ref[2] = sums[0:32, 64:128]
    up_ref[3] = sums[32:64, 64:128]
    for j in range(3):
        inner_ref[j] = sums[64:80, 32 * j : 32 * j + 32]
    outer_ref[...] = sums[64:80, 96:128]
    out_ref[...] = sums[80:87, 0:32]
    store.wait()


def local(n_dp, n_tm, latent, target, up_kernel, inner_kernel, outer_kernel, out_kernel):
    dft, mels, tapers = tables()
    frames = latent.shape[2]
    n_z = n_tm // Y_HI
    n_plane = n_dp * Y_HI
    shape = jax.ShapeDtypeStruct
    hbm = pl.BlockSpec(memory_space=pltpu.HBM)
    vmem = pl.BlockSpec(memory_space=pltpu.VMEM)
    grad, total = pl.pallas_call(
        functools.partial(kernel, n_dp, n_tm),
        out_shape=(pltpu.VMEM((64, frames), F32), pltpu.VMEM((8 * TILES, 128), F32)),
        in_specs=[hbm] * 9,
        out_specs=(vmem, vmem),
        scratch_shapes=[
            pltpu.VMEM((64, frames), F32),
            pltpu.VMEM((3, 8, 128), F32),
            pltpu.VMEM((3, 1, 2 * frames), F32),
            pltpu.VMEM((4, 32, 64), F32),
            pltpu.VMEM((3, 16, 32), F32),
            pltpu.VMEM((16, 32), F32),
            pltpu.VMEM((7, 32), F32),
            pltpu.VMEM((ROWS, 256), BF16),
            pltpu.VMEM((640, 128), BF16),
            pltpu.VMEM((8, 256), F32),
            pltpu.VMEM((16, 256), F32),
            pltpu.VMEM((24, 256), F32),
            pltpu.VMEM((3, 8, 128), F32),
            pltpu.VMEM((24, 256), F32),
            pltpu.VMEM((4, 16, 256), F32),
            pltpu.VMEM((3, 8, 256), F32),
            pltpu.VMEM((n_z, 1, 128), F32),
            pltpu.VMEM((3, 8 * TILES, 128), F32),
            pltpu.VMEM((3, 64, frames), F32),
            pltpu.VMEM((2, 1, 128), F32),
            pltpu.VMEM((n_plane, 1, 128), F32),
            pltpu.VMEM((n_plane, 3, 8, 128), F32),
            pltpu.VMEM((n_z, 8, 128), F32),
            pltpu.SemaphoreType.DMA((9,)),
            pltpu.SemaphoreType.DMA((6,)),
            pltpu.SemaphoreType.DMA((6,)),
            pltpu.SemaphoreType.DMA((6,)),
            pltpu.SemaphoreType.DMA((6,)),
            pltpu.SemaphoreType.REGULAR,
            pltpu.SemaphoreType.REGULAR,
        ],
        compiler_params=pltpu.CompilerParams(
            collective_id=0, has_side_effects=True, vmem_limit_bytes=32 * 1024 * 1024
        ),
    )(
        *(
            pltpu.with_memory_space_constraint(x, pltpu.HBM)
            for x in (
                latent,
                target,
                up_kernel,
                inner_kernel,
                outer_kernel.T,
                out_kernel,
                jnp.asarray(dft),
                jnp.asarray(mels),
                jnp.asarray(tapers),
            )
        )
    )
    grad, up, inner, outer, out = pl.pallas_call(
        finish,
        out_shape=(
            shape(latent.shape, F32),
            shape((4, 32, 64), F32),
            shape((3, 16, 32), F32),
            shape((16, 32), F32),
            shape((7, 32), F32),
        ),
        in_specs=[vmem] * 2,
        out_specs=(hbm, vmem, vmem, vmem, vmem),
        scratch_shapes=[pltpu.SemaphoreType.DMA],
    )(*(pltpu.with_memory_space_constraint(x, pltpu.VMEM) for x in (grad, total)))
    return grad, up, inner, outer.T, out


def solution(mesh):
    return jax.shard_map(
        functools.partial(local, mesh.shape["dp"], mesh.shape["tm"]),
        mesh=mesh,
        in_specs=(P("dp", None, "tm"), P("dp", "tm"), P(), P(), P(), P()),
        out_specs=(P("dp", None, "tm"), P(), P(), P(), P()),
        check_vma=False,
    )
```

```python
import functools

import jax
import jax.numpy as jnp
import ml_dtypes
import numpy as np
from jax import lax
from jax.experimental import pallas as pl
from jax.experimental.pallas import tpu as pltpu
from jax.sharding import PartitionSpec as P

F32 = jnp.float32
BF16 = jnp.bfloat16
MESH = pl.DeviceIdType.MESH
MELS = 64
COEFFS = (0.25, 0.5, 0.5)
PARAMS = 10464
Y_HI = 2
TILES = 11


def mel_bank(window):
    half = window // 2
    top = 2595.0 * np.log10(1.0 + 12000.0 / 700.0)
    points = (np.arange(MELS + 1) + 1.0) / (MELS + 2.0) * top
    centers = 700.0 * (np.power(10.0, points / 2595.0) - 1.0) / 12000.0 * half
    spacing = np.maximum(centers[1:] - centers[:-1], 1.0)
    places = np.arange(half)[:, None]
    return np.maximum(0.0, 1.0 - np.abs(places - centers[None, :MELS]) / spacing[None, :])


def halves(x):
    high = x.astype(ml_dtypes.bfloat16)
    low = (x - high.astype(np.float64)).astype(ml_dtypes.bfloat16)
    return high, low


@functools.cache
def tables():
    lane = np.arange(256)
    place = np.where(lane < 128, 2 * lane, 2 * (lane - 128) + 1)

    def waves(bins, window):
        angle = 2.0 * np.pi * ((place[:, None] * bins[None, :]) % window) / window
        return np.cos(angle), np.sin(angle)

    p = np.arange(128)
    cos0, sin0 = waves(4 * p, 1024)
    cos2, sin2 = waves(4 * p + 2, 1024)
    cos1, sin1 = waves(4 * p + 1, 1024)
    cos3, sin3 = waves(4 * p + 3, 1024)
    t0 = np.concatenate([cos0, -sin0], axis=1)
    t2 = np.concatenate([cos2, -sin2], axis=1)
    real = np.concatenate(
        [np.concatenate([cos1, cos3], axis=1), np.concatenate([-sin1, sin3], axis=1)], axis=0
    )
    imag = np.concatenate(
        [np.concatenate([-sin1, -sin3], axis=1), np.concatenate([-cos1, cos3], axis=1)], axis=0
    )
    cosf, sinf = waves(p, 256)
    fine = np.concatenate([cosf, -sinf], axis=1)
    high, low = halves(np.concatenate([t0, t2, real, imag], axis=0))
    fine_high, fine_low = halves(fine)
    move = np.zeros((256, 256))
    move[place, lane] = 1.0
    dft = np.concatenate(
        [high, low, fine_high, fine_low, move.astype(ml_dtypes.bfloat16)], axis=0
    )
    order = np.concatenate([4 * p, 4 * p + 2, 4 * p + 1, 4 * p + 3])
    mels = np.concatenate([mel_bank(1024)[order], mel_bank(256)], axis=0)
    mels = np.concatenate(halves(mels), axis=1)
    taper = 0.5 - 0.5 * np.cos(2.0 * np.pi * (np.arange(4)[:, None] * 256 + place) / 1024)
    taper_fine = 0.5 - 0.5 * np.cos(2.0 * np.pi * place[None, :] / 256)
    tapers = np.concatenate([taper, taper_fine, np.zeros((3, 256))], axis=0).astype(np.float32)
    return dft, mels, tapers


HIGH, LOW, FINE_HIGH, FINE_LOW, MOVE, ROWS = 0, 1536, 3072, 3328, 3584, 3840


def split(x):
    high = x.astype(BF16)
    return high, (x - high.astype(F32)).astype(BF16)


def dot(a, b):
    return lax.dot_general(a, b, (((1,), (0,)), ((), ())), preferred_element_type=F32)


def dot_nt(a, b):
    return lax.dot_general(a, b, (((1,), (1,)), ((), ())), preferred_element_type=F32)


def weight_dot(w, x):
    high, low = w
    m = high.shape[0]
    xh, xl = split(x)
    both = dot(jnp.concatenate([high, low], axis=0), xh)
    return both[:m] + both[m:] + dot(high, xl)


def rows_dot(x, high, low, product=dot):
    m = x.shape[0]
    xh, xl = split(x)
    both = product(jnp.concatenate([xh, xl], axis=0), high)
    return both[:m] + both[m:] + product(xh, low)


def gram(a, b):
    m = a.shape[0]
    ah, al = split(a)
    bh, bl = split(b)
    both = dot_nt(jnp.concatenate([ah, al], axis=0), bh)
    return both[:m] + both[m:] + dot_nt(ah, bl)


def elu_and_slope(x):
    slope = jnp.exp(jnp.minimum(x, 0.0))
    return jnp.maximum(x, 0.0) + (slope - 1.0), slope


def roll(x, by, axis=1):
    return pltpu.roll(x, by % x.shape[axis], axis)


def coarse_spectrum(blocks, tapers, table):
    x = [blocks[b : b + 16, :] * tapers[b : b + 1, :] for b in range(4)]
    even, odd = x[0] + x[2], x[1] + x[3]
    cross = jnp.concatenate([x[0] - x[2], x[1] - x[3]], axis=1)
    return (
        rows_dot(even + odd, table[HIGH : HIGH + 256, :], table[LOW : LOW + 256, :]),
        rows_dot(even - odd, table[HIGH + 256 : HIGH + 512, :], table[LOW + 256 : LOW + 512, :]),
        rows_dot(cross, table[HIGH + 512 : HIGH + 1024, :], table[LOW + 512 : LOW + 1024, :]),
        rows_dot(cross, table[HIGH + 1024 : HIGH + 1536, :], table[LOW + 1024 : LOW + 1536, :]),
    )


def coarse_energy(parts):
    s0, s2, re, im = (part * part for part in parts)
    return jnp.concatenate(
        [s0[:, :128] + s0[:, 128:], s2[:, :128] + s2[:, 128:], re + im], axis=1
    )


def fine_frames(blocks, tapers):
    now, later = blocks[3:11, :], blocks[4:12, :]
    lane = lax.broadcasted_iota(jnp.int32, (8, 128), 1)
    frames = [now]
    for d in range(1, 4):
        keep = lane < 128 - 32 * d
        frames.append(
            jnp.concatenate(
                [
                    jnp.where(
                        keep,
                        roll(now[:, s : s + 128], -32 * d),
                        roll(later[:, s : s + 128], -32 * d),
                    )
                    for s in (0, 128)
                ],
                axis=1,
            )
        )
    return jnp.concatenate(frames, axis=0) * tapers[4:5, :]


def fine_spectrum(blocks, tapers, table):
    return rows_dot(
        fine_frames(blocks, tapers),
        table[FINE_HIGH : FINE_HIGH + 256, :],
        table[FINE_LOW : FINE_LOW + 256, :],
    )


def level_of(energy, bank):
    m = energy.shape[0]
    eh, el = split(energy)
    both = dot(jnp.concatenate([eh, el], axis=0), bank)
    both = both[:m] + both[m:]
    return jnp.sqrt(both + roll(both, MELS) + 1.0)


def energy_slope(level, target_level, valid, bank):
    m = level.shape[0]
    slope = jnp.where(valid, 1.0 - target_level / level, 0.0)
    sh, sl = split(slope)
    both = dot_nt(jnp.concatenate([sh, sl], axis=0), bank)
    return 2.0 * (both[:m] + both[m:])


def kernel(
    n_dp,
    n_tm,
    latent_hbm,
    target_hbm,
    up_hbm,
    inner_hbm,
    outer_hbm,
    out_hbm,
    dft_hbm,
    mels_hbm,
    tapers_hbm,
    grad_out,
    total,
    latent,
    halo,
    target_rows,
    up_k,
    inner_k,
    outer_k,
    out_k,
    table,
    mels,
    tapers,
    natural,
    target_blocks,
    wave_tiles,
    wave_blocks,
    frame_grads,
    grad_blocks,
    squares,
    packed_rows,
    grad_rows,
    halves_own,
    plane_halves,
    plane_rows,
    ring_rows,
    load_sem,
    near_send,
    near_recv,
    far_send,
    far_recv,
    near_sem,
    far_sem,
):
    dp = lax.axis_index("dp")
    tm = lax.axis_index("tm")
    n_z = n_tm // Y_HI
    n_plane = n_dp * Y_HI
    y_hi = tm // n_z
    z = lax.rem(tm, n_z)
    plane = y_hi * n_dp + dp
    right = lax.rem(tm + 1, n_tm)
    left = lax.rem(tm + n_tm - 1, n_tm)
    other = lax.rem(y_hi + 1, Y_HI) * n_z + z
    first = tm == 0
    last = tm == n_tm - 1

    loads = [
        pltpu.make_async_copy(source, place, load_sem.at[i])
        for i, (source, place) in enumerate(
            [
                (latent_hbm.at[0], latent),
                (target_hbm, target_rows.at[1]),
                (up_hbm, up_k),
                (inner_hbm, inner_k),
                (outer_hbm, outer_k),
                (out_hbm, out_k),
                (dft_hbm, table),
                (mels_hbm, mels),
                (tapers_hbm, tapers),
            ]
        )
    ]
    for load in loads:
        load.start()
    frames = latent.shape[1]
    wide = frames + 128

    barrier = pltpu.get_barrier_semaphore()

    def owner_of(index):
        return (index * n_plane) // TILES

    def tile_of(member):
        return (member * TILES + n_plane - 1) // n_plane

    def is_owner(member):
        index = tile_of(member)
        return (index < TILES) & (owner_of(index) == member)

    def along_z(i):
        half = (i + 1) // 2
        return lax.rem(z + n_z // 2 + half - 2 * half * lax.rem(i, 2) + n_z, n_z)

    def in_plane(visit):
        core, x, y_lo = lax.rem(dp, 2), lax.rem(dp // 2, 4), dp // 8
        for dx in (2, 1, 3, 0):

            @pl.loop(0, 8 if dx else 7)
            def _(i):
                bits = 7 - i
                y = lax.rem(y_hi + bits // 4, 2)
                y_in = lax.rem(y_lo + lax.rem(bits // 2, 2), 2)
                side = lax.rem(core + lax.rem(bits, 2), 2)
                visit(y * n_dp + y_in * 8 + lax.rem(x + dx, 4) * 2 + side)

    def member_id(member):
        return (lax.rem(member, n_dp), (member // n_dp) * n_z + z)

    owns = is_owner(plane)

    def greet(device):
        pl.semaphore_signal(barrier, inc=1, device_id=device, device_id_type=MESH)

    def shifted_z(by):
        return (dp, y_hi * n_z + lax.rem(z + n_z + by, n_z))

    core, column, y_lo = lax.rem(dp, 2), lax.rem(dp // 2, 4), dp // 8
    others_in_y = [
        (lax.rem(y_lo + in_lo, 2) * 8 + 2 * column + core, lax.rem(y_hi + in_hi, 2) * n_z + z)
        for in_lo, in_hi in ((0, 1), (1, 1), (1, 0))
    ]
    for by in (2, -2, 1, -1):
        greet(shifted_z(by))
    for device in others_in_y:
        greet(device)
    for dx, side in ((2, 1), (2, 0), (1, 1), (3, 1), (1, 0), (3, 0), (0, 1)):
        greet((y_lo * 8 + lax.rem(column + dx, 4) * 2 + lax.rem(core + side, 2), tm))

    @pl.when(z == n_z - 1)
    def _():
        greet((dp, right))

    @pl.when(z == 0)
    def _():
        greet((dp, left))

    greeted = 14 + jnp.where((z == 0) | (z == n_z - 1), 1, 0)

    loads[0].wait()
    lane_8 = lax.broadcasted_iota(jnp.int32, (8, 128), 1)
    lent = jnp.zeros((8, 128), F32)
    for g in range(8):
        start = latent[8 * g : 8 * g + 8, 0:128]
        end = latent[8 * g : 8 * g + 8, frames - 128 : frames]
        lent = jnp.where(lane_8 // 4 == g, roll(start, 4 * g), lent)
        lent = jnp.where(lane_8 // 4 == 16 + g, roll(end, 4 * g - 60), lent)
    halo[1] = lent

    pl.semaphore_wait(barrier, greeted)

    def send(source, place, slot, device):
        copy = pltpu.make_async_remote_copy(
            src_ref=source,
            dst_ref=place,
            send_sem=near_send.at[slot],
            recv_sem=near_recv.at[slot],
            device_id=device,
            device_id_type=MESH,
        )
        copy.start()
        return copy

    near = [
        send(halo.at[1], halo.at[0], 0, (dp, right)),
        send(halo.at[1], halo.at[2], 1, (dp, left)),
        send(target_hbm, target_rows.at[0], 2, (dp, right)),
        send(target_hbm, target_rows.at[2], 3, (dp, left)),
    ]

    def tell(semaphore, device):
        pl.semaphore_signal(semaphore, inc=1, device_id=device, device_id_type=MESH)

    for device in (shifted_z(2), shifted_z(-2), *others_in_y):
        tell(near_sem, device)

    loads[2].wait()
    loads[3].wait()
    loads[4].wait()
    loads[5].wait()
    up_rows = up_k[...]
    up_all = jnp.concatenate([up_rows[r] for r in range(4)], axis=0)
    up_w = jnp.concatenate(
        [
            jnp.concatenate([up_rows[0], up_rows[2]], axis=1),
            jnp.concatenate([up_rows[1], up_rows[3]], axis=1),
        ],
        axis=0,
    )
    up_fwd = split(up_w)
    up_bwd = split(up_all.T)
    taps = jnp.concatenate(
        [inner_k[0], inner_k[1], inner_k[2], jnp.zeros((16, 32), F32)], axis=1
    )
    inner_w = jnp.concatenate([taps, roll(taps, 32)], axis=0)
    inner_fwd = split(inner_w)
    zero = jnp.zeros((16, 32), F32)
    k0, k1, k2 = inner_k[0], inner_k[1], inner_k[2]
    inner_t = jnp.concatenate(
        [
            jnp.concatenate([k1, k2], axis=1),
            jnp.concatenate([k0, k1], axis=1),
            jnp.concatenate([k2, zero], axis=1),
            jnp.concatenate([zero, k0], axis=1),
        ],
        axis=0,
    )
    inner_bwd = split(inner_t.T)
    outer_t = outer_k[...]
    outer_w = jnp.concatenate(
        [jnp.concatenate([outer_t, zero], axis=1), jnp.concatenate([zero, outer_t], axis=1)],
        axis=0,
    )
    outer_bwd = split(outer_w)
    outer_fwd = split(outer_w.T)
    pad = jnp.zeros((1, 32), F32)
    taps_out = out_k[...]
    out_w = jnp.concatenate(
        [
            jnp.concatenate([pad, taps_out], axis=0),
            jnp.concatenate([taps_out, pad], axis=0),
        ],
        axis=1,
    )
    out_w16 = jnp.concatenate([out_w, jnp.zeros((8, 64), F32)], axis=0)
    out_fwd = split(out_w16)
    out_bwd = split(out_w16.T)

    lane = lax.broadcasted_iota(jnp.int32, (1, wide), 1)
    inside = (
        (lane < frames)
        | ((lane < frames + 4) & jnp.logical_not(last))
        | ((lane >= wide - 4) & jnp.logical_not(first))
    )

    near[0].wait_recv()
    near[1].wait_recv()
    before, behind = halo[0], halo[2]
    rim = []
    for g in range(8):
        tile = jnp.where((lane_8 < 4) & jnp.logical_not(last), roll(behind, -4 * g), 0.0)
        rim.append(
            jnp.where((lane_8 >= 124) & jnp.logical_not(first), roll(before, 60 - 4 * g), tile)
        )
    rim = jnp.concatenate(rim, axis=0)
    activated, slope_in = elu_and_slope(jnp.concatenate([latent[...], rim], axis=1))
    stacked = jnp.concatenate([activated, roll(activated, 1)], axis=0)
    upper = jnp.where(inside, weight_dot(up_fwd, stacked), 0.0)
    lifted, slope_upper = elu_and_slope(upper)
    even, odd = lifted[:32], lifted[32:]
    tapped = jnp.concatenate([roll(odd, 1), even, odd, roll(even, -1)], axis=0)
    hidden, slope_inner = elu_and_slope(weight_dot(inner_fwd, tapped))
    mixed = jnp.where(inside, upper + weight_dot(outer_fwd, hidden), 0.0)
    final, slope_mixed = elu_and_slope(mixed)
    taps_8 = weight_dot(out_fwd, final)[:8]
    row = lax.broadcasted_iota(jnp.int32, (8, wide), 0)
    moves = ((2, 0, 0), (1, 1, 2), (-1, 5, 6), (-2, 7, 7))
    aligned = taps_8
    for by, low, high in moves:
        aligned = jnp.where((row >= low) & (row <= high), roll(taps_8, by), aligned)
    aligned = aligned[:, :frames]
    aligned = aligned + roll(aligned, 4, 0)
    aligned = aligned + roll(aligned, 2, 0)
    is_even = lax.rem(row[:, :frames], 2) == 0
    swapped = roll(aligned, 1, 0)
    wave_even = jnp.where(is_even, aligned, swapped)
    wave_odd = jnp.where(is_even, swapped, aligned)
    tile = jnp.zeros((8, 128), F32)
    row_8 = row[:, :128]
    for b in range(4):
        tile = jnp.where(row_8 == b, wave_even[:, 128 * b : 128 * b + 128], tile)
        tile = jnp.where(row_8 == 4 + b, wave_odd[:, 128 * b : 128 * b + 128], tile)
    wave_tiles[1] = tile
    near += [
        send(wave_tiles.at[1], wave_tiles.at[0], 4, (dp, right)),
        send(wave_tiles.at[1], wave_tiles.at[2], 5, (dp, left)),
    ]

    pl.semaphore_wait(near_sem, 5)
    tell(far_sem, shifted_z(4))
    tell(far_sem, shifted_z(-4))

    for load in (loads[1], loads[6], loads[7], loads[8]):
        load.wait()
    near[2].wait_recv()
    near[3].wait_recv()
    natural[...] = jnp.zeros(natural.shape, F32)
    for s in range(3):
        for b in range(4):
            line = target_rows[s, :, 256 * b : 256 * b + 256]
            if s == 0:
                line = jnp.where(first, 0.0, line)
            if s == 2:
                line = jnp.where(last, 0.0, line)
            natural[4 * s + b : 4 * s + b + 1, :] = line
    nh, nl = split(natural[...])
    moved = dot(jnp.concatenate([nh, nl], axis=0), table[MOVE : MOVE + 256, :])
    target_blocks[...] = jnp.zeros(target_blocks.shape, F32)
    target_blocks[0:16, :] = moved[:16] + moved[16:]
    bank, bank_fine = mels[0:512, :], mels[512:640, :]
    target_coarse = level_of(coarse_energy(coarse_spectrum(target_blocks, tapers, table)), bank)
    s = fine_spectrum(target_blocks, tapers, table)
    s = s * s
    target_fine = level_of(s[:, :128] + s[:, 128:], bank_fine)

    wave_blocks[...] = jnp.zeros(wave_blocks.shape, F32)
    near[4].wait_recv()
    near[5].wait_recv()
    for s in range(3):
        for half in range(2):
            lines = wave_tiles[s, 4 * half : 4 * half + 4, :]
            if s == 0:
                lines = jnp.where(first, 0.0, lines)
            if s == 2:
                lines = jnp.where(last, 0.0, lines)
            wave_blocks[4 * s : 4 * s + 4, 128 * half : 128 * half + 128] = lines
    parts = coarse_spectrum(wave_blocks, tapers, table)
    level = level_of(coarse_energy(parts), bank)
    frame = lax.broadcasted_iota(jnp.int32, (16, 128), 0)
    index = 4 * tm + frame - 4
    valid = (frame < 9) & (index >= 0) & (index < 4 * n_tm)
    slope = energy_slope(level, target_coarse, valid, bank)
    s0, s2, re, im = parts
    twice = functools.partial(jnp.concatenate, axis=1)
    d0 = s0 * twice([slope[:, 0:128]] * 2)
    d2 = s2 * twice([slope[:, 128:256]] * 2)
    d_even = rows_dot(d0, table[HIGH : HIGH + 256, :], table[LOW : LOW + 256, :], dot_nt)
    d_odd = rows_dot(
        d2, table[HIGH + 256 : HIGH + 512, :], table[LOW + 256 : LOW + 512, :], dot_nt
    )
    d_cross = rows_dot(
        re * slope[:, 256:512],
        table[HIGH + 512 : HIGH + 1024, :],
        table[LOW + 512 : LOW + 1024, :],
        dot_nt,
    ) + rows_dot(
        im * slope[:, 256:512],
        table[HIGH + 1024 : HIGH + 1536, :],
        table[LOW + 1024 : LOW + 1536, :],
        dot_nt,
    )
    d_first, d_second = d_cross[:, :256], d_cross[:, 256:]
    both, apart = d_even + d_odd, d_even - d_odd
    for b, d in enumerate((both + d_first, apart + d_second, both - d_first, apart - d_second)):
        frame_grads[b] = d * tapers[b : b + 1, :]
    coarse = frame_grads[0, 3:11, :]
    for b in range(1, 4):
        coarse = coarse + frame_grads[b, 3 - b : 11 - b, :]

    spectrum = fine_spectrum(wave_blocks, tapers, table)
    s = spectrum * spectrum
    level = level_of(s[:, :128] + s[:, 128:], bank_fine)
    frame = lax.broadcasted_iota(jnp.int32, (32, 128), 0)
    index = 16 * tm + 4 * (lax.rem(frame, 8) - 1) + frame // 8
    valid = (index >= 0) & (index < 16 * n_tm)
    slope = energy_slope(level, target_fine, valid, bank_fine)
    d = rows_dot(
        spectrum * twice([slope] * 2),
        table[FINE_HIGH : FINE_HIGH + 256, :],
        table[FINE_LOW : FINE_LOW + 256, :],
        dot_nt,
    )
    d = d * tapers[4:5, :]
    fine = []
    for start in (0, 128):
        here = d[0:8, start : start + 128]
        after = jnp.zeros((8, 128), F32)
        for k in range(1, 4):
            moved = roll(d[8 * k : 8 * k + 8, start : start + 128], 32 * k)
            here = here + jnp.where(lane_8 >= 32 * k, moved, 0.0)
            after = after + jnp.where(lane_8 < 32 * k, moved, 0.0)
        fine.append(here + roll(after, 1, 0))
    fine = twice(fine)
    timed = 2.0 * (wave_blocks[3:11, :] - target_blocks[3:11, :])

    row_256 = lax.broadcasted_iota(jnp.int32, (8, 256), 0)
    own = (row_256 >= 1) & (row_256 <= 4)
    lane_1 = lax.broadcasted_iota(jnp.int32, (1, 128), 1)
    line = jnp.zeros((1, 128), F32)
    for i, member in enumerate((timed, coarse, fine)):
        kept = jnp.where(own, member * member, 0.0)
        line = jnp.where(lane_1 == i, jnp.sum(kept, keepdims=True), line)
    squares[z] = line

    def far(source, place, slot, device):
        return pltpu.make_async_remote_copy(
            src_ref=source,
            dst_ref=place,
            send_sem=far_send.at[slot],
            recv_sem=far_recv.at[slot],
            device_id=device,
            device_id_type=MESH,
        )

    def arrived(ref, slot):
        pltpu.make_async_copy(ref, ref, far_recv.at[slot]).wait()

    def sent(ref, slot):
        pltpu.make_async_copy(ref, ref, far_send.at[slot]).wait()

    pl.semaphore_wait(far_sem, 2)

    @pl.loop(0, n_z - 1)
    def _(i):
        far(squares.at[z], squares.at[z], 0, (dp, y_hi * n_z + along_z(i))).start()

    grad_blocks[0] = timed
    grad_blocks[1] = coarse
    grad_blocks[2] = fine
    even_8 = lax.rem(row_8, 2) == 0

    def shifted(x):
        result = x
        for by, low, high in moves:
            result = jnp.where((row >= low) & (row <= high), roll(x, -by), result)
        return jnp.concatenate([result, jnp.zeros_like(result)], axis=0)

    for i in range(3):
        spread = []
        for b in range(5):
            r = b + 1
            even = jnp.broadcast_to(grad_blocks[i, r : r + 1, 0:128], (8, 128))
            odd = jnp.broadcast_to(grad_blocks[i, r : r + 1, 128:256], (8, 128))
            lines = jnp.where(even_8, even, odd)
            if b == 4:
                even = jnp.broadcast_to(grad_blocks[i, 0:1, 0:128], (8, 128))
                odd = jnp.broadcast_to(grad_blocks[i, 0:1, 128:256], (8, 128))
                lines = jnp.where(lane_8 < 64, lines, jnp.where(even_8, even, odd))
            spread.append(lines)
        wide_grad = jnp.where(inside, jnp.concatenate(spread, axis=1), 0.0)
        grad_final = weight_dot(out_bwd, shifted(wide_grad))
        owned = jnp.where(lane < frames, wide_grad, 0.0)
        out_rows = gram(shifted(owned), final)[:8]
        grad_mixed = jnp.where(inside, grad_final * slope_mixed, 0.0)
        outer_rows = gram(hidden[:, :frames], grad_mixed[:, :frames])
        grad_inner = weight_dot(outer_bwd, grad_mixed) * slope_inner
        inner_rows = gram(grad_inner[:, :frames], tapped[:, :frames])
        even, odd = grad_inner[:16], grad_inner[16:]
        around = jnp.concatenate([even, odd, roll(odd, 1), roll(even, -1)], axis=0)
        grad_lifted = weight_dot(inner_bwd, around)
        grad_upper = jnp.where(inside, grad_mixed + grad_lifted * slope_upper, 0.0)
        packed_rows[i, 0:64, :] = gram(grad_upper[:, :frames], stacked[:, :frames])
        taps = inner_rows[:16] + roll(inner_rows[16:], -32)
        pair = outer_rows[:16, :32] + outer_rows[16:, 32:]
        packed_rows[i, 64:80, :] = jnp.concatenate([taps[:, :96], pair], axis=1)
        taps_7 = out_rows[0:7, 32:64] + out_rows[1:8, 0:32]
        packed_rows[i, 80:88, :] = jnp.zeros((8, 128), F32)
        packed_rows[i, 80:87, 0:32] = taps_7
        after = jnp.concatenate([grad_upper, roll(grad_upper, -1)], axis=0)
        grad_rows[i] = weight_dot(up_bwd, after[:, :frames]) * slope_in[:, :frames]

    for i in range(TILES):
        owner = owner_of(i)
        chunk = packed_rows.at[:, pl.ds(8 * i, 8)]
        mine = plane == owner

        @pl.when(mine)
        def _():
            plane_rows[plane] = chunk[...]

        @pl.when(jnp.logical_not(mine))
        def _():
            far(chunk, plane_rows.at[plane], 1, member_id(owner)).start()

    arrived(squares.at[pl.ds(0, n_z - 1)], 0)
    sums = squares[0]
    for i in range(1, n_z):
        sums = sums + squares[i]
    halves_own[0] = sums
    for i in range(TILES):
        owner = owner_of(i)
        mine = plane == owner

        @pl.when(mine)
        def _():
            plane_halves[plane] = sums

        @pl.when(jnp.logical_not(mine))
        def _():
            far(halves_own.at[0], plane_halves.at[plane], 4, member_id(owner)).start()

    far(halves_own.at[0], halves_own.at[1], 5, (dp, other)).start()

    def scales_of(sums):
        coeffs = jnp.where(lane_1 == 0, COEFFS[0], jnp.where(lane_1 == 1, COEFFS[1], COEFFS[2]))
        return coeffs * lax.rsqrt(sums / (n_tm * 2.0 * frames) + 1e-06)

    arrived(halves_own.at[1], 5)
    scales = scales_of(halves_own[0] + halves_own[1])
    grad_out[...] = (
        scales[:, 0:1] * grad_rows[0] + scales[:, 1:2] * grad_rows[1] + scales[:, 2:3] * grad_rows[2]
    )

    tile_index = tile_of(plane)
    tile_rows = pl.ds(pl.multiple_of(8 * tile_index, 8), 8)

    @pl.when(owns)
    def _():
        arrived(plane_rows.at[pl.ds(0, n_plane - 1)], 1)
        arrived(plane_halves.at[pl.ds(0, n_plane - 1)], 4)
        chunk = jnp.zeros((8, 128), F32)
        for c in range(n_dp):
            scales = scales_of(plane_halves[c] + plane_halves[n_dp + c])
            for i in range(3):
                both = plane_rows[c, i] + plane_rows[n_dp + c, i]
                chunk = chunk + scales[:, i : i + 1] * both
        ring_rows[z] = chunk

        @pl.loop(0, n_z - 1)
        def _(i):
            far(ring_rows.at[z], ring_rows.at[z], 2, (dp, y_hi * n_z + along_z(i))).start()

        arrived(ring_rows.at[pl.ds(0, n_z - 1)], 2)
        chunk = ring_rows[0]
        for i in range(1, n_z):
            chunk = chunk + ring_rows[i]
        total[tile_rows, :] = chunk

        def give(member):
            far(total.at[tile_rows], total.at[tile_rows], 3, member_id(member)).start()

        in_plane(give)
        arrived(total.at[pl.ds(0, 8 * (TILES - 1))], 3)

    @pl.when(jnp.logical_not(owns))
    def _():
        arrived(total.at[pl.ds(0, 8 * TILES)], 3)

    for copy in near:
        copy.wait_send()
    sent(squares.at[pl.ds(0, n_z - 1)], 0)
    sent(halves_own.at[0], 5)

    @pl.when(owns)
    def _():
        sent(plane_rows.at[pl.ds(0, TILES - 1)], 1)
        sent(plane_halves.at[pl.ds(0, TILES - 1)], 4)
        sent(ring_rows.at[pl.ds(0, n_z - 1)], 2)
        sent(plane_rows.at[pl.ds(0, n_plane - 1), 0], 3)

    @pl.when(jnp.logical_not(owns))
    def _():
        sent(plane_rows.at[pl.ds(0, TILES)], 1)
        sent(plane_halves.at[pl.ds(0, TILES)], 4)


def finish(grad_ref, total_ref, latent_ref, up_ref, inner_ref, outer_ref, out_ref, store_sem):
    store = pltpu.make_async_copy(grad_ref, latent_ref.at[0], store_sem)
    store.start()
    sums = total_ref[...]
    square = jnp.sum(sums * sums, keepdims=True)
    factor = jnp.minimum(1.0, lax.rsqrt(square / PARAMS + 1e-06))
    sums = sums * factor
    up_ref[0] = sums[0:32, 0:64]
    up_ref[1] = sums[32:64, 0:64]
    up_ref[2] = sums[0:32, 64:128]
    up_ref[3] = sums[32:64, 64:128]
    for j in range(3):
        inner_ref[j] = sums[64:80, 32 * j : 32 * j + 32]
    outer_ref[...] = sums[64:80, 96:128]
    out_ref[...] = sums[80:87, 0:32]
    store.wait()


def local(n_dp, n_tm, latent, target, up_kernel, inner_kernel, outer_kernel, out_kernel):
    dft, mels, tapers = tables()
    frames = latent.shape[2]
    n_z = n_tm // Y_HI
    n_plane = n_dp * Y_HI
    shape = jax.ShapeDtypeStruct
    hbm = pl.BlockSpec(memory_space=pltpu.HBM)
    vmem = pl.BlockSpec(memory_space=pltpu.VMEM)
    grad, total = pl.pallas_call(
        functools.partial(kernel, n_dp, n_tm),
        out_shape=(pltpu.VMEM((64, frames), F32), pltpu.VMEM((8 * TILES, 128), F32)),
        in_specs=[hbm] * 9,
        out_specs=(vmem, vmem),
        scratch_shapes=[
            pltpu.VMEM((64, frames), F32),
            pltpu.VMEM((3, 8, 128), F32),
            pltpu.VMEM((3, 1, 2 * frames), F32),
            pltpu.VMEM((4, 32, 64), F32),
            pltpu.VMEM((3, 16, 32), F32),
            pltpu.VMEM((16, 32), F32),
            pltpu.VMEM((7, 32), F32),
            pltpu.VMEM((ROWS, 256), BF16),
            pltpu.VMEM((640, 128), BF16),
            pltpu.VMEM((8, 256), F32),
            pltpu.VMEM((16, 256), F32),
            pltpu.VMEM((24, 256), F32),
            pltpu.VMEM((3, 8, 128), F32),
            pltpu.VMEM((24, 256), F32),
            pltpu.VMEM((4, 16, 256), F32),
            pltpu.VMEM((3, 8, 256), F32),
            pltpu.VMEM((n_z, 1, 128), F32),
            pltpu.VMEM((3, 8 * TILES, 128), F32),
            pltpu.VMEM((3, 64, frames), F32),
            pltpu.VMEM((2, 1, 128), F32),
            pltpu.VMEM((n_plane, 1, 128), F32),
            pltpu.VMEM((n_plane, 3, 8, 128), F32),
            pltpu.VMEM((n_z, 8, 128), F32),
            pltpu.SemaphoreType.DMA((9,)),
            pltpu.SemaphoreType.DMA((6,)),
            pltpu.SemaphoreType.DMA((6,)),
            pltpu.SemaphoreType.DMA((6,)),
            pltpu.SemaphoreType.DMA((6,)),
            pltpu.SemaphoreType.REGULAR,
            pltpu.SemaphoreType.REGULAR,
        ],
        compiler_params=pltpu.CompilerParams(
            collective_id=0, has_side_effects=True, vmem_limit_bytes=32 * 1024 * 1024
        ),
    )(
        *(
            pltpu.with_memory_space_constraint(x, pltpu.HBM)
            for x in (
                latent,
                target,
                up_kernel,
                inner_kernel,
                outer_kernel.T,
                out_kernel,
                jnp.asarray(dft),
                jnp.asarray(mels),
                jnp.asarray(tapers),
            )
        )
    )
    grad, up, inner, outer, out = pl.pallas_call(
        finish,
        out_shape=(
            shape(latent.shape, F32),
            shape((4, 32, 64), F32),
            shape((3, 16, 32), F32),
            shape((16, 32), F32),
            shape((7, 32), F32),
        ),
        in_specs=[vmem] * 2,
        out_specs=(hbm, vmem, vmem, vmem, vmem),
        scratch_shapes=[pltpu.SemaphoreType.DMA],
    )(*(pltpu.with_memory_space_constraint(x, pltpu.VMEM) for x in (grad, total)))
    return grad, up, inner, outer.T, out


def solution(mesh):
    return jax.shard_map(
        functools.partial(local, mesh.shape["dp"], mesh.shape["tm"]),
        mesh=mesh,
        in_specs=(P("dp", None, "tm"), P("dp", "tm"), P(), P(), P(), P()),
        out_specs=(P("dp", None, "tm"), P(), P(), P(), P()),
        check_vma=False,
    )
```

```python
import functools

import jax
import jax.numpy as jnp
import ml_dtypes
import numpy as np
from jax import lax
from jax.experimental import pallas as pl
from jax.experimental.pallas import tpu as pltpu
from jax.sharding import PartitionSpec as P

F32 = jnp.float32
BF16 = jnp.bfloat16
MESH = pl.DeviceIdType.MESH
MELS = 64
COEFFS = (0.25, 0.5, 0.5)
PARAMS = 10464
Y_HI = 2
TILES = 11


def mel_bank(window):
    half = window // 2
    top = 2595.0 * np.log10(1.0 + 12000.0 / 700.0)
    points = (np.arange(MELS + 1) + 1.0) / (MELS + 2.0) * top
    centers = 700.0 * (np.power(10.0, points / 2595.0) - 1.0) / 12000.0 * half
    spacing = np.maximum(centers[1:] - centers[:-1], 1.0)
    places = np.arange(half)[:, None]
    return np.maximum(0.0, 1.0 - np.abs(places - centers[None, :MELS]) / spacing[None, :])


def halves(x):
    high = x.astype(ml_dtypes.bfloat16)
    low = (x - high.astype(np.float64)).astype(ml_dtypes.bfloat16)
    return high, low


@functools.cache
def tables():
    lane = np.arange(256)
    place = np.where(lane < 128, 2 * lane, 2 * (lane - 128) + 1)

    def waves(bins, window):
        angle = 2.0 * np.pi * ((place[:, None] * bins[None, :]) % window) / window
        return np.cos(angle), np.sin(angle)

    p = np.arange(128)
    cos0, sin0 = waves(4 * p, 1024)
    cos2, sin2 = waves(4 * p + 2, 1024)
    cos1, sin1 = waves(4 * p + 1, 1024)
    cos3, sin3 = waves(4 * p + 3, 1024)
    t0 = np.concatenate([cos0, -sin0], axis=1)
    t2 = np.concatenate([cos2, -sin2], axis=1)
    real = np.concatenate(
        [np.concatenate([cos1, cos3], axis=1), np.concatenate([-sin1, sin3], axis=1)], axis=0
    )
    imag = np.concatenate(
        [np.concatenate([-sin1, -sin3], axis=1), np.concatenate([-cos1, cos3], axis=1)], axis=0
    )
    cosf, sinf = waves(p, 256)
    fine = np.concatenate([cosf, -sinf], axis=1)
    high, low = halves(np.concatenate([t0, t2, real, imag], axis=0))
    fine_high, fine_low = halves(fine)
    move = np.zeros((256, 256))
    move[place, lane] = 1.0
    dft = np.concatenate(
        [high, low, fine_high, fine_low, move.astype(ml_dtypes.bfloat16)], axis=0
    )
    both = np.concatenate([real, imag], axis=1).T
    back_high, back_low = halves(
        np.concatenate([t0.T, t2.T, both[:, :256], both[:, 256:]], axis=0)
    )
    fine_back_high, fine_back_low = halves(fine.T)
    back = np.concatenate([back_high, back_low, fine_back_high, fine_back_low], axis=0)
    order = np.concatenate([4 * p, 4 * p + 2, 4 * p + 1, 4 * p + 3])
    mels = np.concatenate([mel_bank(1024)[order], mel_bank(256)], axis=0)
    mels = np.concatenate(halves(mels), axis=1)
    taper = 0.5 - 0.5 * np.cos(2.0 * np.pi * (np.arange(4)[:, None] * 256 + place) / 1024)
    taper_fine = 0.5 - 0.5 * np.cos(2.0 * np.pi * place[None, :] / 256)
    tapers = np.concatenate([taper, taper_fine, np.zeros((3, 256))], axis=0).astype(np.float32)
    return dft, back, mels, tapers


HIGH, LOW, FINE_HIGH, FINE_LOW, MOVE, ROWS = 0, 1536, 3072, 3328, 3584, 3840
BACK_ROWS = 3584


def split(x):
    high = x.astype(BF16)
    return high, (x - high.astype(F32)).astype(BF16)


def dot(a, b):
    return lax.dot_general(a, b, (((1,), (0,)), ((), ())), preferred_element_type=F32)


def dot_nt(a, b):
    return lax.dot_general(a, b, (((1,), (1,)), ((), ())), preferred_element_type=F32)


def weight_dot(w, x):
    high, low = w
    m = high.shape[0]
    xh, xl = split(x)
    both = dot(jnp.concatenate([high, low], axis=0), xh)
    return both[:m] + both[m:] + dot(high, xl)


def rows_dot(x, high, low):
    m = x.shape[0]
    xh, xl = split(x)
    both = dot(jnp.concatenate([xh, xl], axis=0), high)
    return both[:m] + both[m:] + dot(xh, low)


def gram(a, b):
    m = a.shape[0]
    ah, al = split(a)
    bh, bl = split(b)
    both = dot_nt(jnp.concatenate([ah, al], axis=0), bh)
    return both[:m] + both[m:] + dot_nt(ah, bl)


def elu_and_slope(x):
    slope = jnp.exp(jnp.minimum(x, 0.0))
    return jnp.maximum(x, 0.0) + (slope - 1.0), slope


def roll(x, by, axis=1):
    return pltpu.roll(x, by % x.shape[axis], axis)


def coarse_spectrum(blocks, tapers, table):
    x = [blocks[b : b + 16, :] * tapers[b : b + 1, :] for b in range(4)]
    even, odd = x[0] + x[2], x[1] + x[3]
    cross = jnp.concatenate([x[0] - x[2], x[1] - x[3]], axis=1)
    return (
        rows_dot(even + odd, table[HIGH : HIGH + 256, :], table[LOW : LOW + 256, :]),
        rows_dot(even - odd, table[HIGH + 256 : HIGH + 512, :], table[LOW + 256 : LOW + 512, :]),
        rows_dot(cross, table[HIGH + 512 : HIGH + 1024, :], table[LOW + 512 : LOW + 1024, :]),
        rows_dot(cross, table[HIGH + 1024 : HIGH + 1536, :], table[LOW + 1024 : LOW + 1536, :]),
    )


def coarse_energy(parts):
    s0, s2, re, im = (part * part for part in parts)
    return jnp.concatenate(
        [s0[:, :128] + s0[:, 128:], s2[:, :128] + s2[:, 128:], re + im], axis=1
    )


def fine_frames(blocks, tapers):
    now, later = blocks[3:11, :], blocks[4:12, :]
    lane = lax.broadcasted_iota(jnp.int32, (8, 128), 1)
    frames = [now]
    for d in range(1, 4):
        keep = lane < 128 - 32 * d
        frames.append(
            jnp.concatenate(
                [
                    jnp.where(
                        keep,
                        roll(now[:, s : s + 128], -32 * d),
                        roll(later[:, s : s + 128], -32 * d),
                    )
                    for s in (0, 128)
                ],
                axis=1,
            )
        )
    return jnp.concatenate(frames, axis=0) * tapers[4:5, :]


def fine_spectrum(blocks, tapers, table):
    return rows_dot(
        fine_frames(blocks, tapers),
        table[FINE_HIGH : FINE_HIGH + 256, :],
        table[FINE_LOW : FINE_LOW + 256, :],
    )


def level_of(energy, bank):
    m = energy.shape[0]
    eh, el = split(energy)
    both = dot(jnp.concatenate([eh, el], axis=0), bank)
    both = both[:m] + both[m:]
    return jnp.sqrt(both + roll(both, MELS) + 1.0)


def energy_slope(level, target_level, valid, bank):
    m = level.shape[0]
    slope = jnp.where(valid, 1.0 - target_level / level, 0.0)
    sh, sl = split(slope)
    both = dot_nt(jnp.concatenate([sh, sl], axis=0), bank)
    return 2.0 * (both[:m] + both[m:])


def kernel(
    n_dp,
    n_tm,
    latent_hbm,
    target_hbm,
    up_hbm,
    inner_hbm,
    outer_hbm,
    out_hbm,
    dft_hbm,
    mels_hbm,
    tapers_hbm,
    back_hbm,
    grad_out,
    total,
    latent,
    halo,
    target_rows,
    up_k,
    inner_k,
    outer_k,
    out_k,
    table,
    mels,
    tapers,
    back_table,
    natural,
    target_blocks,
    wave_tiles,
    wave_blocks,
    frame_grads,
    grad_blocks,
    squares,
    packed_rows,
    grad_rows,
    halves_own,
    plane_halves,
    plane_rows,
    ring_rows,
    load_sem,
    near_send,
    near_recv,
    far_send,
    far_recv,
    near_sem,
    far_sem,
):
    dp = lax.axis_index("dp")
    tm = lax.axis_index("tm")
    n_z = n_tm // Y_HI
    n_plane = n_dp * Y_HI
    y_hi = tm // n_z
    z = lax.rem(tm, n_z)
    plane = y_hi * n_dp + dp
    right = lax.rem(tm + 1, n_tm)
    left = lax.rem(tm + n_tm - 1, n_tm)
    other = lax.rem(y_hi + 1, Y_HI) * n_z + z
    first = tm == 0
    last = tm == n_tm - 1

    loads = [
        pltpu.make_async_copy(source, place, load_sem.at[i])
        for i, (source, place) in enumerate(
            [
                (latent_hbm.at[0], latent),
                (target_hbm, target_rows.at[1]),
                (up_hbm, up_k),
                (inner_hbm, inner_k),
                (outer_hbm, outer_k),
                (out_hbm, out_k),
                (dft_hbm, table),
                (mels_hbm, mels),
                (tapers_hbm, tapers),
                (back_hbm, back_table),
            ]
        )
    ]
    for load in loads:
        load.start()
    frames = latent.shape[1]
    wide = frames + 128

    barrier = pltpu.get_barrier_semaphore()

    def owner_of(index):
        return (index * n_plane) // TILES

    def tile_of(member):
        return (member * TILES + n_plane - 1) // n_plane

    def is_owner(member):
        index = tile_of(member)
        return (index < TILES) & (owner_of(index) == member)

    def along_z(i):
        half = (i + 1) // 2
        return lax.rem(z + n_z // 2 + half - 2 * half * lax.rem(i, 2) + n_z, n_z)

    def in_plane(visit):
        core, x, y_lo = lax.rem(dp, 2), lax.rem(dp // 2, 4), dp // 8
        for dx in (2, 1, 3, 0):

            @pl.loop(0, 8 if dx else 7)
            def _(i):
                bits = 7 - i
                y = lax.rem(y_hi + bits // 4, 2)
                y_in = lax.rem(y_lo + lax.rem(bits // 2, 2), 2)
                side = lax.rem(core + lax.rem(bits, 2), 2)
                visit(y * n_dp + y_in * 8 + lax.rem(x + dx, 4) * 2 + side)

    def member_id(member):
        return (lax.rem(member, n_dp), (member // n_dp) * n_z + z)

    owns = is_owner(plane)

    def greet(device):
        pl.semaphore_signal(barrier, inc=1, device_id=device, device_id_type=MESH)

    def shifted_z(by):
        return (dp, y_hi * n_z + lax.rem(z + n_z + by, n_z))

    core, column, y_lo = lax.rem(dp, 2), lax.rem(dp // 2, 4), dp // 8
    others_in_y = [
        (lax.rem(y_lo + in_lo, 2) * 8 + 2 * column + core, lax.rem(y_hi + in_hi, 2) * n_z + z)
        for in_lo, in_hi in ((0, 1), (1, 1), (1, 0))
    ]
    for by in (2, -2, 1, -1):
        greet(shifted_z(by))
    for device in others_in_y:
        greet(device)
    for dx, side in ((2, 1), (2, 0), (1, 1), (3, 1), (1, 0), (3, 0), (0, 1)):
        greet((y_lo * 8 + lax.rem(column + dx, 4) * 2 + lax.rem(core + side, 2), tm))

    @pl.when(z == n_z - 1)
    def _():
        greet((dp, right))

    @pl.when(z == 0)
    def _():
        greet((dp, left))

    greeted = 14 + jnp.where((z == 0) | (z == n_z - 1), 1, 0)

    loads[0].wait()
    lane_8 = lax.broadcasted_iota(jnp.int32, (8, 128), 1)
    lent = jnp.zeros((8, 128), F32)
    for g in range(8):
        start = latent[8 * g : 8 * g + 8, 0:128]
        end = latent[8 * g : 8 * g + 8, frames - 128 : frames]
        lent = jnp.where(lane_8 // 4 == g, roll(start, 4 * g), lent)
        lent = jnp.where(lane_8 // 4 == 16 + g, roll(end, 4 * g - 60), lent)
    halo[1] = lent

    pl.semaphore_wait(barrier, greeted)

    def send(source, place, slot, device):
        copy = pltpu.make_async_remote_copy(
            src_ref=source,
            dst_ref=place,
            send_sem=near_send.at[slot],
            recv_sem=near_recv.at[slot],
            device_id=device,
            device_id_type=MESH,
        )
        copy.start()
        return copy

    near = [
        send(halo.at[1], halo.at[0], 0, (dp, right)),
        send(halo.at[1], halo.at[2], 1, (dp, left)),
        send(target_hbm, target_rows.at[0], 2, (dp, right)),
        send(target_hbm, target_rows.at[2], 3, (dp, left)),
    ]

    def tell(semaphore, device):
        pl.semaphore_signal(semaphore, inc=1, device_id=device, device_id_type=MESH)

    for device in (shifted_z(2), shifted_z(-2), *others_in_y):
        tell(near_sem, device)

    loads[2].wait()
    loads[3].wait()
    loads[4].wait()
    loads[5].wait()
    up_rows = up_k[...]
    up_all = jnp.concatenate([up_rows[r] for r in range(4)], axis=0)
    up_w = jnp.concatenate(
        [
            jnp.concatenate([up_rows[0], up_rows[2]], axis=1),
            jnp.concatenate([up_rows[1], up_rows[3]], axis=1),
        ],
        axis=0,
    )
    up_fwd = split(up_w)
    up_bwd = split(up_all.T)
    taps = jnp.concatenate(
        [inner_k[0], inner_k[1], inner_k[2], jnp.zeros((16, 32), F32)], axis=1
    )
    inner_w = jnp.concatenate([taps, roll(taps, 32)], axis=0)
    inner_fwd = split(inner_w)
    zero = jnp.zeros((16, 32), F32)
    k0, k1, k2 = inner_k[0], inner_k[1], inner_k[2]
    inner_t = jnp.concatenate(
        [
            jnp.concatenate([k1, k2], axis=1),
            jnp.concatenate([k0, k1], axis=1),
            jnp.concatenate([k2, zero], axis=1),
            jnp.concatenate([zero, k0], axis=1),
        ],
        axis=0,
    )
    inner_bwd = split(inner_t.T)
    outer_t = outer_k[...]
    outer_w = jnp.concatenate(
        [jnp.concatenate([outer_t, zero], axis=1), jnp.concatenate([zero, outer_t], axis=1)],
        axis=0,
    )
    outer_bwd = split(outer_w)
    outer_fwd = split(outer_w.T)
    pad = jnp.zeros((1, 32), F32)
    taps_out = out_k[...]
    out_w = jnp.concatenate(
        [
            jnp.concatenate([pad, taps_out], axis=0),
            jnp.concatenate([taps_out, pad], axis=0),
        ],
        axis=1,
    )
    out_w16 = jnp.concatenate([out_w, jnp.zeros((8, 64), F32)], axis=0)
    out_fwd = split(out_w16)
    out_bwd = split(out_w16.T)

    lane = lax.broadcasted_iota(jnp.int32, (1, wide), 1)
    inside = (
        (lane < frames)
        | ((lane < frames + 4) & jnp.logical_not(last))
        | ((lane >= wide - 4) & jnp.logical_not(first))
    )

    near[0].wait_recv()
    near[1].wait_recv()
    before, behind = halo[0], halo[2]
    rim = []
    for g in range(8):
        tile = jnp.where((lane_8 < 4) & jnp.logical_not(last), roll(behind, -4 * g), 0.0)
        rim.append(
            jnp.where((lane_8 >= 124) & jnp.logical_not(first), roll(before, 60 - 4 * g), tile)
        )
    rim = jnp.concatenate(rim, axis=0)
    activated, slope_in = elu_and_slope(jnp.concatenate([latent[...], rim], axis=1))
    stacked = jnp.concatenate([activated, roll(activated, 1)], axis=0)
    upper = jnp.where(inside, weight_dot(up_fwd, stacked), 0.0)
    lifted, slope_upper = elu_and_slope(upper)
    even, odd = lifted[:32], lifted[32:]
    tapped = jnp.concatenate([roll(odd, 1), even, odd, roll(even, -1)], axis=0)
    hidden, slope_inner = elu_and_slope(weight_dot(inner_fwd, tapped))
    mixed = jnp.where(inside, upper + weight_dot(outer_fwd, hidden), 0.0)
    final, slope_mixed = elu_and_slope(mixed)
    taps_8 = weight_dot(out_fwd, final)[:8]
    row = lax.broadcasted_iota(jnp.int32, (8, wide), 0)
    moves = ((2, 0, 0), (1, 1, 2), (-1, 5, 6), (-2, 7, 7))
    aligned = taps_8
    for by, low, high in moves:
        aligned = jnp.where((row >= low) & (row <= high), roll(taps_8, by), aligned)
    aligned = aligned[:, :frames]
    aligned = aligned + roll(aligned, 4, 0)
    aligned = aligned + roll(aligned, 2, 0)
    is_even = lax.rem(row[:, :frames], 2) == 0
    swapped = roll(aligned, 1, 0)
    wave_even = jnp.where(is_even, aligned, swapped)
    wave_odd = jnp.where(is_even, swapped, aligned)
    tile = jnp.zeros((8, 128), F32)
    row_8 = row[:, :128]
    for b in range(4):
        tile = jnp.where(row_8 == b, wave_even[:, 128 * b : 128 * b + 128], tile)
        tile = jnp.where(row_8 == 4 + b, wave_odd[:, 128 * b : 128 * b + 128], tile)
    wave_tiles[1] = tile
    near += [
        send(wave_tiles.at[1], wave_tiles.at[0], 4, (dp, right)),
        send(wave_tiles.at[1], wave_tiles.at[2], 5, (dp, left)),
    ]

    pl.semaphore_wait(near_sem, 5)
    tell(far_sem, shifted_z(4))
    tell(far_sem, shifted_z(-4))

    for load in (loads[1], loads[6], loads[7], loads[8]):
        load.wait()
    near[2].wait_recv()
    near[3].wait_recv()
    natural[...] = jnp.zeros(natural.shape, F32)
    for s in range(3):
        for b in range(4):
            line = target_rows[s, :, 256 * b : 256 * b + 256]
            if s == 0:
                line = jnp.where(first, 0.0, line)
            if s == 2:
                line = jnp.where(last, 0.0, line)
            natural[4 * s + b : 4 * s + b + 1, :] = line
    nh, nl = split(natural[...])
    moved = dot(jnp.concatenate([nh, nl], axis=0), table[MOVE : MOVE + 256, :])
    target_blocks[...] = jnp.zeros(target_blocks.shape, F32)
    target_blocks[0:16, :] = moved[:16] + moved[16:]
    bank, bank_fine = mels[0:512, :], mels[512:640, :]
    target_coarse = level_of(coarse_energy(coarse_spectrum(target_blocks, tapers, table)), bank)
    s = fine_spectrum(target_blocks, tapers, table)
    s = s * s
    target_fine = level_of(s[:, :128] + s[:, 128:], bank_fine)

    loads[9].wait()

    wave_blocks[...] = jnp.zeros(wave_blocks.shape, F32)
    near[4].wait_recv()
    near[5].wait_recv()
    for s in range(3):
        for half in range(2):
            lines = wave_tiles[s, 4 * half : 4 * half + 4, :]
            if s == 0:
                lines = jnp.where(first, 0.0, lines)
            if s == 2:
                lines = jnp.where(last, 0.0, lines)
            wave_blocks[4 * s : 4 * s + 4, 128 * half : 128 * half + 128] = lines
    parts = coarse_spectrum(wave_blocks, tapers, table)
    level = level_of(coarse_energy(parts), bank)
    frame = lax.broadcasted_iota(jnp.int32, (16, 128), 0)
    index = 4 * tm + frame - 4
    valid = (frame < 9) & (index >= 0) & (index < 4 * n_tm)
    slope = energy_slope(level, target_coarse, valid, bank)
    s0, s2, re, im = parts
    twice = functools.partial(jnp.concatenate, axis=1)
    d0 = s0 * twice([slope[:, 0:128]] * 2)
    d2 = s2 * twice([slope[:, 128:256]] * 2)
    across = twice([re * slope[:, 256:512], im * slope[:, 256:512]])

    def backed(x, start):
        high, low = HIGH + start, LOW + start
        depth = x.shape[1]
        return rows_dot(x, back_table[high : high + depth, :], back_table[low : low + depth, :])

    d_even, d_odd = backed(d0, 0), backed(d2, 256)
    d_first, d_second = backed(across, 512), backed(across, 1024)
    both, apart = d_even + d_odd, d_even - d_odd
    for b, d in enumerate((both + d_first, apart + d_second, both - d_first, apart - d_second)):
        frame_grads[b] = d * tapers[b : b + 1, :]
    coarse = frame_grads[0, 3:11, :]
    for b in range(1, 4):
        coarse = coarse + frame_grads[b, 3 - b : 11 - b, :]

    spectrum = fine_spectrum(wave_blocks, tapers, table)
    s = spectrum * spectrum
    level = level_of(s[:, :128] + s[:, 128:], bank_fine)
    frame = lax.broadcasted_iota(jnp.int32, (32, 128), 0)
    index = 16 * tm + 4 * (lax.rem(frame, 8) - 1) + frame // 8
    valid = (index >= 0) & (index < 16 * n_tm)
    slope = energy_slope(level, target_fine, valid, bank_fine)
    d = rows_dot(
        spectrum * twice([slope] * 2),
        back_table[FINE_HIGH : FINE_HIGH + 256, :],
        back_table[FINE_LOW : FINE_LOW + 256, :],
    )
    d = d * tapers[4:5, :]
    fine = []
    for start in (0, 128):
        here = d[0:8, start : start + 128]
        after = jnp.zeros((8, 128), F32)
        for k in range(1, 4):
            moved = roll(d[8 * k : 8 * k + 8, start : start + 128], 32 * k)
            here = here + jnp.where(lane_8 >= 32 * k, moved, 0.0)
            after = after + jnp.where(lane_8 < 32 * k, moved, 0.0)
        fine.append(here + roll(after, 1, 0))
    fine = twice(fine)
    timed = 2.0 * (wave_blocks[3:11, :] - target_blocks[3:11, :])

    row_256 = lax.broadcasted_iota(jnp.int32, (8, 256), 0)
    own = (row_256 >= 1) & (row_256 <= 4)
    lane_1 = lax.broadcasted_iota(jnp.int32, (1, 128), 1)
    line = jnp.zeros((1, 128), F32)
    for i, member in enumerate((timed, coarse, fine)):
        kept = jnp.where(own, member * member, 0.0)
        line = jnp.where(lane_1 == i, jnp.sum(kept, keepdims=True), line)
    squares[z] = line

    def far(source, place, slot, device):
        return pltpu.make_async_remote_copy(
            src_ref=source,
            dst_ref=place,
            send_sem=far_send.at[slot],
            recv_sem=far_recv.at[slot],
            device_id=device,
            device_id_type=MESH,
        )

    def arrived(ref, slot):
        pltpu.make_async_copy(ref, ref, far_recv.at[slot]).wait()

    def sent(ref, slot):
        pltpu.make_async_copy(ref, ref, far_send.at[slot]).wait()

    pl.semaphore_wait(far_sem, 2)

    @pl.loop(0, n_z - 1)
    def _(i):
        far(squares.at[z], squares.at[z], 0, (dp, y_hi * n_z + along_z(i))).start()

    grad_blocks[0] = timed
    grad_blocks[1] = coarse
    grad_blocks[2] = fine
    even_8 = lax.rem(row_8, 2) == 0

    def shifted(x):
        result = x
        for by, low, high in moves:
            result = jnp.where((row >= low) & (row <= high), roll(x, -by), result)
        return jnp.concatenate([result, jnp.zeros_like(result)], axis=0)

    for i in range(3):
        spread = []
        for b in range(5):
            r = b + 1
            even = jnp.broadcast_to(grad_blocks[i, r : r + 1, 0:128], (8, 128))
            odd = jnp.broadcast_to(grad_blocks[i, r : r + 1, 128:256], (8, 128))
            lines = jnp.where(even_8, even, odd)
            if b == 4:
                even = jnp.broadcast_to(grad_blocks[i, 0:1, 0:128], (8, 128))
                odd = jnp.broadcast_to(grad_blocks[i, 0:1, 128:256], (8, 128))
                lines = jnp.where(lane_8 < 64, lines, jnp.where(even_8, even, odd))
            spread.append(lines)
        wide_grad = jnp.where(inside, jnp.concatenate(spread, axis=1), 0.0)
        grad_final = weight_dot(out_bwd, shifted(wide_grad))
        owned = jnp.where(lane < frames, wide_grad, 0.0)
        out_rows = gram(shifted(owned), final)[:8]
        grad_mixed = jnp.where(inside, grad_final * slope_mixed, 0.0)
        outer_rows = gram(hidden[:, :frames], grad_mixed[:, :frames])
        grad_inner = weight_dot(outer_bwd, grad_mixed) * slope_inner
        inner_rows = gram(grad_inner[:, :frames], tapped[:, :frames])
        even, odd = grad_inner[:16], grad_inner[16:]
        around = jnp.concatenate([even, odd, roll(odd, 1), roll(even, -1)], axis=0)
        grad_lifted = weight_dot(inner_bwd, around)
        grad_upper = jnp.where(inside, grad_mixed + grad_lifted * slope_upper, 0.0)
        packed_rows[i, 0:64, :] = gram(grad_upper[:, :frames], stacked[:, :frames])
        taps = inner_rows[:16] + roll(inner_rows[16:], -32)
        pair = outer_rows[:16, :32] + outer_rows[16:, 32:]
        packed_rows[i, 64:80, :] = jnp.concatenate([taps[:, :96], pair], axis=1)
        taps_7 = out_rows[0:7, 32:64] + out_rows[1:8, 0:32]
        packed_rows[i, 80:88, :] = jnp.zeros((8, 128), F32)
        packed_rows[i, 80:87, 0:32] = taps_7
        after = jnp.concatenate([grad_upper, roll(grad_upper, -1)], axis=0)
        grad_rows[i] = weight_dot(up_bwd, after[:, :frames]) * slope_in[:, :frames]

    for i in range(TILES):
        owner = owner_of(i)
        chunk = packed_rows.at[:, pl.ds(8 * i, 8)]
        mine = plane == owner

        @pl.when(mine)
        def _():
            plane_rows[plane] = chunk[...]

        @pl.when(jnp.logical_not(mine))
        def _():
            far(chunk, plane_rows.at[plane], 1, member_id(owner)).start()

    arrived(squares.at[pl.ds(0, n_z - 1)], 0)
    sums = squares[0]
    for i in range(1, n_z):
        sums = sums + squares[i]
    halves_own[0] = sums
    for i in range(TILES):
        owner = owner_of(i)
        mine = plane == owner

        @pl.when(mine)
        def _():
            plane_halves[plane] = sums

        @pl.when(jnp.logical_not(mine))
        def _():
            far(halves_own.at[0], plane_halves.at[plane], 4, member_id(owner)).start()

    far(halves_own.at[0], halves_own.at[1], 5, (dp, other)).start()

    def scales_of(sums):
        coeffs = jnp.where(lane_1 == 0, COEFFS[0], jnp.where(lane_1 == 1, COEFFS[1], COEFFS[2]))
        return coeffs * lax.rsqrt(sums / (n_tm * 2.0 * frames) + 1e-06)

    arrived(halves_own.at[1], 5)
    scales = scales_of(halves_own[0] + halves_own[1])
    grad_out[...] = (
        scales[:, 0:1] * grad_rows[0] + scales[:, 1:2] * grad_rows[1] + scales[:, 2:3] * grad_rows[2]
    )

    tile_index = tile_of(plane)
    tile_rows = pl.ds(pl.multiple_of(8 * tile_index, 8), 8)

    @pl.when(owns)
    def _():
        arrived(plane_rows.at[pl.ds(0, n_plane - 1)], 1)
        arrived(plane_halves.at[pl.ds(0, n_plane - 1)], 4)
        chunk = jnp.zeros((8, 128), F32)
        for c in range(n_dp):
            scales = scales_of(plane_halves[c] + plane_halves[n_dp + c])
            for i in range(3):
                both = plane_rows[c, i] + plane_rows[n_dp + c, i]
                chunk = chunk + scales[:, i : i + 1] * both
        ring_rows[z] = chunk

        @pl.loop(0, n_z - 1)
        def _(i):
            far(ring_rows.at[z], ring_rows.at[z], 2, (dp, y_hi * n_z + along_z(i))).start()

        arrived(ring_rows.at[pl.ds(0, n_z - 1)], 2)
        chunk = ring_rows[0]
        for i in range(1, n_z):
            chunk = chunk + ring_rows[i]
        total[tile_rows, :] = chunk

        def give(member):
            far(total.at[tile_rows], total.at[tile_rows], 3, member_id(member)).start()

        in_plane(give)
        arrived(total.at[pl.ds(0, 8 * (TILES - 1))], 3)

    @pl.when(jnp.logical_not(owns))
    def _():
        arrived(total.at[pl.ds(0, 8 * TILES)], 3)

    for copy in near:
        copy.wait_send()
    sent(squares.at[pl.ds(0, n_z - 1)], 0)
    sent(halves_own.at[0], 5)

    @pl.when(owns)
    def _():
        sent(plane_rows.at[pl.ds(0, TILES - 1)], 1)
        sent(plane_halves.at[pl.ds(0, TILES - 1)], 4)
        sent(ring_rows.at[pl.ds(0, n_z - 1)], 2)
        sent(plane_rows.at[pl.ds(0, n_plane - 1), 0], 3)

    @pl.when(jnp.logical_not(owns))
    def _():
        sent(plane_rows.at[pl.ds(0, TILES)], 1)
        sent(plane_halves.at[pl.ds(0, TILES)], 4)


def finish(grad_ref, total_ref, latent_ref, up_ref, inner_ref, outer_ref, out_ref, store_sem):
    store = pltpu.make_async_copy(grad_ref, latent_ref.at[0], store_sem)
    store.start()
    sums = total_ref[...]
    square = jnp.sum(sums * sums, keepdims=True)
    factor = jnp.minimum(1.0, lax.rsqrt(square / PARAMS + 1e-06))
    sums = sums * factor
    up_ref[0] = sums[0:32, 0:64]
    up_ref[1] = sums[32:64, 0:64]
    up_ref[2] = sums[0:32, 64:128]
    up_ref[3] = sums[32:64, 64:128]
    for j in range(3):
        inner_ref[j] = sums[64:80, 32 * j : 32 * j + 32]
    outer_ref[...] = sums[64:80, 96:128]
    out_ref[...] = sums[80:87, 0:32]
    store.wait()


def local(n_dp, n_tm, latent, target, up_kernel, inner_kernel, outer_kernel, out_kernel):
    dft, back, mels, tapers = tables()
    frames = latent.shape[2]
    n_z = n_tm // Y_HI
    n_plane = n_dp * Y_HI
    shape = jax.ShapeDtypeStruct
    hbm = pl.BlockSpec(memory_space=pltpu.HBM)
    vmem = pl.BlockSpec(memory_space=pltpu.VMEM)
    grad, total = pl.pallas_call(
        functools.partial(kernel, n_dp, n_tm),
        out_shape=(pltpu.VMEM((64, frames), F32), pltpu.VMEM((8 * TILES, 128), F32)),
        in_specs=[hbm] * 10,
        out_specs=(vmem, vmem),
        scratch_shapes=[
            pltpu.VMEM((64, frames), F32),
            pltpu.VMEM((3, 8, 128), F32),
            pltpu.VMEM((3, 1, 2 * frames), F32),
            pltpu.VMEM((4, 32, 64), F32),
            pltpu.VMEM((3, 16, 32), F32),
            pltpu.VMEM((16, 32), F32),
            pltpu.VMEM((7, 32), F32),
            pltpu.VMEM((ROWS, 256), BF16),
            pltpu.VMEM((640, 128), BF16),
            pltpu.VMEM((8, 256), F32),
            pltpu.VMEM((BACK_ROWS, 256), BF16),
            pltpu.VMEM((16, 256), F32),
            pltpu.VMEM((24, 256), F32),
            pltpu.VMEM((3, 8, 128), F32),
            pltpu.VMEM((24, 256), F32),
            pltpu.VMEM((4, 16, 256), F32),
            pltpu.VMEM((3, 8, 256), F32),
            pltpu.VMEM((n_z, 1, 128), F32),
            pltpu.VMEM((3, 8 * TILES, 128), F32),
            pltpu.VMEM((3, 64, frames), F32),
            pltpu.VMEM((2, 1, 128), F32),
            pltpu.VMEM((n_plane, 1, 128), F32),
            pltpu.VMEM((n_plane, 3, 8, 128), F32),
            pltpu.VMEM((n_z, 8, 128), F32),
            pltpu.SemaphoreType.DMA((10,)),
            pltpu.SemaphoreType.DMA((6,)),
            pltpu.SemaphoreType.DMA((6,)),
            pltpu.SemaphoreType.DMA((6,)),
            pltpu.SemaphoreType.DMA((6,)),
            pltpu.SemaphoreType.REGULAR,
            pltpu.SemaphoreType.REGULAR,
        ],
        compiler_params=pltpu.CompilerParams(
            collective_id=0, has_side_effects=True, vmem_limit_bytes=32 * 1024 * 1024
        ),
    )(
        *(
            pltpu.with_memory_space_constraint(x, pltpu.HBM)
            for x in (
                latent,
                target,
                up_kernel,
                inner_kernel,
                outer_kernel.T,
                out_kernel,
                jnp.asarray(dft),
                jnp.asarray(mels),
                jnp.asarray(tapers),
                jnp.asarray(back),
            )
        )
    )
    grad, up, inner, outer, out = pl.pallas_call(
        finish,
        out_shape=(
            shape(latent.shape, F32),
            shape((4, 32, 64), F32),
            shape((3, 16, 32), F32),
            shape((16, 32), F32),
            shape((7, 32), F32),
        ),
        in_specs=[vmem] * 2,
        out_specs=(hbm, vmem, vmem, vmem, vmem),
        scratch_shapes=[pltpu.SemaphoreType.DMA],
    )(*(pltpu.with_memory_space_constraint(x, pltpu.VMEM) for x in (grad, total)))
    return grad, up, inner, outer.T, out


def solution(mesh):
    return jax.shard_map(
        functools.partial(local, mesh.shape["dp"], mesh.shape["tm"]),
        mesh=mesh,
        in_specs=(P("dp", None, "tm"), P("dp", "tm"), P(), P(), P(), P()),
        out_specs=(P("dp", None, "tm"), P(), P(), P(), P()),
        check_vma=False,
    )
```

```python
import functools

import jax
import jax.numpy as jnp
import ml_dtypes
import numpy as np
from jax import lax
from jax.experimental import pallas as pl
from jax.experimental.pallas import tpu as pltpu
from jax.sharding import PartitionSpec as P

F32 = jnp.float32
BF16 = jnp.bfloat16
MESH = pl.DeviceIdType.MESH
MELS = 64
COEFFS = (0.25, 0.5, 0.5)
PARAMS = 10464
Y_HI = 2
TILES = 11


def mel_bank(window):
    half = window // 2
    top = 2595.0 * np.log10(1.0 + 12000.0 / 700.0)
    points = (np.arange(MELS + 1) + 1.0) / (MELS + 2.0) * top
    centers = 700.0 * (np.power(10.0, points / 2595.0) - 1.0) / 12000.0 * half
    spacing = np.maximum(centers[1:] - centers[:-1], 1.0)
    places = np.arange(half)[:, None]
    return np.maximum(0.0, 1.0 - np.abs(places - centers[None, :MELS]) / spacing[None, :])


def halves(x):
    high = x.astype(ml_dtypes.bfloat16)
    low = (x - high.astype(np.float64)).astype(ml_dtypes.bfloat16)
    return high, low


@functools.cache
def tables():
    lane = np.arange(256)
    place = np.where(lane < 128, 2 * lane, 2 * (lane - 128) + 1)

    def waves(bins, window):
        angle = 2.0 * np.pi * ((place[:, None] * bins[None, :]) % window) / window
        return np.cos(angle), np.sin(angle)

    p = np.arange(128)
    cos0, sin0 = waves(4 * p, 1024)
    cos2, sin2 = waves(4 * p + 2, 1024)
    cos1, sin1 = waves(4 * p + 1, 1024)
    cos3, sin3 = waves(4 * p + 3, 1024)
    t0 = np.concatenate([cos0, -sin0], axis=1)
    t2 = np.concatenate([cos2, -sin2], axis=1)
    real = np.concatenate(
        [np.concatenate([cos1, cos3], axis=1), np.concatenate([-sin1, sin3], axis=1)], axis=0
    )
    imag = np.concatenate(
        [np.concatenate([-sin1, -sin3], axis=1), np.concatenate([-cos1, cos3], axis=1)], axis=0
    )
    cosf, sinf = waves(p, 256)
    fine = np.concatenate([cosf, -sinf], axis=1)
    high, low = halves(np.concatenate([t0, t2, real, imag], axis=0))
    fine_high, fine_low = halves(fine)
    move = np.zeros((256, 256))
    move[place, lane] = 1.0
    dft = np.concatenate(
        [high, low, fine_high, fine_low, move.astype(ml_dtypes.bfloat16)], axis=0
    )
    both = np.concatenate([real, imag], axis=1).T
    back_high, back_low = halves(
        np.concatenate([t0.T, t2.T, both[:, :256], both[:, 256:]], axis=0)
    )
    fine_back_high, fine_back_low = halves(fine.T)
    back = np.concatenate([back_high, back_low, fine_back_high, fine_back_low], axis=0)
    order = np.concatenate([4 * p, 4 * p + 2, 4 * p + 1, 4 * p + 3])
    mels = np.concatenate([mel_bank(1024)[order], mel_bank(256)], axis=0)
    mels = np.concatenate(halves(mels), axis=1)
    taper = 0.5 - 0.5 * np.cos(2.0 * np.pi * (np.arange(4)[:, None] * 256 + place) / 1024)
    taper_fine = 0.5 - 0.5 * np.cos(2.0 * np.pi * place[None, :] / 256)
    tapers = np.concatenate([taper, taper_fine, np.zeros((3, 256))], axis=0).astype(np.float32)
    return dft, back, mels, tapers


HIGH, LOW, FINE_HIGH, FINE_LOW, MOVE, ROWS = 0, 1536, 3072, 3328, 3584, 3840
BACK_ROWS = 3584


def split(x):
    high = x.astype(BF16)
    return high, (x - high.astype(F32)).astype(BF16)


def dot(a, b):
    return lax.dot_general(a, b, (((1,), (0,)), ((), ())), preferred_element_type=F32)


def dot_nt(a, b):
    return lax.dot_general(a, b, (((1,), (1,)), ((), ())), preferred_element_type=F32)


def weight_dot(w, x):
    high, low = w
    m = high.shape[0]
    xh, xl = split(x)
    both = dot(jnp.concatenate([high, low], axis=0), xh)
    return both[:m] + both[m:] + dot(high, xl)


def rows_dot(x, high, low):
    m = x.shape[0]
    xh, xl = split(x)
    both = dot(jnp.concatenate([xh, xl], axis=0), high)
    return both[:m] + both[m:] + dot(xh, low)


def gram(a, b):
    m = a.shape[0]
    ah, al = split(a)
    bh, bl = split(b)
    both = dot_nt(jnp.concatenate([ah, al], axis=0), bh)
    return both[:m] + both[m:] + dot_nt(ah, bl)


def elu_and_slope(x):
    slope = jnp.exp(jnp.minimum(x, 0.0))
    return jnp.maximum(x, 0.0) + (slope - 1.0), slope


def roll(x, by, axis=1):
    return pltpu.roll(x, by % x.shape[axis], axis)


def coarse_spectrum(blocks, tapers, table):
    x = [blocks[b : b + 16, :] * tapers[b : b + 1, :] for b in range(4)]
    even, odd = x[0] + x[2], x[1] + x[3]
    cross = jnp.concatenate([x[0] - x[2], x[1] - x[3]], axis=1)
    return (
        rows_dot(even + odd, table[HIGH : HIGH + 256, :], table[LOW : LOW + 256, :]),
        rows_dot(even - odd, table[HIGH + 256 : HIGH + 512, :], table[LOW + 256 : LOW + 512, :]),
        rows_dot(cross, table[HIGH + 512 : HIGH + 1024, :], table[LOW + 512 : LOW + 1024, :]),
        rows_dot(cross, table[HIGH + 1024 : HIGH + 1536, :], table[LOW + 1024 : LOW + 1536, :]),
    )


def coarse_energy(parts):
    s0, s2, re, im = (part * part for part in parts)
    return jnp.concatenate(
        [s0[:, :128] + s0[:, 128:], s2[:, :128] + s2[:, 128:], re + im], axis=1
    )


def fine_frames(blocks, tapers):
    now, later = blocks[3:11, :], blocks[4:12, :]
    lane = lax.broadcasted_iota(jnp.int32, (8, 128), 1)
    frames = [now]
    for d in range(1, 4):
        keep = lane < 128 - 32 * d
        frames.append(
            jnp.concatenate(
                [
                    jnp.where(
                        keep,
                        roll(now[:, s : s + 128], -32 * d),
                        roll(later[:, s : s + 128], -32 * d),
                    )
                    for s in (0, 128)
                ],
                axis=1,
            )
        )
    return jnp.concatenate(frames, axis=0) * tapers[4:5, :]


def fine_spectrum(blocks, tapers, table):
    return rows_dot(
        fine_frames(blocks, tapers),
        table[FINE_HIGH : FINE_HIGH + 256, :],
        table[FINE_LOW : FINE_LOW + 256, :],
    )


def level_of(energy, bank):
    m = energy.shape[0]
    eh, el = split(energy)
    both = dot(jnp.concatenate([eh, el], axis=0), bank)
    both = both[:m] + both[m:]
    return jnp.sqrt(both + roll(both, MELS) + 1.0)


def energy_slope(level, target_level, valid, bank):
    m = level.shape[0]
    slope = jnp.where(valid, 1.0 - target_level / level, 0.0)
    sh, sl = split(slope)
    both = dot_nt(jnp.concatenate([sh, sl], axis=0), bank)
    return 2.0 * (both[:m] + both[m:])


def kernel(
    n_dp,
    n_tm,
    latent_hbm,
    target_hbm,
    up_hbm,
    inner_hbm,
    outer_hbm,
    out_hbm,
    dft_hbm,
    mels_hbm,
    tapers_hbm,
    back_hbm,
    grad_out,
    total,
    latent,
    halo,
    target_rows,
    up_k,
    inner_k,
    outer_k,
    out_k,
    table,
    mels,
    tapers,
    back_table,
    natural,
    target_blocks,
    wave_tiles,
    wave_blocks,
    frame_grads,
    grad_blocks,
    squares,
    packed_rows,
    grad_rows,
    halves_own,
    plane_halves,
    plane_rows,
    ring_rows,
    load_sem,
    near_send,
    near_recv,
    far_send,
    far_recv,
    near_sem,
    far_sem,
):
    dp = lax.axis_index("dp")
    tm = lax.axis_index("tm")
    n_z = n_tm // Y_HI
    n_plane = n_dp * Y_HI
    y_hi = tm // n_z
    z = lax.rem(tm, n_z)
    plane = y_hi * n_dp + dp
    right = lax.rem(tm + 1, n_tm)
    left = lax.rem(tm + n_tm - 1, n_tm)
    other = lax.rem(y_hi + 1, Y_HI) * n_z + z
    first = tm == 0
    last = tm == n_tm - 1

    loads = [
        pltpu.make_async_copy(source, place, load_sem.at[i])
        for i, (source, place) in enumerate(
            [
                (latent_hbm.at[0], latent),
                (target_hbm, target_rows.at[1]),
                (up_hbm, up_k),
                (inner_hbm, inner_k),
                (outer_hbm, outer_k),
                (out_hbm, out_k),
                (dft_hbm, table),
                (mels_hbm, mels),
                (tapers_hbm, tapers),
                (back_hbm, back_table),
            ]
        )
    ]
    for load in loads:
        load.start()
    frames = latent.shape[1]
    wide = frames + 128

    barrier = pltpu.get_barrier_semaphore()

    def owner_of(index):
        return (index * n_plane) // TILES

    def tile_of(member):
        return (member * TILES + n_plane - 1) // n_plane

    def is_owner(member):
        index = tile_of(member)
        return (index < TILES) & (owner_of(index) == member)

    def along_z(i):
        half = (i + 1) // 2
        return lax.rem(z + n_z // 2 + half - 2 * half * lax.rem(i, 2) + n_z, n_z)

    def in_plane(visit):
        core, x, y_lo = lax.rem(dp, 2), lax.rem(dp // 2, 4), dp // 8
        for dx in (2, 1, 3, 0):

            @pl.loop(0, 8 if dx else 7)
            def _(i):
                bits = 7 - i
                y = lax.rem(y_hi + bits // 4, 2)
                y_in = lax.rem(y_lo + lax.rem(bits // 2, 2), 2)
                side = lax.rem(core + lax.rem(bits, 2), 2)
                visit(y * n_dp + y_in * 8 + lax.rem(x + dx, 4) * 2 + side)

    def member_id(member):
        return (lax.rem(member, n_dp), (member // n_dp) * n_z + z)

    owns = is_owner(plane)

    def greet(device):
        pl.semaphore_signal(barrier, inc=1, device_id=device, device_id_type=MESH)

    def shifted_z(by):
        return (dp, y_hi * n_z + lax.rem(z + n_z + by, n_z))

    core, column, y_lo = lax.rem(dp, 2), lax.rem(dp // 2, 4), dp // 8
    others_in_y = [
        (lax.rem(y_lo + in_lo, 2) * 8 + 2 * column + core, lax.rem(y_hi + in_hi, 2) * n_z + z)
        for in_lo, in_hi in ((0, 1), (1, 1), (1, 0))
    ]
    for by in (2, -2, 1, -1):
        greet(shifted_z(by))
    for device in others_in_y:
        greet(device)
    for dx, side in ((2, 1), (2, 0), (1, 1), (3, 1), (1, 0), (3, 0), (0, 1)):
        greet((y_lo * 8 + lax.rem(column + dx, 4) * 2 + lax.rem(core + side, 2), tm))

    @pl.when(z == n_z - 1)
    def _():
        greet((dp, right))

    @pl.when(z == 0)
    def _():
        greet((dp, left))

    greeted = 14 + jnp.where((z == 0) | (z == n_z - 1), 1, 0)

    loads[0].wait()
    lane_8 = lax.broadcasted_iota(jnp.int32, (8, 128), 1)
    lent = jnp.zeros((8, 128), F32)
    for g in range(8):
        start = latent[8 * g : 8 * g + 8, 0:128]
        end = latent[8 * g : 8 * g + 8, frames - 128 : frames]
        lent = jnp.where(lane_8 // 4 == g, roll(start, 4 * g), lent)
        lent = jnp.where(lane_8 // 4 == 16 + g, roll(end, 4 * g - 60), lent)
    halo[1] = lent

    pl.semaphore_wait(barrier, greeted)

    def send(source, place, slot, device):
        copy = pltpu.make_async_remote_copy(
            src_ref=source,
            dst_ref=place,
            send_sem=near_send.at[slot],
            recv_sem=near_recv.at[slot],
            device_id=device,
            device_id_type=MESH,
        )
        copy.start()
        return copy

    near = [
        send(halo.at[1], halo.at[0], 0, (dp, right)),
        send(halo.at[1], halo.at[2], 1, (dp, left)),
        send(target_hbm, target_rows.at[0], 2, (dp, right)),
        send(target_hbm, target_rows.at[2], 3, (dp, left)),
    ]

    def tell(semaphore, device):
        pl.semaphore_signal(semaphore, inc=1, device_id=device, device_id_type=MESH)

    for device in (shifted_z(2), shifted_z(-2), *others_in_y):
        tell(near_sem, device)

    loads[2].wait()
    loads[3].wait()
    loads[4].wait()
    loads[5].wait()
    up_rows = up_k[...]
    up_all = jnp.concatenate([up_rows[r] for r in range(4)], axis=0)
    up_w = jnp.concatenate(
        [
            jnp.concatenate([up_rows[0], up_rows[2]], axis=1),
            jnp.concatenate([up_rows[1], up_rows[3]], axis=1),
        ],
        axis=0,
    )
    up_fwd = split(up_w)
    up_bwd = split(up_all.T)
    taps = jnp.concatenate(
        [inner_k[0], inner_k[1], inner_k[2], jnp.zeros((16, 32), F32)], axis=1
    )
    inner_w = jnp.concatenate([taps, roll(taps, 32)], axis=0)
    inner_fwd = split(inner_w)
    zero = jnp.zeros((16, 32), F32)
    k0, k1, k2 = inner_k[0], inner_k[1], inner_k[2]
    inner_t = jnp.concatenate(
        [
            jnp.concatenate([k1, k2], axis=1),
            jnp.concatenate([k0, k1], axis=1),
            jnp.concatenate([k2, zero], axis=1),
            jnp.concatenate([zero, k0], axis=1),
        ],
        axis=0,
    )
    inner_bwd = split(inner_t.T)
    outer_t = outer_k[...]
    outer_w = jnp.concatenate(
        [jnp.concatenate([outer_t, zero], axis=1), jnp.concatenate([zero, outer_t], axis=1)],
        axis=0,
    )
    outer_bwd = split(outer_w)
    outer_fwd = split(outer_w.T)
    pad = jnp.zeros((1, 32), F32)
    taps_out = out_k[...]
    out_w = jnp.concatenate(
        [
            jnp.concatenate([pad, taps_out], axis=0),
            jnp.concatenate([taps_out, pad], axis=0),
        ],
        axis=1,
    )
    out_w16 = jnp.concatenate([out_w, jnp.zeros((8, 64), F32)], axis=0)
    out_fwd = split(out_w16)
    out_bwd = split(out_w16.T)

    lane = lax.broadcasted_iota(jnp.int32, (1, wide), 1)
    inside = (
        (lane < frames)
        | ((lane < frames + 4) & jnp.logical_not(last))
        | ((lane >= wide - 4) & jnp.logical_not(first))
    )

    near[0].wait_recv()
    near[1].wait_recv()
    before, behind = halo[0], halo[2]
    rim = []
    for g in range(8):
        tile = jnp.where((lane_8 < 4) & jnp.logical_not(last), roll(behind, -4 * g), 0.0)
        rim.append(
            jnp.where((lane_8 >= 124) & jnp.logical_not(first), roll(before, 60 - 4 * g), tile)
        )
    rim = jnp.concatenate(rim, axis=0)
    activated, slope_in = elu_and_slope(jnp.concatenate([latent[...], rim], axis=1))
    stacked = jnp.concatenate([activated, roll(activated, 1)], axis=0)
    upper = jnp.where(inside, weight_dot(up_fwd, stacked), 0.0)
    lifted, slope_upper = elu_and_slope(upper)
    even, odd = lifted[:32], lifted[32:]
    tapped = jnp.concatenate([roll(odd, 1), even, odd, roll(even, -1)], axis=0)
    hidden, slope_inner = elu_and_slope(weight_dot(inner_fwd, tapped))
    mixed = jnp.where(inside, upper + weight_dot(outer_fwd, hidden), 0.0)
    final, slope_mixed = elu_and_slope(mixed)
    taps_8 = weight_dot(out_fwd, final)[:8]
    row = lax.broadcasted_iota(jnp.int32, (8, wide), 0)
    moves = ((2, 0, 0), (1, 1, 2), (-1, 5, 6), (-2, 7, 7))
    aligned = taps_8
    for by, low, high in moves:
        aligned = jnp.where((row >= low) & (row <= high), roll(taps_8, by), aligned)
    aligned = aligned[:, :frames]
    aligned = aligned + roll(aligned, 4, 0)
    aligned = aligned + roll(aligned, 2, 0)
    is_even = lax.rem(row[:, :frames], 2) == 0
    swapped = roll(aligned, 1, 0)
    wave_even = jnp.where(is_even, aligned, swapped)
    wave_odd = jnp.where(is_even, swapped, aligned)
    tile = jnp.zeros((8, 128), F32)
    row_8 = row[:, :128]
    for b in range(4):
        tile = jnp.where(row_8 == b, wave_even[:, 128 * b : 128 * b + 128], tile)
        tile = jnp.where(row_8 == 4 + b, wave_odd[:, 128 * b : 128 * b + 128], tile)
    wave_tiles[1] = tile
    near += [
        send(wave_tiles.at[1], wave_tiles.at[0], 4, (dp, right)),
        send(wave_tiles.at[1], wave_tiles.at[2], 5, (dp, left)),
    ]

    pl.semaphore_wait(near_sem, 5)
    tell(far_sem, shifted_z(4))
    tell(far_sem, shifted_z(-4))

    for load in (loads[1], loads[6], loads[7], loads[8]):
        load.wait()
    near[2].wait_recv()
    near[3].wait_recv()
    natural[...] = jnp.zeros(natural.shape, F32)
    for s in range(3):
        for b in range(4):
            line = target_rows[s, :, 256 * b : 256 * b + 256]
            if s == 0:
                line = jnp.where(first, 0.0, line)
            if s == 2:
                line = jnp.where(last, 0.0, line)
            natural[4 * s + b : 4 * s + b + 1, :] = line
    nh, nl = split(natural[...])
    moved = dot(jnp.concatenate([nh, nl], axis=0), table[MOVE : MOVE + 256, :])
    target_blocks[...] = jnp.zeros(target_blocks.shape, F32)
    target_blocks[0:16, :] = moved[:16] + moved[16:]
    bank, bank_fine = mels[0:512, :], mels[512:640, :]
    target_coarse = level_of(coarse_energy(coarse_spectrum(target_blocks, tapers, table)), bank)
    s = fine_spectrum(target_blocks, tapers, table)
    s = s * s
    target_fine = level_of(s[:, :128] + s[:, 128:], bank_fine)

    loads[9].wait()

    wave_blocks[...] = jnp.zeros(wave_blocks.shape, F32)
    near[4].wait_recv()
    near[5].wait_recv()
    for s in range(3):
        for half in range(2):
            lines = wave_tiles[s, 4 * half : 4 * half + 4, :]
            if s == 0:
                lines = jnp.where(first, 0.0, lines)
            if s == 2:
                lines = jnp.where(last, 0.0, lines)
            wave_blocks[4 * s : 4 * s + 4, 128 * half : 128 * half + 128] = lines
    parts = coarse_spectrum(wave_blocks, tapers, table)
    level = level_of(coarse_energy(parts), bank)
    frame = lax.broadcasted_iota(jnp.int32, (16, 128), 0)
    index = 4 * tm + frame - 4
    valid = (frame < 9) & (index >= 0) & (index < 4 * n_tm)
    slope = energy_slope(level, target_coarse, valid, bank)
    s0, s2, re, im = parts
    twice = functools.partial(jnp.concatenate, axis=1)
    d0 = s0 * twice([slope[:, 0:128]] * 2)
    d2 = s2 * twice([slope[:, 128:256]] * 2)
    across = twice([re * slope[:, 256:512], im * slope[:, 256:512]])

    def backed(x, start):
        high, low = HIGH + start, LOW + start
        depth = x.shape[1]
        return rows_dot(x, back_table[high : high + depth, :], back_table[low : low + depth, :])

    d_even, d_odd = backed(d0, 0), backed(d2, 256)
    d_first, d_second = backed(across, 512), backed(across, 1024)
    both, apart = d_even + d_odd, d_even - d_odd
    for b, d in enumerate((both + d_first, apart + d_second, both - d_first, apart - d_second)):
        frame_grads[b] = d * tapers[b : b + 1, :]
    coarse = frame_grads[0, 3:11, :]
    for b in range(1, 4):
        coarse = coarse + frame_grads[b, 3 - b : 11 - b, :]

    spectrum = fine_spectrum(wave_blocks, tapers, table)
    s = spectrum * spectrum
    level = level_of(s[:, :128] + s[:, 128:], bank_fine)
    frame = lax.broadcasted_iota(jnp.int32, (32, 128), 0)
    index = 16 * tm + 4 * (lax.rem(frame, 8) - 1) + frame // 8
    valid = (index >= 0) & (index < 16 * n_tm)
    slope = energy_slope(level, target_fine, valid, bank_fine)
    d = rows_dot(
        spectrum * twice([slope] * 2),
        back_table[FINE_HIGH : FINE_HIGH + 256, :],
        back_table[FINE_LOW : FINE_LOW + 256, :],
    )
    d = d * tapers[4:5, :]
    fine = []
    for start in (0, 128):
        here = d[0:8, start : start + 128]
        after = jnp.zeros((8, 128), F32)
        for k in range(1, 4):
            moved = roll(d[8 * k : 8 * k + 8, start : start + 128], 32 * k)
            here = here + jnp.where(lane_8 >= 32 * k, moved, 0.0)
            after = after + jnp.where(lane_8 < 32 * k, moved, 0.0)
        fine.append(here + roll(after, 1, 0))
    fine = twice(fine)
    timed = 2.0 * (wave_blocks[3:11, :] - target_blocks[3:11, :])

    row_256 = lax.broadcasted_iota(jnp.int32, (8, 256), 0)
    own = (row_256 >= 1) & (row_256 <= 4)
    lane_1 = lax.broadcasted_iota(jnp.int32, (1, 128), 1)
    line = jnp.zeros((1, 128), F32)
    for i, member in enumerate((timed, coarse, fine)):
        kept = jnp.where(own, member * member, 0.0)
        line = jnp.where(lane_1 == i, jnp.sum(kept, keepdims=True), line)
    squares[z] = line

    def far(source, place, slot, device):
        return pltpu.make_async_remote_copy(
            src_ref=source,
            dst_ref=place,
            send_sem=far_send.at[slot],
            recv_sem=far_recv.at[slot],
            device_id=device,
            device_id_type=MESH,
        )

    def arrived(ref, slot):
        pltpu.make_async_copy(ref, ref, far_recv.at[slot]).wait()

    def sent(ref, slot):
        pltpu.make_async_copy(ref, ref, far_send.at[slot]).wait()

    pl.semaphore_wait(far_sem, 2)

    @pl.loop(0, n_z - 1)
    def _(i):
        far(squares.at[z], squares.at[z], 0, (dp, y_hi * n_z + along_z(i))).start()

    grad_blocks[0] = timed
    grad_blocks[1] = coarse
    grad_blocks[2] = fine
    even_8 = lax.rem(row_8, 2) == 0

    def shifted(x):
        result = x
        for by, low, high in moves:
            result = jnp.where((row >= low) & (row <= high), roll(x, -by), result)
        return jnp.concatenate([result, jnp.zeros_like(result)], axis=0)

    for i in range(3):
        spread = []
        for b in range(5):
            r = b + 1
            even = jnp.broadcast_to(grad_blocks[i, r : r + 1, 0:128], (8, 128))
            odd = jnp.broadcast_to(grad_blocks[i, r : r + 1, 128:256], (8, 128))
            lines = jnp.where(even_8, even, odd)
            if b == 4:
                even = jnp.broadcast_to(grad_blocks[i, 0:1, 0:128], (8, 128))
                odd = jnp.broadcast_to(grad_blocks[i, 0:1, 128:256], (8, 128))
                lines = jnp.where(lane_8 < 64, lines, jnp.where(even_8, even, odd))
            spread.append(lines)
        wide_grad = jnp.where(inside, jnp.concatenate(spread, axis=1), 0.0)
        grad_final = weight_dot(out_bwd, shifted(wide_grad))
        owned = jnp.where(lane < frames, wide_grad, 0.0)
        out_rows = gram(shifted(owned), final)[:8]
        grad_mixed = jnp.where(inside, grad_final * slope_mixed, 0.0)
        outer_rows = gram(hidden[:, :frames], grad_mixed[:, :frames])
        grad_inner = weight_dot(outer_bwd, grad_mixed) * slope_inner
        inner_rows = gram(grad_inner[:, :frames], tapped[:, :frames])
        even, odd = grad_inner[:16], grad_inner[16:]
        around = jnp.concatenate([even, odd, roll(odd, 1), roll(even, -1)], axis=0)
        grad_lifted = weight_dot(inner_bwd, around)
        grad_upper = jnp.where(inside, grad_mixed + grad_lifted * slope_upper, 0.0)
        packed_rows[i, 0:64, :] = gram(grad_upper[:, :frames], stacked[:, :frames])
        taps = inner_rows[:16] + roll(inner_rows[16:], -32)
        pair = outer_rows[:16, :32] + outer_rows[16:, 32:]
        packed_rows[i, 64:80, :] = jnp.concatenate([taps[:, :96], pair], axis=1)
        taps_7 = out_rows[0:7, 32:64] + out_rows[1:8, 0:32]
        packed_rows[i, 80:88, :] = jnp.zeros((8, 128), F32)
        packed_rows[i, 80:87, 0:32] = taps_7
        after = jnp.concatenate([grad_upper, roll(grad_upper, -1)], axis=0)
        grad_rows[i] = weight_dot(up_bwd, after[:, :frames]) * slope_in[:, :frames]

    for i in range(TILES):
        owner = owner_of(i)
        chunk = packed_rows.at[:, pl.ds(8 * i, 8)]
        mine = plane == owner

        @pl.when(mine)
        def _():
            plane_rows[plane] = chunk[...]

        @pl.when(jnp.logical_not(mine))
        def _():
            far(chunk, plane_rows.at[plane], 1, member_id(owner)).start()

    arrived(squares.at[pl.ds(0, n_z - 1)], 0)
    sums = squares[0]
    for i in range(1, n_z):
        sums = sums + squares[i]
    halves_own[0] = sums
    for i in range(TILES):
        owner = owner_of(i)
        mine = plane == owner

        @pl.when(mine)
        def _():
            plane_halves[plane] = sums

        @pl.when(jnp.logical_not(mine))
        def _():
            far(halves_own.at[0], plane_halves.at[plane], 4, member_id(owner)).start()

    far(halves_own.at[0], halves_own.at[1], 5, (dp, other)).start()

    def scales_of(sums):
        coeffs = jnp.where(lane_1 == 0, COEFFS[0], jnp.where(lane_1 == 1, COEFFS[1], COEFFS[2]))
        return coeffs * lax.rsqrt(sums / (n_tm * 2.0 * frames) + 1e-06)

    arrived(halves_own.at[1], 5)
    scales = scales_of(halves_own[0] + halves_own[1])
    grad_out[...] = (
        scales[:, 0:1] * grad_rows[0] + scales[:, 1:2] * grad_rows[1] + scales[:, 2:3] * grad_rows[2]
    )

    tile_index = tile_of(plane)
    tile_rows = pl.ds(pl.multiple_of(8 * tile_index, 8), 8)

    @pl.when(owns)
    def _():
        arrived(plane_rows.at[pl.ds(0, n_plane - 1)], 1)
        for c in range(n_dp):
            plane_rows[c] = plane_rows[c] + plane_rows[n_dp + c]
        arrived(plane_halves.at[pl.ds(0, n_plane - 1)], 4)
        chunk = jnp.zeros((8, 128), F32)
        for c in range(n_dp):
            scales = scales_of(plane_halves[c] + plane_halves[n_dp + c])
            for i in range(3):
                chunk = chunk + scales[:, i : i + 1] * plane_rows[c, i]
        ring_rows[z] = chunk

        @pl.loop(0, n_z - 1)
        def _(i):
            far(ring_rows.at[z], ring_rows.at[z], 2, (dp, y_hi * n_z + along_z(i))).start()

        arrived(ring_rows.at[pl.ds(0, n_z - 1)], 2)
        chunk = ring_rows[0]
        for i in range(1, n_z):
            chunk = chunk + ring_rows[i]
        total[tile_rows, :] = chunk

        def give(member):
            far(total.at[tile_rows], total.at[tile_rows], 3, member_id(member)).start()

        in_plane(give)
        arrived(total.at[pl.ds(0, 8 * (TILES - 1))], 3)

    @pl.when(jnp.logical_not(owns))
    def _():
        arrived(total.at[pl.ds(0, 8 * TILES)], 3)

    for copy in near:
        copy.wait_send()
    sent(squares.at[pl.ds(0, n_z - 1)], 0)
    sent(halves_own.at[0], 5)

    @pl.when(owns)
    def _():
        sent(plane_rows.at[pl.ds(0, TILES - 1)], 1)
        sent(plane_halves.at[pl.ds(0, TILES - 1)], 4)
        sent(ring_rows.at[pl.ds(0, n_z - 1)], 2)
        sent(plane_rows.at[pl.ds(0, n_plane - 1), 0], 3)

    @pl.when(jnp.logical_not(owns))
    def _():
        sent(plane_rows.at[pl.ds(0, TILES)], 1)
        sent(plane_halves.at[pl.ds(0, TILES)], 4)


def finish(grad_ref, total_ref, latent_ref, up_ref, inner_ref, outer_ref, out_ref, store_sem):
    store = pltpu.make_async_copy(grad_ref, latent_ref.at[0], store_sem)
    store.start()
    sums = total_ref[...]
    square = jnp.sum(sums * sums, keepdims=True)
    factor = jnp.minimum(1.0, lax.rsqrt(square / PARAMS + 1e-06))
    sums = sums * factor
    up_ref[0] = sums[0:32, 0:64]
    up_ref[1] = sums[32:64, 0:64]
    up_ref[2] = sums[0:32, 64:128]
    up_ref[3] = sums[32:64, 64:128]
    for j in range(3):
        inner_ref[j] = sums[64:80, 32 * j : 32 * j + 32]
    outer_ref[...] = sums[64:80, 96:128]
    out_ref[...] = sums[80:87, 0:32]
    store.wait()


def local(n_dp, n_tm, latent, target, up_kernel, inner_kernel, outer_kernel, out_kernel):
    dft, back, mels, tapers = tables()
    frames = latent.shape[2]
    n_z = n_tm // Y_HI
    n_plane = n_dp * Y_HI
    shape = jax.ShapeDtypeStruct
    hbm = pl.BlockSpec(memory_space=pltpu.HBM)
    vmem = pl.BlockSpec(memory_space=pltpu.VMEM)
    grad, total = pl.pallas_call(
        functools.partial(kernel, n_dp, n_tm),
        out_shape=(pltpu.VMEM((64, frames), F32), pltpu.VMEM((8 * TILES, 128), F32)),
        in_specs=[hbm] * 10,
        out_specs=(vmem, vmem),
        scratch_shapes=[
            pltpu.VMEM((64, frames), F32),
            pltpu.VMEM((3, 8, 128), F32),
            pltpu.VMEM((3, 1, 2 * frames), F32),
            pltpu.VMEM((4, 32, 64), F32),
            pltpu.VMEM((3, 16, 32), F32),
            pltpu.VMEM((16, 32), F32),
            pltpu.VMEM((7, 32), F32),
            pltpu.VMEM((ROWS, 256), BF16),
            pltpu.VMEM((640, 128), BF16),
            pltpu.VMEM((8, 256), F32),
            pltpu.VMEM((BACK_ROWS, 256), BF16),
            pltpu.VMEM((16, 256), F32),
            pltpu.VMEM((24, 256), F32),
            pltpu.VMEM((3, 8, 128), F32),
            pltpu.VMEM((24, 256), F32),
            pltpu.VMEM((4, 16, 256), F32),
            pltpu.VMEM((3, 8, 256), F32),
            pltpu.VMEM((n_z, 1, 128), F32),
            pltpu.VMEM((3, 8 * TILES, 128), F32),
            pltpu.VMEM((3, 64, frames), F32),
            pltpu.VMEM((2, 1, 128), F32),
            pltpu.VMEM((n_plane, 1, 128), F32),
            pltpu.VMEM((n_plane, 3, 8, 128), F32),
            pltpu.VMEM((n_z, 8, 128), F32),
            pltpu.SemaphoreType.DMA((10,)),
            pltpu.SemaphoreType.DMA((6,)),
            pltpu.SemaphoreType.DMA((6,)),
            pltpu.SemaphoreType.DMA((6,)),
            pltpu.SemaphoreType.DMA((6,)),
            pltpu.SemaphoreType.REGULAR,
            pltpu.SemaphoreType.REGULAR,
        ],
        compiler_params=pltpu.CompilerParams(
            collective_id=0, has_side_effects=True, vmem_limit_bytes=32 * 1024 * 1024
        ),
    )(
        *(
            pltpu.with_memory_space_constraint(x, pltpu.HBM)
            for x in (
                latent,
                target,
                up_kernel,
                inner_kernel,
                outer_kernel.T,
                out_kernel,
                jnp.asarray(dft),
                jnp.asarray(mels),
                jnp.asarray(tapers),
                jnp.asarray(back),
            )
        )
    )
    grad, up, inner, outer, out = pl.pallas_call(
        finish,
        out_shape=(
            shape(latent.shape, F32),
            shape((4, 32, 64), F32),
            shape((3, 16, 32), F32),
            shape((16, 32), F32),
            shape((7, 32), F32),
        ),
        in_specs=[vmem] * 2,
        out_specs=(hbm, vmem, vmem, vmem, vmem),
        scratch_shapes=[pltpu.SemaphoreType.DMA],
    )(*(pltpu.with_memory_space_constraint(x, pltpu.VMEM) for x in (grad, total)))
    return grad, up, inner, outer.T, out


def solution(mesh):
    return jax.shard_map(
        functools.partial(local, mesh.shape["dp"], mesh.shape["tm"]),
        mesh=mesh,
        in_specs=(P("dp", None, "tm"), P("dp", "tm"), P(), P(), P(), P()),
        out_specs=(P("dp", None, "tm"), P(), P(), P(), P()),
        check_vma=False,
    )
```
